32 devices in a mesh: ctx: 8 (over y, x, core), wa: 4 (over z).
Axes of the slice: x: 2, y: 2, z: 4, core: 2. Of those that a mesh axis runs over, the one named last changes fastest.
Arguments:
- tokens: bfloat16 [4, 1024, 1536], P('wa', 'ctx'), may hold values from -6 to 6
- cotangent: bfloat16 [4, 1024, 1536], P('wa', 'ctx'), may hold values from -6 to 6
- adapter_index: int32 [4], P('wa'), may hold values from 0 to 3
- deal: int32 [8], replicated, may hold values from 0 to 7, each once
- frozen_qkv_weight: bfloat16 [1536, 2048], P('wa'), may hold values from -0.15625 to 0.15625
- frozen_qkv_bias: bfloat16 [2048], replicated, may hold values from -3 to 3
- frozen_output_weight: bfloat16 [1536, 1536], P('wa'), may hold values from -0.625 to 0.625
- frozen_gate_up_weight: bfloat16 [2, 1536, 8960], P(None, None, 'wa'), may hold values from -0.15625 to 0.15625
- frozen_down_weight: bfloat16 [8960, 1536], P('wa'), may hold values from -0.0625 to 0.0625
- gain_attn: bfloat16 [1536], replicated, may hold values from 0.099609375 to 1.8984375
- gain_mlp: bfloat16 [1536], replicated, may hold values from 0.099609375 to 1.8984375
- a_qkv: bfloat16 [4, 48, 1536], replicated, may hold values from -0.15625 to 0.15625
- b_q: bfloat16 [4, 16, 1536], replicated, may hold values from -0.75 to 0.75
- b_kv: bfloat16 [4, 2, 16, 256], replicated, may hold values from -0.75 to 0.75
- a_o: bfloat16 [4, 16, 1536], replicated, may hold values from -0.15625 to 0.15625
- output_adapter_lift: bfloat16 [4, 16, 1536], replicated, may hold values from -3 to 3
- a_gu: bfloat16 [4, 32, 1536], replicated, may hold values from -0.15625 to 0.15625
- gate_up_adapter_lift: bfloat16 [4, 2, 16, 8960], replicated, may hold values from -0.75 to 0.75
- a_down: bfloat16 [4, 16, 8960], replicated, may hold values from -0.0625 to 0.0625
- down_adapter_lift: bfloat16 [4, 16, 1536], replicated, may hold values from -0.75 to 0.75
Outputs:
- out: bfloat16 [4, 1024, 1536], P('wa', 'ctx')
- grad_tokens: float32 [4, 1024, 1536], P('wa', 'ctx')
- grad_a_qkv: float32 [4, 48, 1536], replicated
- grad_b_q: float32 [4, 16, 1536], replicated
- grad_b_kv: float32 [4, 2, 16, 256], replicated
- grad_a_o: float32 [4, 16, 1536], replicated
- grad_b_o: float32 [4, 16, 1536], replicated
- grad_a_gu: float32 [4, 32, 1536], replicated
- grad_b_gu: float32 [4, 2, 16, 8960], replicated
- grad_a_down: float32 [4, 16, 8960], replicated
- grad_b_down: float32 [4, 16, 1536], replicated
The draws below stay inside these ranges and needn't reach their ends.
Inputs may be any that keep to these rules, and one draw needn't show every extreme that they name: `deal`: each context index appears once.
All inputs are finite; a program needn't handle non-finite values.
Results may differ from the reference program's by a relative error of at most 0.024.
Values may be sent and summed in bfloat16 or wider, within the bound.
No kernel may reach another device: no remote copies, remote signals or barrier semaphores. Data moves between devices by JAX's collectives and lax.ppermute only.
A program may use at most 320 MiB of HBM per device.

```python
import math
import jax
import jax.numpy as jnp
from jax import lax

D = 1536
H = 12
KVH = 2
HD = 128
FF = 8960
ADAPTER_RANK = 16
ADAPT = 4
BLK = 64
LEN = 1024
SEQS = 4
KVD = 256
QKV = 2048
N_CTX = 8


def plant(array, stream_key, low, high):
    place = [jax.random.randint(jax.random.fold_in(stream_key, axis), (), 0, length) for axis, length in enumerate(array.shape)]
    longest = array.shape.index(max(array.shape))
    next_to = place[:longest] + [(place[longest] + 1) % array.shape[longest]] + place[longest + 1:]
    return array.at[tuple(place)].set(low).at[tuple(next_to)].set(high)


def levels(stream_key, dims, pieces, low, top_value):
    def one(dim, shards_of):
        heights = jax.random.uniform(jax.random.fold_in(jax.random.fold_in(stream_key, 6), dim), (shards_of,), jnp.float32, low / len(pieces), top_value / len(pieces))
        return jnp.repeat(jnp.exp(heights), dims[dim] // shards_of).reshape((-1,) + (1,) * (len(dims) - dim - 1))

    factor_of = one(*pieces[0])
    for cut in pieces[1:]:
        factor_of = factor_of * one(*cut)
    return factor_of


def centred(own_key, shape, deviation, limit, cuts=(), held_as=jnp.bfloat16):
    array = jax.random.normal(own_key, shape, jnp.float32) * deviation
    if len(cuts) > 0:
        array = levels(own_key, shape, cuts, -0.22, 0.18) * array
    return jnp.clip(array, min=-limit, max=limit).astype(held_as)


def setup_inputs(seed: int = 0) -> dict:
    splits = jax.random.split(jax.random.key(seed), 21)
    return {
        "tokens": centred(splits[0], (SEQS, LEN, D), 1.0, 6.0, ((0, 4), (1, 8))),
        "cotangent": centred(splits[1], (SEQS, LEN, D), 1.0, 6.0, ((0, 4), (1, 8))),
        "adapter_index": plant(jax.random.randint(splits[2], (SEQS,), 0, ADAPT), jax.random.fold_in(splits[2], 1), 0, ADAPT - 1).astype(jnp.int32),
        "deal": jax.random.permutation(splits[3], N_CTX).astype(jnp.int32),
        "frozen_qkv_weight": centred(splits[4], (D, QKV), D ** -0.5, 0.15625, ((0, 4),)),
        "frozen_qkv_bias": centred(splits[5], (QKV,), 0.5, 3.0),
        "frozen_output_weight": centred(splits[6], (D, D), (D // 16) ** -0.5, 0.625, ((0, 4),)),
        "frozen_gate_up_weight": centred(splits[7], (2, D, FF), D ** -0.5, 0.15625, ((2, 4),)),
        "frozen_down_weight": centred(splits[8], (FF, D), FF ** -0.5, 0.0625, ((0, 4),)),
        "gain_attn": jnp.clip(1.0 + 0.18 * jax.random.normal(splits[9], (D,), jnp.float32), 0.099609375, 1.8984375).astype(jnp.bfloat16),
        "gain_mlp": jnp.clip(1.0 + 0.18 * jax.random.normal(splits[10], (D,), jnp.float32), 0.099609375, 1.8984375).astype(jnp.bfloat16),
        "a_qkv": centred(splits[11], (ADAPT, 3 * ADAPTER_RANK, D), D ** -0.5, 0.15625),
        "b_q": centred(splits[12], (ADAPT, ADAPTER_RANK, D), (4 * ADAPTER_RANK) ** -0.5, 0.75),
        "b_kv": centred(splits[13], (ADAPT, 2, ADAPTER_RANK, KVD), (4 * ADAPTER_RANK) ** -0.5, 0.75),
        "a_o": centred(splits[14], (ADAPT, ADAPTER_RANK, D), D ** -0.5, 0.15625),
        "output_adapter_lift": centred(splits[15], (ADAPT, ADAPTER_RANK, D), 4 ** -0.5, 3.0),
        "a_gu": centred(splits[16], (ADAPT, 2 * ADAPTER_RANK, D), D ** -0.5, 0.15625),
        "gate_up_adapter_lift": centred(splits[17], (ADAPT, 2, ADAPTER_RANK, FF), (4 * ADAPTER_RANK) ** -0.5, 0.75),
        "a_down": centred(splits[18], (ADAPT, ADAPTER_RANK, FF), FF ** -0.5, 0.0625),
        "down_adapter_lift": centred(splits[19], (ADAPT, ADAPTER_RANK, D), (4 * ADAPTER_RANK) ** -0.5, 0.75),
    }


@jax.custom_vjp
def low(v):
    return lax.optimization_barrier(v.astype(jnp.bfloat16)).astype(jnp.float32)

@jax.custom_vjp
def low_rank_backward(v):
    return v

def low_keep(v):
    return (low(v), None)

def low_pass(kept, grad):
    return (grad,)

def back_keep(v):
    return (v, None)

def back_low(kept, grad):
    return (low(grad),)
low.defvjp(low_keep, low_pass)
low_rank_backward.defvjp(back_keep, back_low)
eps = 1e-06
rope_base = 1000000.0
adapter_scale = 2.0
masked_value = -1e+30

def rounded_both(v):
    return low(low_rank_backward(v))

def precise_product(left, right):
    return jnp.dot(left, right, precision=lax.Precision.HIGHEST)

def normed(input_rows, gain):
    return input_rows * lax.rsqrt(lax.optimization_barrier(jnp.mean(input_rows * input_rows, axis=-1, keepdims=True)) + eps) * gain

def rope_tables(pos, model_width):
    half = model_width // 2
    freq = rope_base ** (-jnp.arange(half, dtype=jnp.float32) * 2.0 / model_width)
    angle = pos.astype(jnp.float32)[:, None] * freq[None, :]
    cosine = jnp.concatenate([jnp.cos(angle), jnp.cos(angle)], axis=-1)[:, None, :]
    sine = jnp.concatenate([jnp.sin(angle), jnp.sin(angle)], axis=-1)[:, None, :]
    return (cosine, sine)

def rotate(values, cosine, sine):
    half = values.shape[-1] // 2
    rolled = jnp.concatenate([-values[..., half:], values[..., :half]], axis=-1)
    return values * cosine + rolled * sine

def positions(deal):
    rows = jnp.arange(LEN, dtype=jnp.int32)
    owner = rows // (2 * BLK)
    local = rows % (2 * BLK)
    pair = deal[owner]
    return jnp.where(local < BLK, pair * BLK + local, (2 * N_CTX - 1 - pair) * BLK + local - BLK)

def attend(queries, keys, values, pos):
    length = queries.shape[0]
    rows_block = math.gcd(length, 512)
    scale = 1.0 / math.sqrt(queries.shape[-1])

    def one_block(item):
        query_rows, query_pos = item
        raw = jnp.einsum('tkgd,nkd->tkgn', query_rows, keys, precision=lax.Precision.HIGHEST) * scale
        scores = low_rank_backward(raw)
        scores = jnp.where(pos[None, None, None, :] <= query_pos[:, None, None, None], scores, masked_value)
        top = lax.optimization_barrier(jnp.max(scores, axis=-1, keepdims=True))
        expo = jnp.exp(scores - top)
        probs = expo / lax.optimization_barrier(jnp.sum(expo, axis=-1, keepdims=True))
        return jnp.einsum('tkgn,nkd->tkgd', low(probs), values, precision=lax.Precision.HIGHEST)
    split = length // rows_block
    blocks = (queries.reshape((split, rows_block) + queries.shape[1:]), pos.reshape(split, rows_block))
    return lax.map(jax.checkpoint(one_block), blocks).reshape(queries.shape)

def layer(input_rows, pos, frozen_qkv_weight, frozen_qkv_bias, frozen_output_weight, frozen_gate_up_weight, frozen_down_weight, gain_attn, gain_mlp, a_qkv, b_q, b_kv, a_o, output_adapter_lift, a_gu, gate_up_adapter_lift, a_down, down_adapter_lift):
    length = input_rows.shape[0]
    group = H // KVH
    kvd = KVH * HD
    first_normed = low(normed(input_rows, gain_attn))
    qkv_low_rank = rounded_both(precise_product(first_normed, a_qkv.T))
    adapter_extra = jnp.concatenate([precise_product(qkv_low_rank[:, :ADAPTER_RANK], b_q), precise_product(qkv_low_rank[:, ADAPTER_RANK:2 * ADAPTER_RANK], b_kv[0]), precise_product(qkv_low_rank[:, 2 * ADAPTER_RANK:], b_kv[1])], axis=1)
    linear_values = low_rank_backward(precise_product(first_normed, frozen_qkv_weight) + frozen_qkv_bias + adapter_scale * adapter_extra)
    cosine, sine = rope_tables(pos, HD)
    queries = low(rotate(linear_values[:, :D].reshape(length, H, HD), cosine, sine)).reshape(length, KVH, group, HD)
    keys = low(rotate(linear_values[:, D:D + kvd].reshape(length, KVH, HD), cosine, sine))
    values = low(linear_values[:, D + kvd:].reshape(length, KVH, HD))
    attention_output = rounded_both(attend(queries, keys, values, pos).reshape(length, D))
    output_low_rank = rounded_both(precise_product(attention_output, a_o.T))
    middle_rows = input_rows + low_rank_backward(precise_product(attention_output, frozen_output_weight) + adapter_scale * precise_product(output_low_rank, output_adapter_lift))
    second_normed = low(normed(middle_rows, gain_mlp))
    gate_up_low_rank = rounded_both(precise_product(second_normed, a_gu.T))
    gate_values = low_rank_backward(precise_product(second_normed, frozen_gate_up_weight[0]) + adapter_scale * precise_product(gate_up_low_rank[:, :ADAPTER_RANK], gate_up_adapter_lift[0]))
    upper_values = low_rank_backward(precise_product(second_normed, frozen_gate_up_weight[1]) + adapter_scale * precise_product(gate_up_low_rank[:, ADAPTER_RANK:], gate_up_adapter_lift[1]))
    hidden_state = low(jax.nn.silu(gate_values) * upper_values)
    down_low_rank = rounded_both(precise_product(hidden_state, a_down.T))
    adapter_branch = low_rank_backward(precise_product(hidden_state, frozen_down_weight) + adapter_scale * precise_product(down_low_rank, down_adapter_lift))
    return middle_rows + adapter_branch

def reference(tokens, cotangent, adapter_index, deal, frozen_qkv_weight, frozen_qkv_bias, frozen_output_weight, frozen_gate_up_weight, frozen_down_weight, gain_attn, gain_mlp, a_qkv, b_q, b_kv, a_o, output_adapter_lift, a_gu, gate_up_adapter_lift, a_down, down_adapter_lift):
    pos = positions(deal)
    frozen = tuple((w.astype(jnp.float32) for w in (frozen_qkv_weight, frozen_qkv_bias, frozen_output_weight, frozen_gate_up_weight, frozen_down_weight, gain_attn, gain_mlp)))
    adapters = tuple((w.astype(jnp.float32) for w in (a_qkv, b_q, b_kv, a_o, output_adapter_lift, a_gu, gate_up_adapter_lift, a_down, down_adapter_lift)))
    checked = jax.checkpoint(layer)

    def forward(input_tokens, chosen):

        def one_sequence(carry, item):
            seq_rows, which = item
            picked = tuple((table[which] for table in chosen))
            return (carry, checked(seq_rows, pos, *frozen, *picked))
        return lax.scan(one_sequence, jnp.zeros((), jnp.float32), (input_tokens, adapter_index))[1]
    result, pull = jax.vjp(forward, tokens.astype(jnp.float32), adapters)
    grad_inputs, grads = pull(cotangent.astype(jnp.float32))
    return (result.astype(jnp.bfloat16), grad_inputs, grads[0], grads[1], grads[2], grads[3], grads[4], grads[5], grads[6], grads[7], grads[8])
```

```python
import math

import jax
import jax.numpy as jnp
from jax import lax
from jax.sharding import PartitionSpec as P

HD = 128
EPS = 1e-06
ROPE_BASE = 1000000.0
ADAPTER_SCALE = 2.0
MASKED = -1e30
F32 = jnp.float32
BF16 = jnp.bfloat16


def dot_nn(a, b):
    return lax.dot_general(a, b, (((1,), (0,)), ((), ())), preferred_element_type=F32)


def dot_tn(a, b):
    return lax.dot_general(a, b, (((0,), (0,)), ((), ())), preferred_element_type=F32)


def dot_nt(a, b):
    return lax.dot_general(a, b, (((1,), (1,)), ((), ())), preferred_element_type=F32)


def inverse_norm(rows):
    return lax.rsqrt(jnp.mean(rows * rows, axis=-1, keepdims=True) + EPS)


def norm_pull(rows, inv, gain, grad):
    scaled = gain * grad
    return inv * scaled - rows * (inv * inv * inv) * jnp.mean(rows * scaled, axis=-1, keepdims=True)


def rope_tables(pos):
    half = HD // 2
    freq = ROPE_BASE ** (-jnp.arange(half, dtype=F32) * 2.0 / HD)
    angle = pos.astype(F32)[:, None] * freq[None, :]
    cosine = jnp.concatenate([jnp.cos(angle), jnp.cos(angle)], axis=-1)[:, None, :]
    sine = jnp.concatenate([jnp.sin(angle), jnp.sin(angle)], axis=-1)[:, None, :]
    return cosine, sine


def rotate(values, cosine, sine):
    half = HD // 2
    rolled = jnp.concatenate([-values[..., half:], values[..., :half]], axis=-1)
    return values * cosine + rolled * sine


def unrotate(grads, cosine, sine):
    half = HD // 2
    turned = grads * sine
    return grads * cosine + jnp.concatenate([turned[..., half:], -turned[..., :half]], axis=-1)


def row_positions(deal, rows, block):
    owner = rows // (2 * block)
    local = rows % (2 * block)
    table = jnp.arange(deal.shape[0], dtype=jnp.int32)
    pair = jnp.sum(jnp.where(owner[:, None] == table[None, :], deal[None, :], 0), axis=1)
    return jnp.where(
        local < block, pair * block + local, (2 * deal.shape[0] - 1 - pair) * block + local - block
    )


def swap(value, axis, count, k):
    return lax.ppermute(value, axis, [(i, i ^ k) for i in range(count)])


def make_per_device(n_ctx, n_wa):
    def wa_exchange(value):
        return [value] + [swap(value, "wa", n_wa, k) for k in range(1, n_wa)]

    def gather_weight(shard):
        part = shard.shape[0] // n_ctx
        mine = lax.dynamic_slice_in_dim(shard, lax.axis_index("ctx") * part, part, 0)
        over_wa = lax.all_gather(mine, "wa", axis=0, tiled=False)
        over_all = lax.all_gather(over_wa, "ctx", axis=0, tiled=False)
        return over_all.transpose(1, 0, 2, 3).reshape(shard.shape[0] * n_wa, shard.shape[1])

    def per_device(
        tokens,
        cotangent,
        adapter_index,
        deal,
        w_qkv,
        b_qkv,
        w_o,
        w_gu,
        w_down,
        gain_attn,
        gain_mlp,
        a_qkv,
        b_q,
        b_kv,
        a_o,
        lift_o,
        a_gu,
        lift_gu,
        a_down,
        lift_down,
    ):
        rows, width = tokens.shape[1:]
        block = rows // 2
        rank = b_q.shape[1]
        slots = a_qkv.shape[0]
        kvd = b_kv.shape[3]
        heads = width // HD
        kvh = kvd // HD
        group = heads // kvh
        part_ff = w_down.shape[0]
        scale = 1.0 / math.sqrt(HD)
        wa = lax.axis_index("wa")
        ctx = lax.axis_index("ctx")
        chosen = adapter_index[0]

        def picked(table):
            return lax.dynamic_index_in_dim(table, chosen, 0, keepdims=False)

        grad_out_bf = cotangent[0]
        index_all = jnp.concatenate(wa_exchange(adapter_index))
        full_qkv = gather_weight(w_qkv)
        full_o = gather_weight(w_o)
        grads_all = jnp.concatenate(wa_exchange(grad_out_bf), axis=0)

        query_pos = row_positions(deal, ctx * rows + jnp.arange(rows, dtype=jnp.int32), block)
        key_pos = row_positions(deal, jnp.arange(n_ctx * rows, dtype=jnp.int32), block)
        mask = (key_pos[None, :] <= query_pos[:, None])[:, None, None, :]
        cosine, sine = rope_tables(query_pos)
        gain_one = gain_attn.astype(F32)
        gain_two = gain_mlp.astype(F32)
        x = tokens[0].astype(F32)
        s_aqkv, s_bq, s_bkv = picked(a_qkv), picked(b_q), picked(b_kv)
        s_ao, s_lo, s_agu, s_ld = picked(a_o), picked(lift_o), picked(a_gu), picked(lift_down)

        inv1 = inverse_norm(x)
        h1 = (x * inv1 * gain_one).astype(BF16)
        u1 = dot_nt(h1, s_aqkv).astype(BF16)
        extra = jnp.concatenate(
            [
                dot_nn(u1[:, :rank], s_bq),
                dot_nn(u1[:, rank : 2 * rank], s_bkv[0]),
                dot_nn(u1[:, 2 * rank :], s_bkv[1]),
            ],
            axis=1,
        )
        lin = dot_nn(h1, full_qkv) + b_qkv.astype(F32) + ADAPTER_SCALE * extra
        queries = rotate(lin[:, :width].reshape(rows, heads, HD), cosine, sine)
        queries = queries.astype(BF16).reshape(rows, kvh, group, HD)
        keys = rotate(lin[:, width : width + kvd].reshape(rows, kvh, HD), cosine, sine)
        kv_mine = jnp.concatenate([keys.reshape(rows, kvd), lin[:, width + kvd :]], axis=1)
        kv_all = lax.all_gather(kv_mine.astype(BF16), "ctx", axis=0, tiled=True)
        k_all = kv_all[:, :kvd].reshape(-1, kvh, HD)
        v_all = kv_all[:, kvd:].reshape(-1, kvh, HD)
        scores = jnp.einsum("tkgd,nkd->tkgn", queries, k_all, preferred_element_type=F32) * scale
        scores = jnp.where(mask, scores, MASKED)
        top = jnp.max(scores, axis=-1, keepdims=True)
        expo = jnp.exp(scores - top)
        total = jnp.sum(expo, axis=-1, keepdims=True)
        probs = expo / total
        probs_bf = probs.astype(BF16)
        attn = jnp.einsum("tkgn,nkd->tkgd", probs_bf, v_all, preferred_element_type=F32)
        ob = attn.reshape(rows, width).astype(BF16)
        uo = dot_nt(ob, s_ao).astype(BF16)
        x1 = x + dot_nn(ob, full_o) + ADAPTER_SCALE * dot_nn(uo, s_lo)
        inv2 = inverse_norm(x1)
        h2 = (x1 * inv2 * gain_two).astype(BF16)

        h2_all = jnp.concatenate(wa_exchange(h2), axis=0)
        row_index = jnp.repeat(index_all, rows)[:, None]

        def own_slot(values, wide):
            lane = lax.broadcasted_iota(jnp.int32, (1, values.shape[1]), 1)
            return jnp.where(lane // wide == row_index, values, 0.0).astype(BF16)

        first = wa * part_ff
        lift_g = lax.dynamic_slice_in_dim(lift_gu[:, 0], first, part_ff, 2).reshape(-1, part_ff)
        lift_u = lax.dynamic_slice_in_dim(lift_gu[:, 1], first, part_ff, 2).reshape(-1, part_ff)
        down_a = lax.dynamic_slice_in_dim(a_down, first, part_ff, 2).reshape(-1, part_ff)
        ug_g = own_slot(dot_nt(h2_all, a_gu[:, :rank].reshape(-1, width)), rank)
        ug_u = own_slot(dot_nt(h2_all, a_gu[:, rank:].reshape(-1, width)), rank)
        gate = dot_nn(h2_all, w_gu[0]) + ADAPTER_SCALE * dot_nn(ug_g, lift_g)
        up = dot_nn(h2_all, w_gu[1]) + ADAPTER_SCALE * dot_nn(ug_u, lift_u)
        sigma = jax.nn.sigmoid(gate)
        swish = gate * sigma
        hidden = (swish * up).astype(BF16)
        dud = own_slot(
            ADAPTER_SCALE * dot_nt(grads_all, lift_down.reshape(-1, width)), rank
        )
        g_adown = dot_tn(dud, hidden)
        d_hidden = dot_nt(grads_all, w_down) + dot_nn(dud, down_a)
        d_gate = (d_hidden * up * (sigma * (1.0 + gate * (1.0 - sigma)))).astype(BF16)
        d_up = (d_hidden * swish).astype(BF16)
        g_bgu = ADAPTER_SCALE * jnp.stack([dot_tn(ug_g, d_gate), dot_tn(ug_u, d_up)])
        out_part = dot_nn(hidden, w_down).astype(BF16)
        ud_part = dot_nt(hidden, down_a)
        d_h2_part = (dot_nt(d_gate, w_gu[0]) + dot_nt(d_up, w_gu[1])).astype(BF16)
        dug_g = ADAPTER_SCALE * dot_nt(d_gate, lift_g)
        dug_u = ADAPTER_SCALE * dot_nt(d_up, lift_u)

        def own_columns(values, k):
            mine = values[k * rows : (k + 1) * rows].reshape(rows, slots, rank)
            hot = (jnp.arange(slots) == index_all[k])[None, :, None]
            return jnp.sum(jnp.where(hot, mine, 0.0), axis=1)

        def wa_collect(parts):
            total = parts[0].astype(F32)
            for k in range(1, n_wa):
                total = total + swap(parts[k], "wa", n_wa, k).astype(F32)
            return total

        d_h2_sent = [d_h2_part[k * rows : (k + 1) * rows] for k in range(n_wa)]
        small_sent = [
            jnp.concatenate(
                [own_columns(dug_g, k), own_columns(dug_u, k), own_columns(ud_part, k)], axis=1
            )
            for k in range(n_wa)
        ]
        small = wa_collect(small_sent).astype(BF16)
        dug, ud = small[:, : 2 * rank], small[:, 2 * rank :]
        d_h2 = wa_collect(d_h2_sent) + dot_nn(dug, s_agu)
        out = (
            x1
            + wa_collect([out_part[k * rows : (k + 1) * rows] for k in range(n_wa)])
            + ADAPTER_SCALE * dot_nn(ud, s_ld)
        ).astype(BF16)
        g_ld = ADAPTER_SCALE * dot_tn(ud, grad_out_bf)
        g_agu = dot_tn(dug, h2)

        d_x1 = grad_out_bf.astype(F32) + norm_pull(x1, inv2, gain_two, d_h2)
        go = d_x1.astype(BF16)
        duo = (ADAPTER_SCALE * dot_nt(go, s_lo)).astype(BF16)
        g_lo = ADAPTER_SCALE * dot_tn(uo, go)
        g_ao = dot_tn(duo, ob)
        dob = (dot_nt(go, full_o) + dot_nn(duo, s_ao)).astype(BF16).reshape(rows, kvh, group, HD)
        delta = jnp.sum(dob.astype(F32) * attn, axis=-1, keepdims=True)
        d_values = jnp.einsum("tkgn,tkgd->nkd", probs_bf, dob, preferred_element_type=F32)
        d_probs = jnp.einsum("tkgd,nkd->tkgn", dob, v_all, preferred_element_type=F32)
        ds = (probs * (d_probs - delta)).astype(BF16)
        d_query = jnp.einsum("tkgn,nkd->tkgd", ds, k_all, preferred_element_type=F32) * scale
        d_keys = jnp.einsum("tkgn,tkgd->nkd", ds, queries, preferred_element_type=F32) * scale
        d_kv_part = jnp.concatenate([d_keys.reshape(-1, kvd), d_values.reshape(-1, kvd)], axis=1)
        d_kv = lax.all_to_all(d_kv_part.astype(BF16), "ctx", 0, 0, tiled=True)
        d_kv = jnp.sum(d_kv.reshape(n_ctx, rows, 2 * kvd).astype(F32), axis=0)
        d_q_lin = unrotate(d_query.reshape(rows, heads, HD), cosine, sine).reshape(rows, width)
        d_k_lin = unrotate(d_kv[:, :kvd].reshape(rows, kvh, HD), cosine, sine).reshape(rows, kvd)
        d_lin = jnp.concatenate([d_q_lin, d_k_lin, d_kv[:, kvd:]], axis=1).astype(BF16)
        dl_q, dl_k, dl_v = d_lin[:, :width], d_lin[:, width : width + kvd], d_lin[:, width + kvd :]
        du1 = (
            ADAPTER_SCALE
            * jnp.concatenate(
                [dot_nt(dl_q, s_bq), dot_nt(dl_k, s_bkv[0]), dot_nt(dl_v, s_bkv[1])], axis=1
            )
        ).astype(BF16)
        g_bq = ADAPTER_SCALE * dot_tn(u1[:, :rank], dl_q)
        g_bk = ADAPTER_SCALE * dot_tn(u1[:, rank : 2 * rank], dl_k)
        g_bv = ADAPTER_SCALE * dot_tn(u1[:, 2 * rank :], dl_v)
        g_aqkv = dot_tn(du1, h1)
        d_h1 = dot_nt(d_lin, full_qkv) + dot_nn(du1, s_aqkv)
        grad_x = d_x1 + norm_pull(x, inv1, gain_one, d_h1)

        def reduce_share(flat):
            count = flat.shape[0]
            padded = -(-count // (n_ctx * 1024)) * n_ctx * 1024
            flat = jnp.pad(flat, (0, padded - count)).reshape(n_ctx, -1, 128).astype(BF16)
            got = lax.all_to_all(flat, "ctx", 0, 0, tiled=True)
            return jnp.sum(got.astype(F32), axis=0).astype(BF16)

        def share_all(share, count):
            over_wa = lax.all_gather(share, "wa", axis=0, tiled=False)
            got = lax.all_gather(over_wa, "ctx", axis=0, tiled=False)
            return got.transpose(1, 0, 2, 3).reshape(n_wa, -1)[:, :count]

        ff_flat = jnp.concatenate(
            [g_bgu.reshape(2, slots, rank, part_ff).transpose(1, 0, 2, 3).ravel(), g_adown.ravel()]
        )
        seq_parts = [g_aqkv, g_bq, g_bk, g_bv, g_ao, g_lo, g_agu, g_ld]
        seq_flat = jnp.concatenate([part.ravel() for part in seq_parts])
        ff_all = share_all(reduce_share(ff_flat), ff_flat.shape[0])
        seq_all = share_all(reduce_share(seq_flat), seq_flat.shape[0])
        cut = slots * 2 * rank * part_ff
        r_bgu = ff_all[:, :cut].reshape(n_wa, slots, 2, rank, part_ff).astype(F32)
        r_bgu = r_bgu.transpose(1, 2, 3, 0, 4).reshape(slots, 2, rank, n_wa * part_ff)
        r_ad = ff_all[:, cut:].reshape(n_wa, slots, rank, part_ff).astype(F32)
        r_ad = r_ad.transpose(1, 2, 0, 3).reshape(slots, rank, n_wa * part_ff)
        own = lax.dynamic_update_slice(jnp.zeros((n_wa,), jnp.int32), adapter_index, (wa,))
        for k in range(1, n_wa):
            own = lax.dynamic_update_slice(own, index_all[k : k + 1], (wa ^ k,))
        hot = (own[None, :] == jnp.arange(slots)[:, None]).astype(F32)
        by_slot = jnp.sum(hot[:, :, None] * seq_all[None].astype(F32), axis=1)
        results = []
        at = 0
        for part in seq_parts:
            results.append(by_slot[:, at : at + part.size].reshape((slots,) + part.shape))
            at += part.size
        r_aqkv, r_bq, r_bk, r_bv, r_ao, r_lo, r_agu, r_ld = results
        return (
            out[None],
            grad_x[None],
            r_aqkv,
            r_bq,
            jnp.stack([r_bk, r_bv], axis=1),
            r_ao,
            r_lo,
            r_agu,
            r_bgu,
            r_ad,
            r_ld,
        )

    return per_device


def solution(mesh):
    rep = P()
    return jax.shard_map(
        make_per_device(mesh.shape["ctx"], mesh.shape["wa"]),
        mesh=mesh,
        in_specs=(
            P("wa", "ctx", None),
            P("wa", "ctx", None),
            P("wa"),
            rep,
            P("wa", None),
            rep,
            P("wa", None),
            P(None, None, "wa"),
            P("wa", None),
        )
        + (rep,) * 11,
        out_specs=(P("wa", "ctx", None), P("wa", "ctx", None)) + (rep,) * 9,
        check_vma=False,
    )
```

```python
import functools
import math

import jax
import jax.numpy as jnp
from jax import lax
from jax.experimental import pallas as pl
from jax.experimental.pallas import tpu as pltpu
from jax.sharding import PartitionSpec as P

HD = 128
EPS = 1e-06
ROPE_BASE = 1000000.0
ADAPTER_SCALE = 2.0
MASKED = -1e30
F32 = jnp.float32
BF16 = jnp.bfloat16


def dot_nn(a, b):
    return lax.dot_general(a, b, (((1,), (0,)), ((), ())), preferred_element_type=F32)


def dot_tn(a, b):
    return lax.dot_general(a, b, (((0,), (0,)), ((), ())), preferred_element_type=F32)


def dot_nt(a, b):
    return lax.dot_general(a, b, (((1,), (1,)), ((), ())), preferred_element_type=F32)


def inverse_norm(rows):
    return lax.rsqrt(jnp.mean(rows * rows, axis=-1, keepdims=True) + EPS)


def norm_pull(rows, inv, gain, grad):
    scaled = gain * grad
    return inv * scaled - rows * (inv * inv * inv) * jnp.mean(rows * scaled, axis=-1, keepdims=True)


def rope_tables(pos):
    half = HD // 2
    freq = ROPE_BASE ** (-jnp.arange(half, dtype=F32) * 2.0 / HD)
    angle = pos.astype(F32)[:, None] * freq[None, :]
    cosine, sine = jnp.cos(angle), jnp.sin(angle)
    return jnp.concatenate([cosine, cosine], axis=1), jnp.concatenate([-sine, sine], axis=1)


def row_positions(deal, rows, block):
    owner = rows // (2 * block)
    local = rows % (2 * block)
    table = jnp.arange(deal.shape[0], dtype=jnp.int32)
    pair = jnp.sum(jnp.where(owner[:, None] == table[None, :], deal[None, :], 0), axis=1)
    return jnp.where(
        local < block, pair * block + local, (2 * deal.shape[0] - 1 - pair) * block + local - block
    )


def ff_results_kernel(wa_ref, got_ref, bgu_ref, ad_ref, *, part_ff):
    n_ctx, n_wa, _, lanes = got_ref.shape
    own = wa_ref[0]
    rank = bgu_ref.shape[2]
    b_rows = bgu_ref.shape[0] * 2 * rank // n_ctx
    a_rows = ad_ref.shape[0] * rank // n_ctx
    starts = [j * part_ff // 128 * 128 for j in range(n_wa)]

    def write(read, store):
        left = None
        for j in range(n_wa):
            block = read(j).astype(F32)
            stop = starts[j + 1] - starts[j] if j + 1 < n_wa else lanes
            if left is not None:
                store(starts[j], block[:, :128] + left)
            first = 0 if left is None else 128
            store(starts[j] + first, block[:, first:stop])
            left = block[:, stop:] if stop < lanes else None

    for c in range(n_ctx):
        at = c * b_rows
        slot, half, low = at // (2 * rank), at // rank % 2, at % rank

        def put_b(lane, value):
            bgu_ref[slot, half, low : low + b_rows, lane : lane + value.shape[1]] = value

        write(lambda j: got_ref[c, own ^ j, :b_rows], put_b)
        at = c * a_rows
        slot, low = at // rank, at % rank

        def put_a(lane, value):
            ad_ref[slot, low : low + a_rows, lane : lane + value.shape[1]] = value

        write(lambda j: got_ref[c, own ^ j, b_rows:], put_a)


def ff_results(wa, got, slots, rank, part_ff):
    n_wa = got.shape[1]
    return pl.pallas_call(
        lambda *refs: ff_results_kernel(*refs, part_ff=part_ff),
        out_shape=(
            jax.ShapeDtypeStruct((slots, 2, rank, n_wa * part_ff), F32),
            jax.ShapeDtypeStruct((slots, rank, n_wa * part_ff), F32),
        ),
        in_specs=[pl.BlockSpec(memory_space=pltpu.SMEM), pl.BlockSpec(memory_space=pltpu.VMEM)],
        out_specs=(pl.BlockSpec(memory_space=pltpu.VMEM),) * 2,
        compiler_params=pltpu.CompilerParams(vmem_limit_bytes=48 << 20),
    )(wa, got)


def seq_results_kernel(wa_ref, index_ref, got_ref, *refs, layout):
    n_ctx, n_wa, share, third = got_ref.shape
    share = share // 3
    whole_refs, out_refs = refs[:n_wa], refs[n_wa:]
    own = wa_ref[0]
    slots = out_refs[0].shape[0]
    hot = [[index_ref[k] == slot for k in range(n_wa)] for slot in range(slots)]
    for c in range(n_ctx):
        for part in range(3):
            terms = [
                got_ref[c, own ^ j, part * share : (part + 1) * share, :].astype(F32)
                for j in range(n_wa)
            ]
            for slot in range(slots):
                total = jnp.zeros((share, third), F32)
                for j in range(n_wa):
                    total = total + jnp.where(index_ref[own ^ j] == slot, terms[j], 0.0)
                for out, first, count in layout:
                    low, high = max(first, c * share), min(first + count, (c + 1) * share)
                    if low >= high:
                        continue
                    value = total[low - c * share : high - c * share]
                    ref = out_refs[out]
                    if len(ref.shape) == 3:
                        lane = slice(part * third, (part + 1) * third)
                        ref[slot, low - first : high - first, lane] = value
                    elif part == 0:
                        wide = ref.shape[3]
                        for i in range(ref.shape[1]):
                            cut = value[:, i * wide : (i + 1) * wide]
                            ref[slot, i, low - first : high - first, :] = cut
    for slot in range(slots):
        total = jnp.zeros(whole_refs[0].shape, F32)
        for j in range(n_wa):
            value = jnp.zeros(whole_refs[0].shape, F32)
            for k in range(n_wa):
                take = jnp.logical_and(own ^ j == k, hot[slot][k])
                value = value + jnp.where(take, whole_refs[k][...].astype(F32), 0.0)
            total = total + value
        out_refs[0][slot] = total


def seq_results(wa, index_all, got, wholes, shapes, layout):
    smem = pl.BlockSpec(memory_space=pltpu.SMEM)
    vmem = pl.BlockSpec(memory_space=pltpu.VMEM)
    return pl.pallas_call(
        lambda *refs: seq_results_kernel(*refs, layout=layout),
        out_shape=tuple(jax.ShapeDtypeStruct(shape, F32) for shape in shapes),
        in_specs=[smem, smem] + [vmem] * (1 + len(wholes)),
        out_specs=(vmem,) * len(shapes),
        compiler_params=pltpu.CompilerParams(vmem_limit_bytes=48 << 20),
    )(wa, index_all, got, *wholes)


def local_call(kernel, out_shapes, *args, scratch=(), limit=56):
    vmem = pl.BlockSpec(memory_space=pltpu.VMEM)
    return pl.pallas_call(
        kernel,
        out_shape=tuple(jax.ShapeDtypeStruct(shape, kind) for shape, kind in out_shapes),
        in_specs=[vmem] * len(args),
        out_specs=(vmem,) * len(out_shapes),
        scratch_shapes=list(scratch),
        compiler_params=pltpu.CompilerParams(vmem_limit_bytes=limit << 20),
    )(*args)


def project_kernel(h1_ref, w_ref, a_ref, b_ref, bias_ref, sent_ref, u1_ref, *, q_cols):
    n_ctx, rows, wide = sent_ref.shape
    kv_cols = w_ref.shape[1] - q_cols
    h1 = h1_ref[...]
    u1 = dot_nt(h1, a_ref[...]).astype(BF16)
    u1_ref[...] = u1
    lin = dot_nn(h1, w_ref[...]) + bias_ref[...] + ADAPTER_SCALE * dot_nn(u1, b_ref[...])
    lin = lin.astype(BF16)
    pieces = [lin[c * rows : (c + 1) * rows, q_cols:] for c in range(n_ctx)]
    kv = jnp.concatenate(pieces, axis=1)
    fill = jnp.zeros((rows, wide - n_ctx * kv_cols - q_cols), BF16)
    for c in range(n_ctx):
        sent_ref[c, :, : n_ctx * kv_cols] = kv
        own = lin[c * rows : (c + 1) * rows, :q_cols]
        sent_ref[c, :, n_ctx * kv_cols :] = jnp.concatenate([own, fill], axis=1)


def turn(value, cosine, sine):
    return value * cosine + pltpu.roll(value, HD // 2, 1) * sine


def turn_back(value, cosine, sine):
    return value * cosine + pltpu.roll(value * sine, HD // 2, 1)


def heads_stacked(table, first, group):
    return jnp.concatenate(
        [table[:, (first + j) * HD : (first + j + 1) * HD] for j in range(group)], axis=0
    )


def attend_kernel(
    got_ref, cos_ref, sin_ref, kcos_ref, ksin_ref, qpos_ref, kpos_ref, x_ref, wo_ref, ao_ref,
    lo_ref, gain_ref, qb_ref, kb_ref, vb_ref, lse_ref, attn_ref, ob_ref, uo_ref, x1_ref, h2_ref,
):
    n_ctx = got_ref.shape[0]
    rows, width = x_ref.shape
    kvd = kb_ref.shape[1]
    kvh, heads = kvd // HD, width // HD
    group = heads // kvh
    q_cols, kv_cols = width // n_ctx, 2 * kvd // n_ctx
    scale = 1.0 / math.sqrt(HD)
    cosine, sine = cos_ref[...], sin_ref[...]
    q_lin = jnp.concatenate(
        [got_ref[c, :, 2 * kvd : 2 * kvd + q_cols] for c in range(n_ctx)], axis=1
    )
    for h in range(heads):
        lane = slice(h * HD, (h + 1) * HD)
        qb_ref[:, lane] = turn(q_lin[:, lane].astype(F32), cosine, sine).astype(BF16)
    for g in range(n_ctx):
        at = slice(g * rows, (g + 1) * rows)
        cut = slice(g * kv_cols, (g + 1) * kv_cols)
        kv_lin = jnp.concatenate([got_ref[c, :, cut] for c in range(n_ctx)], axis=1)
        kcos, ksin = kcos_ref[at, :], ksin_ref[at, :]
        for h in range(kvh):
            lane = slice(h * HD, (h + 1) * HD)
            kb_ref[at, lane] = turn(kv_lin[:, lane].astype(F32), kcos, ksin).astype(BF16)
        vb_ref[at, :] = kv_lin[:, kvd:]
    qpos = jnp.concatenate([qpos_ref[...]] * group, axis=0)
    seen = kpos_ref[...] <= qpos
    for g in range(kvh):
        q = heads_stacked(qb_ref, g * group, group)
        s = dot_nt(q, kb_ref[:, g * HD : (g + 1) * HD]) * scale
        s = jnp.where(seen, s, MASKED)
        top = jnp.max(s, axis=1, keepdims=True)
        e = jnp.exp(s - top)
        total = jnp.sum(e, axis=1, keepdims=True)
        lse_ref[g] = top + jnp.log(total)
        pb = (e * (1.0 / total)).astype(BF16)
        o = dot_nn(pb, vb_ref[:, g * HD : (g + 1) * HD])
        for j in range(group):
            lane = slice((g * group + j) * HD, (g * group + j + 1) * HD)
            attn_ref[:, lane] = o[j * rows : (j + 1) * rows]
    ob = attn_ref[...].astype(BF16)
    ob_ref[...] = ob
    uo = dot_nt(ob, ao_ref[...]).astype(BF16)
    uo_ref[...] = uo
    x1 = x_ref[...].astype(F32) + dot_nn(ob, wo_ref[...])
    x1 = x1 + ADAPTER_SCALE * dot_nn(uo, lo_ref[...])
    x1_ref[...] = x1
    h2_ref[...] = (x1 * inverse_norm(x1) * gain_ref[...]).astype(BF16)


def attend_back_kernel(*refs, n_wa, n_ctx):
    parts, refs = refs[:n_wa], refs[n_wa:]
    (
        agu_ref, gain_ref, x1_ref, g_ref, h2_ref, wo_ref, lo_ref, ao_ref, attn_ref, ob_ref, uo_ref,
        qb_ref, kb_ref, vb_ref, lse_ref, qpos_ref, kpos_ref, cos_ref, sin_ref, kcos_ref, ksin_ref,
        u1_ref, u1all_ref, dx1_ref, dlq_ref, sent_ref, ud_ref, dob, dq_acc, grads,
    ) = refs
    rows, width = x1_ref.shape
    keys, kvd = kb_ref.shape
    kvh, heads = kvd // HD, width // HD
    group = heads // kvh
    rank = uo_ref.shape[1]
    scale = 1.0 / math.sqrt(HD)
    got = parts[0][...].astype(F32)
    for part in parts[1:]:
        got = got + part[...].astype(F32)
    small = got[:, width : width + 3 * rank].astype(BF16)
    dug, ud = small[:, : 2 * rank], small[:, 2 * rank :]
    ud_ref[...] = ud
    d_h2 = got[:, :width] + dot_nn(dug, agu_ref[...])
    x1 = x1_ref[...]
    g = g_ref[...]
    d_x1 = g.astype(F32) + norm_pull(x1, inverse_norm(x1), gain_ref[...], d_h2)
    dx1_ref[...] = d_x1
    go = d_x1.astype(BF16)
    duo = (ADAPTER_SCALE * dot_nt(go, lo_ref[...])).astype(BF16)
    grads[: 2 * rank] = dot_tn(dug, h2_ref[...])
    grads[2 * rank : 3 * rank] = ADAPTER_SCALE * dot_tn(ud, g)
    grads[3 * rank : 4 * rank] = dot_tn(duo, ob_ref[...])
    grads[4 * rank : 5 * rank] = ADAPTER_SCALE * dot_tn(uo_ref[...], go)
    dob[...] = (dot_nt(go, wo_ref[...]) + dot_nn(duo, ao_ref[...])).astype(BF16)
    qpos = jnp.concatenate([qpos_ref[...]] * group, axis=0)
    step = math.gcd(keys, 1024)
    share = step // rows
    grads[6 * rank :] = jnp.zeros((2 * rank, width), F32)
    for kv in range(kvh):
        lane = slice(kv * HD, (kv + 1) * HD)
        v_lane = slice(kvd + kv * HD, kvd + (kv + 1) * HD)
        q = heads_stacked(qb_ref, kv * group, group)
        do = heads_stacked(dob, kv * group, group)
        o = heads_stacked(attn_ref, kv * group, group)
        delta = jnp.sum(do.astype(F32) * o, axis=1, keepdims=True)
        lse = lse_ref[kv]
        dq_acc[...] = jnp.zeros_like(dq_acc)

        def visit(turn_index):
            at = pl.ds(pl.multiple_of(turn_index * step, step), step)
            k = kb_ref[at, lane]
            s = dot_nt(q, k) * scale
            seen = kpos_ref[:, at] <= qpos
            p = jnp.exp(jnp.where(seen, s, MASKED) - lse)
            dp = dot_nt(do, vb_ref[at, lane])
            ds = (p * (dp - delta)).astype(BF16)
            dq_acc[...] += dot_nn(ds, k)
            dk = turn_back(dot_tn(ds, q) * scale, kcos_ref[at, :], ksin_ref[at, :]).astype(BF16)
            dv = dot_tn(p.astype(BF16), do).astype(BF16)
            u1 = u1all_ref[at, :]
            grads[6 * rank : 7 * rank, lane] += dot_tn(u1[:, rank : 2 * rank], dk)
            grads[6 * rank : 7 * rank, v_lane] += dot_tn(u1[:, 2 * rank :], dv)
            owners = pl.ds(turn_index * share, share)
            sent_ref[owners, :rows, lane] = dk.reshape(share, rows, HD)
            sent_ref[owners, :rows, v_lane] = dv.reshape(share, rows, HD)

        if keys == step:
            visit(0)
        else:
            pl.loop(0, keys // step)(visit)
        for j in range(group):
            head = slice((kv * group + j) * HD, (kv * group + j + 1) * HD)
            dq = dq_acc[j * rows : (j + 1) * rows] * scale
            dlq_ref[:, head] = turn_back(dq, cos_ref[...], sin_ref[...]).astype(BF16)
    grads[5 * rank : 6 * rank] = ADAPTER_SCALE * dot_tn(u1_ref[:, :rank], dlq_ref[...])
    grads[6 * rank : 7 * rank] = grads[6 * rank : 7 * rank] * ADAPTER_SCALE
    count = 8 * rank // n_ctx
    third = width // 3
    for c in range(n_ctx):
        for i in range(3):
            at = rows + i * count
            value = grads[c * count : (c + 1) * count, i * third : (i + 1) * third]
            sent_ref[c, at : at + count, :] = value.astype(BF16)


def collect_kernel(got_ref, dlq_ref, bq_ref, bkv_ref, dlkv_ref, du1_ref, share_ref):
    rows = dlq_ref.shape[0]
    rank = bq_ref.shape[0]
    kvd = bkv_ref.shape[2]
    total = got_ref[0].astype(F32)
    for c in range(1, got_ref.shape[0]):
        total = total + got_ref[c].astype(F32)
    dlkv = total[:rows].astype(BF16)
    dlkv_ref[...] = dlkv
    share_ref[...] = total[rows:].astype(BF16)
    du1 = [
        dot_nt(dlq_ref[...], bq_ref[...]),
        dot_nt(dlkv[:, :kvd], bkv_ref[0]),
        dot_nt(dlkv[:, kvd:], bkv_ref[1]),
    ]
    du1_ref[...] = (ADAPTER_SCALE * jnp.concatenate(du1, axis=1)).astype(BF16)


def finish_kernel(*refs, n_wa):
    parts, refs = refs[:n_wa], refs[n_wa:]
    (
        x1_ref, ud_ref, ld_ref, x_ref, gain_ref, dx1_ref, dlq_ref, dlkv_ref, du1_ref, w_ref, a_ref,
        out_ref, gx_ref,
    ) = refs
    n_ctx = w_ref.shape[0]
    q_cols, kv_cols = dlq_ref.shape[1] // n_ctx, dlkv_ref.shape[1] // n_ctx
    out = x1_ref[...] + ADAPTER_SCALE * dot_nn(ud_ref[...], ld_ref[...])
    for part in parts:
        out = out + part[...].astype(F32)
    out_ref[...] = out.astype(BF16)
    d_h1 = dot_nn(du1_ref[...], a_ref[...])
    for c in range(n_ctx):
        block = jnp.concatenate(
            [
                dlq_ref[:, c * q_cols : (c + 1) * q_cols],
                dlkv_ref[:, c * kv_cols : (c + 1) * kv_cols],
            ],
            axis=1,
        )
        d_h1 = d_h1 + dot_nt(block, w_ref[c])
    x = x_ref[...].astype(F32)
    gx_ref[...] = dx1_ref[...] + norm_pull(x, inverse_norm(x), gain_ref[...], d_h1)


def mlp_kernel(*refs, chunks, part_ff, tile, last):
    refs = list(refs)
    index_ref, shift_ref = refs[:2]
    h2_refs, g_refs = refs[2 : 2 + chunks], refs[2 + chunks : 2 + 2 * chunks]
    refs = refs[2 + 2 * chunks :]
    agu_ref, ld_ref, gu_ref, down_ref, lift_ref, ad_ref, prior_ref = refs[:7]
    refs = refs[7:]
    out_refs, dh_refs = refs[:chunks], refs[chunks : 2 * chunks]
    grads_ref = refs[2 * chunks]
    h2, gd, low, low_t, out_acc, dh_acc, small_acc, grads = refs[2 * chunks + 1 :]
    rows, width = h2_refs[0].shape
    slots, _, rank, _ = lift_ref.shape
    span = slots * rank
    step, steps = pl.program_id(0), pl.num_programs(0)

    def row_slot(lanes):
        return jnp.concatenate(
            [jnp.full((rows, lanes), index_ref[k], jnp.int32) for k in range(chunks)], axis=0
        )

    @pl.when(step == 0)
    def _():
        for k in range(chunks):
            h2[k * rows : (k + 1) * rows, :] = h2_refs[k][...]
            gd[k * rows : (k + 1) * rows, :] = g_refs[k][...]
        out_acc[...] = jnp.zeros_like(out_acc)
        dh_acc[...] = jnp.zeros_like(dh_acc)
        small_acc[...] = jnp.zeros_like(small_acc)
        grads[...] = prior_ref[...]
        lane = lax.broadcasted_iota(jnp.int32, (chunks * rows, span), 1)
        own = lane // rank == row_slot(span)
        flat_a = agu_ref[...]
        parts = [
            dot_nt(h2[...], flat_a[:, :rank].reshape(span, width)).astype(BF16),
            dot_nt(h2[...], flat_a[:, rank:].reshape(span, width)).astype(BF16),
            dot_nt(gd[...], ld_ref[...].reshape(span, width)).astype(BF16),
        ]
        for i, part in enumerate(parts):
            value = jnp.where(own, part.astype(F32) * ADAPTER_SCALE, 0.0)
            low[i] = value.astype(BF16)
            low_t[i] = value.T.astype(BF16)

    def work(first, wide):
        lanes = pl.ds(first, wide)
        w_g, w_u = gu_ref[0, :wide, :], gu_ref[1, :wide, :]
        w_d = down_ref[:wide, :]
        l_g = lift_ref[:, 0, :, :wide].reshape(span, wide)
        l_u = lift_ref[:, 1, :, :wide].reshape(span, wide)
        a_d = ad_ref[:, :, :wide].reshape(span, wide)
        gate = dot_nt(h2[...], w_g) + dot_nn(low[0], l_g)
        up = dot_nt(h2[...], w_u) + dot_nn(low[1], l_u)
        sigma = 1.0 / (1.0 + jnp.exp(-gate))
        swish = gate * sigma
        hidden = (swish * up).astype(BF16)
        d_hidden = dot_nt(gd[...], w_d) + dot_nn(low[2], a_d)
        d_gate = (d_hidden * up * (sigma + swish * (1.0 - sigma))).astype(BF16)
        d_up = (d_hidden * swish).astype(BF16)
        out_acc[...] += dot_nn(hidden, w_d)
        dh_acc[...] += dot_nn(d_gate, w_g) + dot_nn(d_up, w_u)
        small_acc[0] += dot_nt(d_gate, l_g)
        small_acc[1] += dot_nt(d_up, l_u)
        small_acc[2] += dot_nt(hidden, a_d)
        grads[0, :, lanes] += dot_nn(low_t[0], d_gate)
        grads[1, :, lanes] += dot_nn(low_t[1], d_up)
        grads[2, :, lanes] += dot_nn(low_t[2], hidden)

    rest = part_ff % tile
    if rest:
        pl.when(step < steps - 1)(lambda: work(pl.multiple_of(step * tile, tile), tile))
        pl.when(step == steps - 1)(lambda: work(part_ff - rest, rest))
    else:
        work(pl.multiple_of(step * tile, tile), tile)

    @pl.when(step == steps - 1)
    def _():
        for k in range(chunks):
            at = slice(k * rows, (k + 1) * rows)
            out_refs[k][...] = out_acc[at, :].astype(BF16)
            dh_refs[k][:, :width] = dh_acc[at, :].astype(BF16)
            picked = []
            for i in range(3):
                value = jnp.zeros((rows, rank), F32)
                for slot in range(slots):
                    mine = small_acc[i, at, slot * rank : (slot + 1) * rank]
                    value = value + jnp.where(index_ref[k] == slot, mine, 0.0)
                picked.append(value * (ADAPTER_SCALE if i < 2 else 1.0))
            picked.append(jnp.zeros((rows, 128 - 3 * rank), F32))
            dh_refs[k][:, width:] = jnp.concatenate(picked, axis=1).astype(BF16)
        if not last:
            grads_ref[...] = grads[...]
        else:
            n_ctx = grads_ref.shape[0]
            b_rows, a_rows = 2 * span // n_ctx, span // n_ctx
            odd = shift_ref[0] != 0
            tables = []
            for i in range(3):
                value = grads[i]
                if rest % 128:
                    value = jnp.where(odd, pltpu.roll(value, part_ff % 128, 1), value)
                tables.append(value.astype(BF16))
            for c in range(n_ctx):
                at = c * b_rows
                slot, half, at = at // (2 * rank), at // rank % 2, at % rank
                at += slot * rank
                grads_ref[c, :b_rows, :] = tables[half][at : at + b_rows]
                grads_ref[c, b_rows:, :] = tables[2][c * a_rows : (c + 1) * a_rows]


def mlp_call(index, shift, h2s, gs, a_gu, lift_down, w_gu, w_down, lift, a_down, prior, n_ctx):
    chunks = len(h2s)
    rows, width = h2s[0].shape
    part_ff = w_down.shape[0]
    slots, _, rank, _ = lift.shape
    span = slots * rank
    tile = 256
    steps = -(-part_ff // tile)
    lanes = prior.shape[2]
    smem = pl.BlockSpec(memory_space=pltpu.SMEM)

    def whole(shape):
        return pl.BlockSpec(shape, lambda i: (0,) * len(shape))

    if n_ctx is None:
        grads_shape = jax.ShapeDtypeStruct((3, span, lanes), F32)
    else:
        grads_shape = jax.ShapeDtypeStruct((n_ctx, 3 * span // n_ctx, lanes), BF16)
    total = chunks * rows
    outs = pl.pallas_call(
        lambda *refs: mlp_kernel(
            *refs, chunks=chunks, part_ff=part_ff, tile=tile, last=n_ctx is not None
        ),
        grid=(steps,),
        out_shape=(jax.ShapeDtypeStruct((rows, width), BF16),) * chunks
        + (jax.ShapeDtypeStruct((rows, width + 128), BF16),) * chunks
        + (grads_shape,),
        in_specs=[smem, smem]
        + [whole((rows, width))] * (2 * chunks)
        + [
            whole(a_gu.shape),
            whole(lift_down.shape),
            pl.BlockSpec((2, tile, width), lambda i: (0, i, 0)),
            pl.BlockSpec((tile, width), lambda i: (i, 0)),
            pl.BlockSpec((slots, 2, rank, tile), lambda i: (0, 0, 0, i)),
            pl.BlockSpec((slots, rank, tile), lambda i: (0, 0, i)),
            whole(prior.shape),
        ],
        out_specs=(whole((rows, width)),) * chunks
        + (whole((rows, width + 128)),) * chunks
        + (whole(grads_shape.shape),),
        scratch_shapes=[
            pltpu.VMEM((total, width), BF16),
            pltpu.VMEM((total, width), BF16),
            pltpu.VMEM((3, total, span), BF16),
            pltpu.VMEM((3, span, total), BF16),
            pltpu.VMEM((total, width), F32),
            pltpu.VMEM((total, width), F32),
            pltpu.VMEM((3, total, span), F32),
            pltpu.VMEM((3, span, lanes), F32),
        ],
        compiler_params=pltpu.CompilerParams(vmem_limit_bytes=50 << 20),
        cost_estimate=pl.CostEstimate(
            flops=12 * total * width * part_ff,
            bytes_accessed=6 * width * part_ff,
            transcendentals=0,
        ),
    )(index, shift, *h2s, *gs, a_gu, lift_down, w_gu, w_down, lift, a_down, prior)
    return outs[:chunks], outs[chunks : 2 * chunks], outs[-1]


def swap(value, axis, count, k):
    return lax.ppermute(value, axis, [(i, i ^ k) for i in range(count)])


def make_per_device(n_ctx, n_wa):
    def wa_exchange(value):
        return [value] + [swap(value, "wa", n_wa, k) for k in range(1, n_wa)]

    def absolute(parts, axis):
        stacked = jnp.stack(parts)
        own = lax.axis_index(axis)
        return jnp.take(stacked, jnp.arange(len(parts)) ^ own, axis=0)

    def rows_over_wa(shard):
        part = shard.shape[0] // n_ctx
        mine = lax.dynamic_slice_in_dim(shard, lax.axis_index("ctx") * part, part, 0)
        return absolute(wa_exchange(mine), "wa")

    def rows_over_ctx(over_wa):
        got = lax.all_gather(over_wa, "ctx", axis=0, tiled=False)
        return got.transpose(1, 0, 2, 3).reshape(-1, over_wa.shape[2])

    def per_device(
        tokens,
        cotangent,
        adapter_index,
        deal,
        w_qkv,
        b_qkv,
        w_o,
        w_gu,
        w_down,
        gain_attn,
        gain_mlp,
        a_qkv,
        b_q,
        b_kv,
        a_o,
        lift_o,
        a_gu,
        lift_gu,
        a_down,
        lift_down,
    ):
        rows, width = tokens.shape[1:]
        block = rows // 2
        rank = b_q.shape[1]
        slots = a_qkv.shape[0]
        kvd = b_kv.shape[3]
        heads = width // HD
        kvh = kvd // HD
        group = heads // kvh
        part_ff = w_down.shape[0]
        wa = lax.axis_index("wa")
        ctx = lax.axis_index("ctx")
        chosen = adapter_index[0]

        def picked(table):
            return lax.dynamic_index_in_dim(table, chosen, 0, keepdims=False)

        grad_out_bf = cotangent[0]
        x_bf = tokens[0]
        q_cols, kv_cols = width // n_ctx, 2 * kvd // n_ctx
        gain_one = gain_attn.astype(F32)[None]
        gain_two = gain_mlp.astype(F32)[None]
        s_aqkv, s_bq, s_bkv = picked(a_qkv), picked(b_q), picked(b_kv)
        s_ao, s_lo, s_agu, s_ld = picked(a_o), picked(lift_o), picked(a_gu), picked(lift_down)

        x = x_bf.astype(F32)
        h1 = (x * inverse_norm(x) * gain_one).astype(BF16)
        h1_all = lax.all_gather(h1, "ctx", axis=0, tiled=True)

        def block_of(table):
            return jnp.concatenate(
                [
                    lax.dynamic_slice_in_dim(table[:, :width], ctx * q_cols, q_cols, 1),
                    lax.dynamic_slice_in_dim(table[:, width:], ctx * kv_cols, kv_cols, 1),
                ],
                axis=1,
            )

        w_block = absolute(wa_exchange(block_of(w_qkv)), "wa").reshape(width, q_cols + kv_cols)
        w_block, w_o = lax.optimization_barrier((w_block, w_o))
        index_all = jnp.concatenate(wa_exchange(adapter_index))
        o_wa = rows_over_wa(w_o)
        o_wa, grad_sent = lax.optimization_barrier((o_wa, grad_out_bf))
        b_all = jnp.concatenate(
            [
                jnp.pad(s_bq, ((0, 0), (0, 2 * kvd))),
                jnp.pad(s_bkv[0], ((0, 0), (width, kvd))),
                jnp.pad(s_bkv[1], ((0, 0), (width + kvd, 0))),
            ],
            axis=0,
        )
        key_pos = row_positions(deal, jnp.arange(n_ctx * rows, dtype=jnp.int32), block)
        key_cos, key_sin = rope_tables(key_pos)

        def own_rows(table):
            return lax.dynamic_slice_in_dim(table, ctx * rows, rows, 0)

        query_pos, cosine, sine = own_rows(key_pos)[:, None], own_rows(key_cos), own_rows(key_sin)
        key_pos = key_pos[None]
        sent, u1_all = local_call(
            functools.partial(project_kernel, q_cols=q_cols),
            [
                ((n_ctx, rows, -(-(2 * kvd + q_cols) // 128) * 128), BF16),
                ((n_ctx * rows, 3 * rank), BF16),
            ],
            h1_all,
            w_block,
            s_aqkv,
            block_of(b_all),
            block_of(b_qkv[None]).astype(F32),
        )
        grads_all = wa_exchange(grad_sent)
        got = lax.all_to_all(sent, "ctx", 0, 0, tiled=True)
        u1 = own_rows(u1_all)
        full_o = rows_over_ctx(o_wa)
        w_blocks = lax.all_gather(w_block, "ctx", axis=0, tiled=False)
        qb, kb, vb, lse, attn, ob, uo, x1, h2 = local_call(
            attend_kernel,
            [
                ((rows, width), BF16),
                ((n_ctx * rows, kvd), BF16),
                ((n_ctx * rows, kvd), BF16),
                ((kvh, group * rows, 1), F32),
                ((rows, width), F32),
                ((rows, width), BF16),
                ((rows, rank), BF16),
                ((rows, width), F32),
                ((rows, width), BF16),
            ],
            got,
            cosine,
            sine,
            key_cos,
            key_sin,
            query_pos,
            key_pos,
            x_bf,
            full_o,
            s_ao,
            s_lo,
            gain_two,
        )
        h2, *grads_all = lax.optimization_barrier((h2, *grads_all))

        first = wa * part_ff
        lift_part = lax.dynamic_slice_in_dim(lift_gu, first, part_ff, 3)
        down_part = lax.dynamic_slice_in_dim(a_down, first, part_ff, 2)
        lanes = -(-max(part_ff + j * part_ff % 128 for j in range(n_wa)) // 128) * 128
        ff_grads = jnp.zeros((3, slots * rank, lanes), F32)
        shift = (first % 128).astype(jnp.int32)[None]
        w_gu_t = w_gu.transpose(0, 2, 1)
        h2_all = wa_exchange(h2)
        out_sent, d_h2_sent = {}, {}
        groups = [[1, 2], [3, 0]]
        for at, group_wa in enumerate(groups):
            done = mlp_call(
                jnp.concatenate([index_all[k : k + 1] for k in group_wa]),
                shift,
                [h2_all[k] for k in group_wa],
                [grads_all[k] for k in group_wa],
                a_gu,
                lift_down,
                w_gu_t,
                w_down,
                lift_part,
                down_part,
                ff_grads,
                n_ctx if at == len(groups) - 1 else None,
            )
            for k, part, d_part in zip(group_wa, done[0], done[1]):
                out_sent[k], d_h2_sent[k] = part, d_part
            ff_grads = done[2]

        def wa_return(parts):
            return [parts[0]] + [swap(parts[k], "wa", n_wa, k) for k in range(1, n_wa)]

        d_h2_parts = wa_return(d_h2_sent)
        ff_got = lax.all_to_all(ff_grads, "ctx", 0, 0, tiled=True)
        ff_share = jnp.sum(ff_got.astype(F32), axis=0).astype(BF16)
        ff_share, *d_h2_parts = lax.optimization_barrier((ff_share, *d_h2_parts))
        ff_wa = jnp.stack(wa_exchange(ff_share))
        count = 8 * rank // n_ctx
        d_x1, dl_q, sent, ud = local_call(
            functools.partial(attend_back_kernel, n_wa=n_wa, n_ctx=n_ctx),
            [
                ((rows, width), F32),
                ((rows, width), BF16),
                ((n_ctx, rows + 3 * count, 2 * kvd), BF16),
                ((rows, rank), BF16),
            ],
            *d_h2_parts,
            s_agu,
            gain_two,
            x1,
            grad_out_bf,
            h2,
            full_o,
            s_lo,
            s_ao,
            attn,
            ob,
            uo,
            qb,
            kb,
            vb,
            lse,
            query_pos,
            key_pos,
            cosine,
            sine,
            key_cos,
            key_sin,
            u1,
            u1_all,
            scratch=[
                pltpu.VMEM((rows, width), BF16),
                pltpu.VMEM((group * rows, HD), F32),
                pltpu.VMEM((8 * rank, width), F32),
            ],
        )
        sent, ff_wa = lax.optimization_barrier((sent, ff_wa))
        got = lax.all_to_all(sent, "ctx", 0, 0, tiled=True)
        out_parts = wa_return(out_sent)
        ff_all = lax.all_gather(ff_wa, "ctx", axis=0, tiled=False)
        dl_kv, du1, share = local_call(
            collect_kernel,
            [
                ((rows, 2 * kvd), BF16),
                ((rows, 3 * rank), BF16),
                ((3 * count, 2 * kvd), BF16),
            ],
            got,
            dl_q,
            s_bq,
            s_bkv,
        )
        du1_sent = jnp.broadcast_to(du1[None], (n_ctx,) + du1.shape)
        du1_all = lax.all_to_all(du1_sent, "ctx", 0, 0, tiled=True).reshape(-1, 3 * rank)
        seq_all = lax.all_gather(jnp.stack(wa_exchange(share)), "ctx", axis=0, tiled=False)
        g_aqkv = dot_tn(du1_all, h1_all).astype(BF16)
        g_aqkv_all = wa_exchange(g_aqkv)
        out, grad_x = local_call(
            functools.partial(finish_kernel, n_wa=n_wa),
            [((rows, width), BF16), ((rows, width), F32)],
            *out_parts,
            x1,
            ud,
            s_ld,
            x_bf,
            gain_one,
            d_x1,
            dl_q,
            dl_kv,
            du1,
            w_blocks,
            s_aqkv,
        )
        own_wa = wa.astype(jnp.int32)[None]
        r_bgu, r_ad = ff_results(own_wa, ff_all, slots, rank, part_ff)
        shapes = [
            a_qkv.shape,
            a_gu.shape,
            lift_down.shape,
            a_o.shape,
            lift_o.shape,
            b_q.shape,
            b_kv.shape,
        ]
        layout, at = [], 0
        for i, tall in enumerate([2 * rank, rank, rank, rank, rank, rank]):
            layout.append((i + 1, at, tall))
            at += tall
        r_aqkv, r_agu, r_ld, r_ao, r_lo, r_bq, r_bkv = seq_results(
            own_wa, index_all, seq_all, g_aqkv_all, shapes, layout
        )
        return (
            out[None],
            grad_x[None],
            r_aqkv,
            r_bq,
            r_bkv,
            r_ao,
            r_lo,
            r_agu,
            r_bgu,
            r_ad,
            r_ld,
        )

    return per_device


def solution(mesh):
    rep = P()
    return jax.shard_map(
        make_per_device(mesh.shape["ctx"], mesh.shape["wa"]),
        mesh=mesh,
        in_specs=(
            P("wa", "ctx", None),
            P("wa", "ctx", None),
            P("wa"),
            rep,
            P("wa", None),
            rep,
            P("wa", None),
            P(None, None, "wa"),
            P("wa", None),
        )
        + (rep,) * 11,
        out_specs=(P("wa", "ctx", None), P("wa", "ctx", None)) + (rep,) * 9,
        check_vma=False,
    )
```

```python
import functools
import math

import jax
import jax.numpy as jnp
from jax import lax
from jax.experimental import pallas as pl
from jax.experimental.pallas import tpu as pltpu
from jax.sharding import PartitionSpec as P

HD = 128
EPS = 1e-06
ROPE_BASE = 1000000.0
ADAPTER_SCALE = 2.0
MASKED = -1e30
F32 = jnp.float32
BF16 = jnp.bfloat16


def dot_nn(a, b):
    return lax.dot_general(a, b, (((1,), (0,)), ((), ())), preferred_element_type=F32)


def dot_tn(a, b):
    return lax.dot_general(a, b, (((0,), (0,)), ((), ())), preferred_element_type=F32)


def dot_nt(a, b):
    return lax.dot_general(a, b, (((1,), (1,)), ((), ())), preferred_element_type=F32)


def inverse_norm(rows):
    return lax.rsqrt(jnp.mean(rows * rows, axis=-1, keepdims=True) + EPS)


def norm_pull(rows, inv, gain, grad):
    scaled = gain * grad
    return inv * scaled - rows * (inv * inv * inv) * jnp.mean(rows * scaled, axis=-1, keepdims=True)


def rope_tables(pos):
    half = HD // 2
    freq = ROPE_BASE ** (-jnp.arange(half, dtype=F32) * 2.0 / HD)
    angle = pos.astype(F32)[:, None] * freq[None, :]
    cosine, sine = jnp.cos(angle), jnp.sin(angle)
    return jnp.concatenate([cosine, cosine], axis=1), jnp.concatenate([-sine, sine], axis=1)


def row_positions(deal, rows, block):
    owner = rows // (2 * block)
    local = rows % (2 * block)
    table = jnp.arange(deal.shape[0], dtype=jnp.int32)
    pair = jnp.sum(jnp.where(owner[:, None] == table[None, :], deal[None, :], 0), axis=1)
    return jnp.where(
        local < block, pair * block + local, (2 * deal.shape[0] - 1 - pair) * block + local - block
    )


def ff_results_kernel(wa_ref, got_ref, bgu_ref, ad_ref, *, part_ff):
    n_ctx, n_wa, _, lanes = got_ref.shape
    own = wa_ref[0]
    rank = bgu_ref.shape[2]
    b_rows = bgu_ref.shape[0] * 2 * rank // n_ctx
    a_rows = ad_ref.shape[0] * rank // n_ctx
    starts = [j * part_ff // 128 * 128 for j in range(n_wa)]

    def write(read, store):
        left = None
        for j in range(n_wa):
            block = read(j).astype(F32)
            stop = starts[j + 1] - starts[j] if j + 1 < n_wa else lanes
            if left is not None:
                store(starts[j], block[:, :128] + left)
            first = 0 if left is None else 128
            store(starts[j] + first, block[:, first:stop])
            left = block[:, stop:] if stop < lanes else None

    for c in range(n_ctx):
        at = c * b_rows
        slot, half, low = at // (2 * rank), at // rank % 2, at % rank

        def put_b(lane, value):
            bgu_ref[slot, half, low : low + b_rows, lane : lane + value.shape[1]] = value

        write(lambda j: got_ref[c, own ^ j, :b_rows], put_b)
        at = c * a_rows
        slot, low = at // rank, at % rank

        def put_a(lane, value):
            ad_ref[slot, low : low + a_rows, lane : lane + value.shape[1]] = value

        write(lambda j: got_ref[c, own ^ j, b_rows:], put_a)


def ff_results(wa, got, slots, rank, part_ff):
    n_wa = got.shape[1]
    return pl.pallas_call(
        lambda *refs: ff_results_kernel(*refs, part_ff=part_ff),
        out_shape=(
            jax.ShapeDtypeStruct((slots, 2, rank, n_wa * part_ff), F32),
            jax.ShapeDtypeStruct((slots, rank, n_wa * part_ff), F32),
        ),
        in_specs=[pl.BlockSpec(memory_space=pltpu.SMEM), pl.BlockSpec(memory_space=pltpu.VMEM)],
        out_specs=(pl.BlockSpec(memory_space=pltpu.VMEM),) * 2,
        compiler_params=pltpu.CompilerParams(vmem_limit_bytes=48 << 20),
    )(wa, got)


def seq_results_kernel(own_ref, index_ref, got_ref, *out_refs, layout):
    _, n_chip, n_wa, share, third = got_ref.shape
    n_ctx = 2 * n_chip
    own, here = own_ref[0], own_ref[1]
    slots = out_refs[0].shape[0]
    for c in range(n_ctx):
        off = here ^ c
        terms = [got_ref[off & 1, off >> 1, own ^ j].astype(F32) for j in range(n_wa)]
        for slot in range(slots):
            total = jnp.zeros((share, third), F32)
            for j in range(n_wa):
                total = total + jnp.where(index_ref[own ^ j] == slot, terms[j], 0.0)
            for ref, (start, tall) in zip(out_refs, layout):
                for part in range(3 if len(ref.shape) == 3 else 1):
                    first = start + part * tall
                    low, high = max(first, c * share), min(first + tall, (c + 1) * share)
                    if low >= high:
                        continue
                    value = total[low - c * share : high - c * share]
                    at = slice(low - first, high - first)
                    if len(ref.shape) == 3:
                        ref[slot, at, part * third : (part + 1) * third] = value
                    else:
                        wide = ref.shape[3]
                        for i in range(ref.shape[1]):
                            ref[slot, i, at, :] = value[:, i * wide : (i + 1) * wide]


def seq_results(wa, index_all, got, shapes, layout):
    smem = pl.BlockSpec(memory_space=pltpu.SMEM)
    vmem = pl.BlockSpec(memory_space=pltpu.VMEM)
    return pl.pallas_call(
        lambda *refs: seq_results_kernel(*refs, layout=layout),
        out_shape=tuple(jax.ShapeDtypeStruct(shape, F32) for shape in shapes),
        in_specs=[smem, smem, vmem],
        out_specs=(vmem,) * len(shapes),
        compiler_params=pltpu.CompilerParams(vmem_limit_bytes=48 << 20),
    )(wa, index_all, got)


def local_call(kernel, out_shapes, *args, scratch=(), limit=56, cost=None, scalars=()):
    vmem = pl.BlockSpec(memory_space=pltpu.VMEM)
    smem = pl.BlockSpec(memory_space=pltpu.SMEM)
    return pl.pallas_call(
        kernel,
        out_shape=tuple(jax.ShapeDtypeStruct(shape, kind) for shape, kind in out_shapes),
        in_specs=[smem] * len(scalars) + [vmem] * len(args),
        out_specs=(vmem,) * len(out_shapes),
        scratch_shapes=list(scratch),
        compiler_params=pltpu.CompilerParams(vmem_limit_bytes=limit << 20),
        cost_estimate=cost and pl.CostEstimate(flops=cost, bytes_accessed=0, transcendentals=0),
    )(*scalars, *args)


def project_kernel(h1_ref, w_ref, a_ref, b_ref, bias_ref, sent_ref, u1_ref, *, q_cols):
    n_ctx, rows, wide = sent_ref.shape
    kv_cols = w_ref.shape[1] - q_cols
    h1 = h1_ref[...]
    u1 = dot_nt(h1, a_ref[...]).astype(BF16)
    u1_ref[...] = u1
    lin = dot_nn(h1, w_ref[...]) + bias_ref[...] + ADAPTER_SCALE * dot_nn(u1, b_ref[...])
    lin = lin.astype(BF16)
    pieces = [lin[c * rows : (c + 1) * rows, q_cols:] for c in range(n_ctx)]
    kv = jnp.concatenate(pieces, axis=1)
    fill = jnp.zeros((rows, wide - n_ctx * kv_cols - q_cols), BF16)
    for c in range(n_ctx):
        sent_ref[c, :, : n_ctx * kv_cols] = kv
        own = lin[c * rows : (c + 1) * rows, :q_cols]
        sent_ref[c, :, n_ctx * kv_cols :] = jnp.concatenate([own, fill], axis=1)


def turn(value, cosine, sine):
    return value * cosine + pltpu.roll(value, HD // 2, 1) * sine


def turn_back(value, cosine, sine):
    return value * cosine + pltpu.roll(value * sine, HD // 2, 1)


def heads_stacked(table, first, group):
    return jnp.concatenate(
        [table[:, (first + j) * HD : (first + j + 1) * HD] for j in range(group)], axis=0
    )


def attend_kernel(
    got_ref, cos_ref, sin_ref, kcos_ref, ksin_ref, qpos_ref, kpos_ref, qb_ref, kb_ref, vb_ref,
    lse_ref, attn_ref, ob_ref,
):
    n_ctx = got_ref.shape[0]
    rows, width = attn_ref.shape
    kvd = kb_ref.shape[1]
    kvh, heads = kvd // HD, width // HD
    group = heads // kvh
    q_cols, kv_cols = width // n_ctx, 2 * kvd // n_ctx
    scale = 1.0 / math.sqrt(HD)
    cosine, sine = cos_ref[...], sin_ref[...]
    q_lin = jnp.concatenate(
        [got_ref[c, :, 2 * kvd : 2 * kvd + q_cols] for c in range(n_ctx)], axis=1
    )
    for h in range(heads):
        lane = slice(h * HD, (h + 1) * HD)
        qb_ref[:, lane] = turn(q_lin[:, lane].astype(F32), cosine, sine).astype(BF16)
    for g in range(n_ctx):
        at = slice(g * rows, (g + 1) * rows)
        cut = slice(g * kv_cols, (g + 1) * kv_cols)
        kv_lin = jnp.concatenate([got_ref[c, :, cut] for c in range(n_ctx)], axis=1)
        kcos, ksin = kcos_ref[at, :], ksin_ref[at, :]
        for h in range(kvh):
            lane = slice(h * HD, (h + 1) * HD)
            kb_ref[at, lane] = turn(kv_lin[:, lane].astype(F32), kcos, ksin).astype(BF16)
        vb_ref[at, :] = kv_lin[:, kvd:]
    qpos = jnp.concatenate([qpos_ref[...]] * group, axis=0)
    seen = kpos_ref[...] <= qpos
    for g in range(kvh):
        q = heads_stacked(qb_ref, g * group, group)
        s = dot_nt(q, kb_ref[:, g * HD : (g + 1) * HD]) * scale
        s = jnp.where(seen, s, MASKED)
        top = jnp.max(s, axis=1, keepdims=True)
        e = jnp.exp(s - top)
        total = jnp.sum(e, axis=1, keepdims=True)
        lse_ref[g] = top + jnp.log(total)
        pb = (e * (1.0 / total)).astype(BF16)
        o = dot_nn(pb, vb_ref[:, g * HD : (g + 1) * HD])
        for j in range(group):
            lane = slice((g * group + j) * HD, (g * group + j + 1) * HD)
            attn_ref[:, lane] = o[j * rows : (j + 1) * rows]
    ob_ref[...] = attn_ref[...].astype(BF16)


def output_kernel(
    own_ref, ob_ref, x_ref, wo_ref, wo2_ref, ao_ref, lo_ref, gain_ref, uo_ref, x1_ref, h2_ref,
    projected,
):
    n_ctx = projected.shape[0]
    ob = ob_ref[...]
    uo = dot_nt(ob, ao_ref[...]).astype(BF16)
    uo_ref[...] = uo
    for r in range(n_ctx):
        block = (wo2_ref if r % 2 else wo_ref)[r // 2]
        projected[own_ref[0] ^ r] = dot_nt(ob, block)
    blocks = [projected[c] for c in range(n_ctx)]
    x1 = x_ref[...].astype(F32) + jnp.concatenate(blocks, axis=1)
    x1 = x1 + ADAPTER_SCALE * dot_nn(uo, lo_ref[...])
    x1_ref[...] = x1
    h2_ref[...] = (x1 * inverse_norm(x1) * gain_ref[...]).astype(BF16)


def flat_starts(rank):
    starts, at = {}, 0
    names = ("a_qkv", 3), ("a_gu", 2), ("lift_down", 1), ("a_o", 1), ("lift_o", 1), ("b_q", 1)
    for name, tall in names:
        starts[name] = at, tall * rank
        at += 3 * tall * rank
    starts["b_kv"] = at, rank
    return starts


def flat_height(rank):
    start, tall = flat_starts(rank)["b_kv"]
    return start + tall


def attend_back_kernel(own_ref, *refs, n_wa, n_ctx):
    parts, refs = refs[:n_wa], refs[n_wa:]
    (
        agu_ref, gain_ref, x1_ref, g_ref, h2_ref, wo_ref, wo2_ref, lo_ref, ao_ref, attn_ref, ob_ref, uo_ref,
        qb_ref, kb_ref, vb_ref, lse_ref, qpos_ref, kpos_ref, cos_ref, sin_ref, kcos_ref, ksin_ref,
        u1_ref, u1all_ref, h1_ref, h1all_ref, bq_ref, bkv_ref, dx1_ref, dlq_ref, sent_ref, ud_ref, dob, dq_acc, flat, bkv_acc, du_acc, go_cut,
    ) = refs
    rows, width = x1_ref.shape
    keys, kvd = kb_ref.shape
    kvh, heads = kvd // HD, width // HD
    group = heads // kvh
    rank = uo_ref.shape[1]
    scale = 1.0 / math.sqrt(HD)
    got = parts[0][...].astype(F32)
    for part in parts[1:]:
        got = got + part[...].astype(F32)
    small = got[:, width : width + 3 * rank].astype(BF16)
    dug, ud = small[:, : 2 * rank], small[:, 2 * rank :]
    ud_ref[...] = ud
    d_h2 = got[:, :width] + dot_nn(dug, agu_ref[...])
    x1 = x1_ref[...]
    g = g_ref[...]
    d_x1 = g.astype(F32) + norm_pull(x1, inverse_norm(x1), gain_ref[...], d_h2)
    dx1_ref[...] = d_x1
    go = d_x1.astype(BF16)
    duo = (ADAPTER_SCALE * dot_nt(go, lo_ref[...])).astype(BF16)
    third = width // 3
    starts = flat_starts(rank)

    def put(name, value, row=0):
        start, tall = starts[name]
        for i in range(3):
            at = start + i * tall + row
            flat[at : at + value.shape[0], :] = value[:, i * third : (i + 1) * third]

    put("a_gu", dot_tn(dug, h2_ref[...]))
    put("lift_down", ADAPTER_SCALE * dot_tn(ud, g))
    put("a_o", dot_tn(duo, ob_ref[...]))
    put("lift_o", ADAPTER_SCALE * dot_tn(uo_ref[...], go))
    d_attn = dot_nn(duo, ao_ref[...])
    cols = width // n_ctx
    for c in range(n_ctx):
        go_cut[c] = go[:, c * cols : (c + 1) * cols]
    for r in range(n_ctx):
        block = (wo2_ref if r % 2 else wo_ref)[r // 2]
        d_attn = d_attn + dot_nn(go_cut[own_ref[0] ^ r], block)
    dob[...] = d_attn.astype(BF16)
    qpos = jnp.concatenate([qpos_ref[...]] * group, axis=0)
    step = math.gcd(keys, 1024)
    share = step // rows
    bkv_acc[...] = jnp.zeros_like(bkv_acc)
    for kv in range(kvh):
        lane = slice(kv * HD, (kv + 1) * HD)
        v_lane = slice(kvd + kv * HD, kvd + (kv + 1) * HD)
        q = heads_stacked(qb_ref, kv * group, group)
        do = heads_stacked(dob, kv * group, group)
        o = heads_stacked(attn_ref, kv * group, group)
        delta = jnp.sum(do.astype(F32) * o, axis=1, keepdims=True)
        lse = lse_ref[kv]
        dq_acc[...] = jnp.zeros_like(dq_acc)

        def visit(turn_index):
            at = pl.ds(pl.multiple_of(turn_index * step, step), step)
            k = kb_ref[at, lane]
            s = dot_nt(q, k) * scale
            seen = kpos_ref[:, at] <= qpos
            p = jnp.exp(jnp.where(seen, s, MASKED) - lse)
            dp = dot_nt(do, vb_ref[at, lane])
            ds = (p * (dp - delta)).astype(BF16)
            dq_acc[...] += dot_nn(ds, k)
            dk = turn_back(dot_tn(ds, q) * scale, kcos_ref[at, :], ksin_ref[at, :]).astype(BF16)
            dv = dot_tn(p.astype(BF16), do).astype(BF16)
            u1 = u1all_ref[at, :]
            bkv_acc[:, lane] += dot_tn(u1[:, rank : 2 * rank], dk)
            bkv_acc[:, v_lane] += dot_tn(u1[:, 2 * rank :], dv)
            owners = pl.ds(turn_index * share, share)
            sent_ref[owners, :rows, lane] = dk.reshape(share, rows, HD)
            sent_ref[owners, :rows, v_lane] = dv.reshape(share, rows, HD)

        if keys == step:
            visit(0)
        else:
            pl.loop(0, keys // step)(visit)
        for j in range(group):
            head = slice((kv * group + j) * HD, (kv * group + j + 1) * HD)
            dq = dq_acc[j * rows : (j + 1) * rows] * scale
            dlq_ref[:, head] = turn_back(dq, cos_ref[...], sin_ref[...]).astype(BF16)
    d_lq = dlq_ref[...]
    put("b_q", ADAPTER_SCALE * dot_tn(u1_ref[:, :rank], d_lq))
    start, tall = starts["b_kv"]
    flat[start : start + tall, :] = bkv_acc[...] * ADAPTER_SCALE
    for c in range(n_ctx):
        at = slice(c * rows, (c + 1) * rows)
        low = [dot_nt(sent_ref[c, :rows, :kvd], bkv_ref[0]), dot_nt(sent_ref[c, :rows, kvd:], bkv_ref[1])]
        du_acc[at, :] = (ADAPTER_SCALE * jnp.concatenate(low, axis=1)).astype(BF16)
    duq = (ADAPTER_SCALE * dot_nt(d_lq, bq_ref[...])).astype(BF16)
    put("a_qkv", dot_tn(duq, h1_ref[...]))
    put("a_qkv", dot_tn(du_acc[...], h1all_ref[...]), rank)
    count = flat.shape[0] // n_ctx
    for c in range(n_ctx):
        share = flat[c * count : (c + 1) * count, :]
        sent_ref[c, rows:, :] = share.astype(BF16)


def collect_kernel(got_ref, dlq_ref, bq_ref, bkv_ref, dlkv_ref, du1_ref, share_ref):
    rows = dlq_ref.shape[0]
    rank = bq_ref.shape[0]
    kvd = bkv_ref.shape[2]
    total = got_ref[0].astype(F32)
    for c in range(1, got_ref.shape[0]):
        total = total + got_ref[c].astype(F32)
    dlkv = total[:rows].astype(BF16)
    dlkv_ref[...] = dlkv
    share_ref[...] = total[rows:].astype(BF16)
    du1 = [
        dot_nt(dlq_ref[...], bq_ref[...]),
        dot_nt(dlkv[:, :kvd], bkv_ref[0]),
        dot_nt(dlkv[:, kvd:], bkv_ref[1]),
    ]
    du1_ref[...] = (ADAPTER_SCALE * jnp.concatenate(du1, axis=1)).astype(BF16)


def finish_kernel(*refs, n_wa):
    parts, refs = refs[:n_wa], refs[n_wa:]
    (
        x1_ref, ud_ref, ld_ref, x_ref, gain_ref, dx1_ref, dlq_ref, dlkv_ref, du1_ref, w_ref, a_ref,
        out_ref, gx_ref,
    ) = refs
    n_ctx = w_ref.shape[0]
    q_cols, kv_cols = dlq_ref.shape[1] // n_ctx, dlkv_ref.shape[1] // n_ctx
    out = x1_ref[...] + ADAPTER_SCALE * dot_nn(ud_ref[...], ld_ref[...])
    for part in parts:
        out = out + part[...].astype(F32)
    out_ref[...] = out.astype(BF16)
    d_h1 = dot_nn(du1_ref[...], a_ref[...])
    for c in range(n_ctx):
        block = jnp.concatenate(
            [
                dlq_ref[:, c * q_cols : (c + 1) * q_cols],
                dlkv_ref[:, c * kv_cols : (c + 1) * kv_cols],
            ],
            axis=1,
        )
        d_h1 = d_h1 + dot_nt(block, w_ref[c])
    x = x_ref[...].astype(F32)
    gx_ref[...] = dx1_ref[...] + norm_pull(x, inverse_norm(x), gain_ref[...], d_h1)


def mlp_kernel(*refs, chunks, part_ff, tile, last):
    refs = list(refs)
    index_ref, shift_ref = refs[:2]
    h2_refs, g_refs = refs[2 : 2 + chunks], refs[2 + chunks : 2 + 2 * chunks]
    refs = refs[2 + 2 * chunks :]
    agu_ref, ld_ref, gu_ref, down_ref, lift_ref, ad_ref, prior_ref = refs[:7]
    refs = refs[7:]
    out_refs, dh_refs = refs[:chunks], refs[chunks : 2 * chunks]
    grads_ref = refs[2 * chunks]
    h2, gd, low, low_t, out_acc, dh_acc, small_acc, grads = refs[2 * chunks + 1 :]
    rows, width = h2_refs[0].shape
    slots, _, rank, _ = lift_ref.shape
    span = slots * rank
    step, steps = pl.program_id(0), pl.num_programs(0)

    def row_slot(lanes):
        return jnp.concatenate(
            [jnp.full((rows, lanes), index_ref[k], jnp.int32) for k in range(chunks)], axis=0
        )

    @pl.when(step == 0)
    def _():
        for k in range(chunks):
            h2[k * rows : (k + 1) * rows, :] = h2_refs[k][...]
            gd[k * rows : (k + 1) * rows, :] = g_refs[k][...]
        out_acc[...] = jnp.zeros_like(out_acc)
        dh_acc[...] = jnp.zeros_like(dh_acc)
        small_acc[...] = jnp.zeros_like(small_acc)
        grads[...] = prior_ref[...]
        lane = lax.broadcasted_iota(jnp.int32, (chunks * rows, span), 1)
        own = lane // rank == row_slot(span)
        flat_a = agu_ref[...]
        parts = [
            dot_nt(h2[...], flat_a[:, :rank].reshape(span, width)).astype(BF16),
            dot_nt(h2[...], flat_a[:, rank:].reshape(span, width)).astype(BF16),
            dot_nt(gd[...], ld_ref[...].reshape(span, width)).astype(BF16),
        ]
        for i, part in enumerate(parts):
            value = jnp.where(own, part.astype(F32) * ADAPTER_SCALE, 0.0)
            low[i] = value.astype(BF16)
            low_t[i] = value.T.astype(BF16)

    def work(first, wide):
        lanes = pl.ds(first, wide)
        w_g, w_u = gu_ref[0, :wide, :], gu_ref[1, :wide, :]
        w_d = down_ref[:wide, :]
        l_g = lift_ref[:, 0, :, :wide].reshape(span, wide)
        l_u = lift_ref[:, 1, :, :wide].reshape(span, wide)
        a_d = ad_ref[:, :, :wide].reshape(span, wide)
        gate = dot_nt(h2[...], w_g) + dot_nn(low[0], l_g)
        up = dot_nt(h2[...], w_u) + dot_nn(low[1], l_u)
        sigma = 1.0 / (1.0 + jnp.exp(-gate))
        swish = gate * sigma
        hidden = (swish * up).astype(BF16)
        d_hidden = dot_nt(gd[...], w_d) + dot_nn(low[2], a_d)
        d_gate = (d_hidden * up * (sigma + swish * (1.0 - sigma))).astype(BF16)
        d_up = (d_hidden * swish).astype(BF16)
        out_acc[...] += dot_nn(hidden, w_d)
        dh_acc[...] += dot_nn(d_gate, w_g) + dot_nn(d_up, w_u)
        small_acc[0] += dot_nt(d_gate, l_g)
        small_acc[1] += dot_nt(d_up, l_u)
        small_acc[2] += dot_nt(hidden, a_d)
        grads[0, :, lanes] += dot_nn(low_t[0], d_gate)
        grads[1, :, lanes] += dot_nn(low_t[1], d_up)
        grads[2, :, lanes] += dot_nn(low_t[2], hidden)

    rest = part_ff % tile
    if rest:
        pl.when(step < steps - 1)(lambda: work(pl.multiple_of(step * tile, tile), tile))
        pl.when(step == steps - 1)(lambda: work(part_ff - rest, rest))
    else:
        work(pl.multiple_of(step * tile, tile), tile)

    @pl.when(step == steps - 1)
    def _():
        for k in range(chunks):
            at = slice(k * rows, (k + 1) * rows)
            out_refs[k][...] = out_acc[at, :].astype(BF16)
            dh_refs[k][:, :width] = dh_acc[at, :].astype(BF16)
            picked = []
            for i in range(3):
                value = jnp.zeros((rows, rank), F32)
                for slot in range(slots):
                    mine = small_acc[i, at, slot * rank : (slot + 1) * rank]
                    value = value + jnp.where(index_ref[k] == slot, mine, 0.0)
                picked.append(value * (ADAPTER_SCALE if i < 2 else 1.0))
            picked.append(jnp.zeros((rows, 128 - 3 * rank), F32))
            dh_refs[k][:, width:] = jnp.concatenate(picked, axis=1).astype(BF16)
        if not last:
            grads_ref[...] = grads[...]
        else:
            n_ctx = grads_ref.shape[0]
            b_rows, a_rows = 2 * span // n_ctx, span // n_ctx
            odd = shift_ref[0] != 0
            tables = []
            for i in range(3):
                value = grads[i]
                if rest % 128:
                    value = jnp.where(odd, pltpu.roll(value, part_ff % 128, 1), value)
                tables.append(value.astype(BF16))
            for c in range(n_ctx):
                at = c * b_rows
                slot, half, at = at // (2 * rank), at // rank % 2, at % rank
                at += slot * rank
                grads_ref[c, :b_rows, :] = tables[half][at : at + b_rows]
                grads_ref[c, b_rows:, :] = tables[2][c * a_rows : (c + 1) * a_rows]


def mlp_call(index, shift, h2s, gs, a_gu, lift_down, w_gu, w_down, lift, a_down, prior, n_ctx):
    chunks = len(h2s)
    rows, width = h2s[0].shape
    part_ff = w_down.shape[0]
    slots, _, rank, _ = lift.shape
    span = slots * rank
    tile = 512
    steps = -(-part_ff // tile)
    lanes = prior.shape[2]
    smem = pl.BlockSpec(memory_space=pltpu.SMEM)

    def whole(shape):
        return pl.BlockSpec(shape, lambda i: (0,) * len(shape))

    if n_ctx is None:
        grads_shape = jax.ShapeDtypeStruct((3, span, lanes), F32)
    else:
        grads_shape = jax.ShapeDtypeStruct((n_ctx, 3 * span // n_ctx, lanes), BF16)
    total = chunks * rows
    outs = pl.pallas_call(
        lambda *refs: mlp_kernel(
            *refs, chunks=chunks, part_ff=part_ff, tile=tile, last=n_ctx is not None
        ),
        grid=(steps,),
        out_shape=(jax.ShapeDtypeStruct((rows, width), BF16),) * chunks
        + (jax.ShapeDtypeStruct((rows, width + 128), BF16),) * chunks
        + (grads_shape,),
        in_specs=[smem, smem]
        + [whole((rows, width))] * (2 * chunks)
        + [
            whole(a_gu.shape),
            whole(lift_down.shape),
            pl.BlockSpec((2, tile, width), lambda i: (0, i, 0)),
            pl.BlockSpec((tile, width), lambda i: (i, 0)),
            pl.BlockSpec((slots, 2, rank, tile), lambda i: (0, 0, 0, i)),
            pl.BlockSpec((slots, rank, tile), lambda i: (0, 0, i)),
            whole(prior.shape),
        ],
        out_specs=(whole((rows, width)),) * chunks
        + (whole((rows, width + 128)),) * chunks
        + (whole(grads_shape.shape),),
        scratch_shapes=[
            pltpu.VMEM((total, width), BF16),
            pltpu.VMEM((total, width), BF16),
            pltpu.VMEM((3, total, span), BF16),
            pltpu.VMEM((3, span, total), BF16),
            pltpu.VMEM((total, width), F32),
            pltpu.VMEM((total, width), F32),
            pltpu.VMEM((3, total, span), F32),
            pltpu.VMEM((3, span, lanes), F32),
        ],
        compiler_params=pltpu.CompilerParams(vmem_limit_bytes=50 << 20),
        cost_estimate=pl.CostEstimate(
            flops=12 * total * width * part_ff,
            bytes_accessed=6 * width * part_ff,
            transcendentals=0,
        ),
    )(index, shift, *h2s, *gs, a_gu, lift_down, w_gu, w_down, lift, a_down, prior)
    return outs[:chunks], outs[chunks : 2 * chunks], outs[-1]


def swap(value, axis, count, k):
    return lax.ppermute(value, axis, [(i, i ^ k) for i in range(count)])


def make_per_device(n_ctx, n_wa):
    def wa_exchange(value):
        return [value] + [swap(value, "wa", n_wa, k) for k in range(1, n_wa)]

    def absolute(parts, axis):
        own = lax.axis_index(axis)
        parts = list(parts)
        bit = 1
        while bit < len(parts):
            other = own & bit != 0
            parts = [jnp.where(other, parts[i ^ bit], parts[i]) for i in range(len(parts))]
            bit *= 2
        return parts

    def gather_near(value):
        return [value] + [swap(value, "ctx", n_ctx, 2 * r) for r in range(1, n_ctx // 2)]

    def gather_cores(same):
        same = jnp.stack(same)
        return same, swap(same, "ctx", n_ctx, 1)

    def per_device(
        tokens,
        cotangent,
        adapter_index,
        deal,
        w_qkv,
        b_qkv,
        w_o,
        w_gu,
        w_down,
        gain_attn,
        gain_mlp,
        a_qkv,
        b_q,
        b_kv,
        a_o,
        lift_o,
        a_gu,
        lift_gu,
        a_down,
        lift_down,
    ):
        rows, width = tokens.shape[1:]
        block = rows // 2
        rank = b_q.shape[1]
        slots = a_qkv.shape[0]
        kvd = b_kv.shape[3]
        heads = width // HD
        kvh = kvd // HD
        group = heads // kvh
        part_ff = w_down.shape[0]
        wa = lax.axis_index("wa")
        ctx = lax.axis_index("ctx")
        chosen = adapter_index[0]

        def picked(table):
            return lax.dynamic_index_in_dim(table, chosen, 0, keepdims=False)

        grad_out_bf = cotangent[0]
        x_bf = tokens[0]
        q_cols, kv_cols = width // n_ctx, 2 * kvd // n_ctx
        gain_one = gain_attn.astype(F32)[None]
        gain_two = gain_mlp.astype(F32)[None]
        s_aqkv, s_bq, s_bkv = picked(a_qkv), picked(b_q), picked(b_kv)
        s_ao, s_lo, s_agu, s_ld = picked(a_o), picked(lift_o), picked(a_gu), picked(lift_down)

        x = x_bf.astype(F32)
        h1 = (x * inverse_norm(x) * gain_one).astype(BF16)
        h1_all = lax.all_gather(h1, "ctx", axis=0, tiled=True)

        def block_of(table):
            return jnp.concatenate(
                [
                    lax.dynamic_slice_in_dim(table[:, :width], ctx * q_cols, q_cols, 1),
                    lax.dynamic_slice_in_dim(table[:, width:], ctx * kv_cols, kv_cols, 1),
                ],
                axis=1,
            )

        o_mine = lax.dynamic_slice_in_dim(w_o, ctx * q_cols, q_cols, 1).T
        mark = jnp.full((16, q_cols + kv_cols), chosen, jnp.int32).astype(BF16)
        w_mine = jnp.concatenate([block_of(w_qkv), mark], axis=0)
        depth = w_qkv.shape[0]
        o_parts = wa_exchange(o_mine)
        o_parts, w_mine = lax.optimization_barrier((o_parts, w_mine))
        w_parts = wa_exchange(w_mine)
        o_block = jnp.concatenate(absolute(o_parts, "wa"), axis=1)
        o_near = gather_near(o_block)
        b_all = jnp.concatenate(
            [
                jnp.pad(s_bq, ((0, 0), (0, 2 * kvd))),
                jnp.pad(s_bkv[0], ((0, 0), (width, kvd))),
                jnp.pad(s_bkv[1], ((0, 0), (width + kvd, 0))),
            ],
            axis=0,
        )
        key_pos = row_positions(deal, jnp.arange(n_ctx * rows, dtype=jnp.int32), block)
        key_cos, key_sin = rope_tables(key_pos)

        def own_rows(table):
            return lax.dynamic_slice_in_dim(table, ctx * rows, rows, 0)

        query_pos, cosine, sine = own_rows(key_pos)[:, None], own_rows(key_cos), own_rows(key_sin)
        key_pos = key_pos[None]
        lift_part = lax.dynamic_slice_in_dim(lift_gu, wa * part_ff, part_ff, 3)
        down_part = lax.dynamic_slice_in_dim(a_down, wa * part_ff, part_ff, 2)
        tables = (key_cos, key_sin, cosine, sine, query_pos, key_pos)
        picks = (s_aqkv, s_bq, s_bkv, s_ao, s_lo, s_agu, s_ld, lift_part, down_part)
        sides = (block_of(b_all), block_of(b_qkv[None]).astype(F32))
        w_parts, grad_sent = lax.optimization_barrier((tuple(w_parts), grad_out_bf))
        held = (h1_all, w_parts, o_near, tables, picks, sides)
        held = lax.optimization_barrier(held)
        h1_all, w_parts, o_near, tables, picks, sides = held
        key_cos, key_sin, cosine, sine, query_pos, key_pos = tables
        s_aqkv, s_bq, s_bkv, s_ao, s_lo, s_agu, s_ld, lift_part, down_part = picks
        w_block = jnp.concatenate(absolute([part[:depth] for part in w_parts], "wa"), axis=0)
        index_all = jnp.stack([part[depth, 0] for part in w_parts]).astype(jnp.int32)
        sent, u1_all = local_call(
            functools.partial(project_kernel, q_cols=q_cols),
            [
                ((n_ctx, rows, -(-(2 * kvd + q_cols) // 128) * 128), BF16),
                ((n_ctx * rows, 3 * rank), BF16),
            ],
            h1_all,
            w_block,
            s_aqkv,
            *sides,
        )
        grads_all = wa_exchange(grad_sent)
        got = lax.all_to_all(sent, "ctx", 0, 0, tiled=True)
        o_near = gather_cores(o_near)
        held = (got, o_near, index_all)
        got, o_near, index_all = lax.optimization_barrier(held)
        u1 = own_rows(u1_all)
        own_ctx = ctx.astype(jnp.int32)[None]
        qb, kb, vb, lse, attn, ob = local_call(
            attend_kernel,
            [
                ((rows, width), BF16),
                ((n_ctx * rows, kvd), BF16),
                ((n_ctx * rows, kvd), BF16),
                ((kvh, group * rows, 1), F32),
                ((rows, width), F32),
                ((rows, width), BF16),
            ],
            got,
            cosine,
            sine,
            key_cos,
            key_sin,
            query_pos,
            key_pos,
            cost=9 * 10**9,
        )
        ob, grads_all = lax.optimization_barrier((ob, grads_all))
        uo, x1, h2 = local_call(
            output_kernel,
            [((rows, rank), BF16), ((rows, width), F32), ((rows, width), BF16)],
            ob,
            x_bf,
            *o_near,
            s_ao,
            s_lo,
            gain_two,
            scalars=(own_ctx,),
            scratch=[pltpu.VMEM((n_ctx, rows, q_cols), F32)],
        )

        h2, w_block = lax.optimization_barrier((h2, w_block))
        w_blocks = lax.all_gather(w_block, "ctx", axis=0, tiled=False)

        first = wa * part_ff
        lanes = -(-max(part_ff + j * part_ff % 128 for j in range(n_wa)) // 128) * 128
        ff_grads = jnp.zeros((3, slots * rank, lanes), F32)
        shift = (first % 128).astype(jnp.int32)[None]
        w_gu_t = w_gu.transpose(0, 2, 1)
        h2_all = [h2] + [swap(h2, "wa", n_wa, k) for k in range(1, n_wa - 1)]
        h2_last, h2_all, grads_all = lax.optimization_barrier((h2, h2_all, grads_all))
        h2_all.append(swap(h2_last, "wa", n_wa, n_wa - 1))
        out_sent, d_h2_sent = {}, {}
        groups = [[0], [1, 2], [3]] if n_wa == 4 else [[k] for k in range(n_wa)]
        for at, group_wa in enumerate(groups):
            done = mlp_call(
                jnp.concatenate([index_all[k : k + 1] for k in group_wa]),
                shift,
                [h2 if k == 0 else h2_all[k] for k in group_wa],
                [grad_out_bf if k == 0 else grads_all[k] for k in group_wa],
                a_gu,
                lift_down,
                w_gu_t,
                w_down,
                lift_part,
                down_part,
                ff_grads,
                n_ctx if at == len(groups) - 1 else None,
            )
            for k, part, d_part in zip(group_wa, done[0], done[1]):
                out_sent[k], d_h2_sent[k] = part, d_part
            ff_grads = done[2]

        def wa_return(parts):
            return [parts[0]] + [swap(parts[k], "wa", n_wa, k) for k in range(1, n_wa)]

        d_h2_parts = wa_return(d_h2_sent)
        held = (ff_grads, tuple(out_sent[k] for k in range(n_wa)), tuple(d_h2_parts), w_blocks)
        ff_grads, out_sent, d_h2_parts, w_blocks = lax.optimization_barrier(held)
        ff_got = lax.all_to_all(ff_grads, "ctx", 0, 0, tiled=True)
        ff_share = jnp.sum(ff_got.astype(F32), axis=0).astype(BF16)
        count = flat_height(rank) // n_ctx
        d_x1, dl_q, sent, ud = local_call(
            functools.partial(attend_back_kernel, n_wa=n_wa, n_ctx=n_ctx),
            [
                ((rows, width), F32),
                ((rows, width), BF16),
                ((n_ctx, rows + count, 2 * kvd), BF16),
                ((rows, rank), BF16),
            ],
            *d_h2_parts,
            s_agu,
            gain_two,
            x1,
            grad_out_bf,
            h2,
            *o_near,
            s_lo,
            s_ao,
            attn,
            ob,
            uo,
            qb,
            kb,
            vb,
            lse,
            query_pos,
            key_pos,
            cosine,
            sine,
            key_cos,
            key_sin,
            u1,
            u1_all,
            h1,
            h1_all,
            s_bq,
            s_bkv,
            scalars=(own_ctx,),
            scratch=[
                pltpu.VMEM((rows, width), BF16),
                pltpu.VMEM((group * rows, HD), F32),
                pltpu.VMEM((count * n_ctx, width // 3), F32),
                pltpu.VMEM((rank, 2 * kvd), F32),
                pltpu.VMEM((n_ctx * rows, 2 * rank), BF16),
                pltpu.VMEM((n_ctx, rows, q_cols), BF16),
            ],
        )
        got = lax.all_to_all(sent, "ctx", 0, 0, tiled=True)
        ff_wa = jnp.stack(wa_exchange(ff_share))
        out_parts = [
            lax.psum_scatter(
                jnp.concatenate(absolute(out_sent, "wa"), axis=0),
                "wa",
                scatter_dimension=0,
                tiled=True,
            )
        ]
        got, ff_wa, out_parts = lax.optimization_barrier((got, ff_wa, out_parts))
        ff_all = lax.all_gather(ff_wa, "ctx", axis=0, tiled=False)
        dl_kv, du1, share = local_call(
            collect_kernel,
            [
                ((rows, 2 * kvd), BF16),
                ((rows, 3 * rank), BF16),
                ((count, 2 * kvd), BF16),
            ],
            got,
            dl_q,
            s_bq,
            s_bkv,
        )
        share_wa = jnp.stack(wa_exchange(share))
        seq_all = jnp.stack(gather_cores(gather_near(share_wa)))
        out, grad_x = local_call(
            functools.partial(finish_kernel, n_wa=len(out_parts)),
            [((rows, width), BF16), ((rows, width), F32)],
            *out_parts,
            x1,
            ud,
            s_ld,
            x_bf,
            gain_one,
            d_x1,
            dl_q,
            dl_kv,
            du1,
            w_blocks,
            s_aqkv,
            cost=7 * 10**9,
        )
        own_wa = wa.astype(jnp.int32)[None]
        r_bgu, r_ad = ff_results(own_wa, ff_all, slots, rank, part_ff)
        tables = {
            "a_qkv": a_qkv,
            "b_q": b_q,
            "b_kv": b_kv,
            "a_o": a_o,
            "lift_o": lift_o,
            "a_gu": a_gu,
            "lift_down": lift_down,
        }
        layout = tuple(flat_starts(rank)[name] for name in tables)
        r_aqkv, r_bq, r_bkv, r_ao, r_lo, r_agu, r_ld = seq_results(
            jnp.concatenate([own_wa, own_ctx]), index_all, seq_all, [table.shape for table in tables.values()], layout
        )
        return (
            out[None],
            grad_x[None],
            r_aqkv,
            r_bq,
            r_bkv,
            r_ao,
            r_lo,
            r_agu,
            r_bgu,
            r_ad,
            r_ld,
        )

    return per_device


def solution(mesh):
    rep = P()
    return jax.shard_map(
        make_per_device(mesh.shape["ctx"], mesh.shape["wa"]),
        mesh=mesh,
        in_specs=(
            P("wa", "ctx", None),
            P("wa", "ctx", None),
            P("wa"),
            rep,
            P("wa", None),
            rep,
            P("wa", None),
            P(None, None, "wa"),
            P("wa", None),
        )
        + (rep,) * 11,
        out_specs=(P("wa", "ctx", None), P("wa", "ctx", None)) + (rep,) * 9,
        check_vma=False,
    )
```

```python
import functools
import math

import jax
import jax.numpy as jnp
from jax import lax
from jax.experimental import pallas as pl
from jax.experimental.pallas import tpu as pltpu
from jax.sharding import PartitionSpec as P

HD = 128
EPS = 1e-06
ROPE_BASE = 1000000.0
ADAPTER_SCALE = 2.0
MASKED = -1e30
F32 = jnp.float32
BF16 = jnp.bfloat16


def dot_nn(a, b):
    return lax.dot_general(a, b, (((1,), (0,)), ((), ())), preferred_element_type=F32)


def dot_tn(a, b):
    return lax.dot_general(a, b, (((0,), (0,)), ((), ())), preferred_element_type=F32)


def dot_nt(a, b):
    return lax.dot_general(a, b, (((1,), (1,)), ((), ())), preferred_element_type=F32)


def inverse_norm(rows):
    return lax.rsqrt(jnp.mean(rows * rows, axis=-1, keepdims=True) + EPS)


def norm_pull(rows, inv, gain, grad):
    scaled = gain * grad
    return inv * scaled - rows * (inv * inv * inv) * jnp.mean(rows * scaled, axis=-1, keepdims=True)


def rope_tables(pos):
    half = HD // 2
    freq = ROPE_BASE ** (-jnp.arange(half, dtype=F32) * 2.0 / HD)
    angle = pos.astype(F32)[:, None] * freq[None, :]
    cosine, sine = jnp.cos(angle), jnp.sin(angle)
    return jnp.concatenate([cosine, cosine], axis=1), jnp.concatenate([-sine, sine], axis=1)


def row_positions(deal, rows, block):
    owner = rows // (2 * block)
    local = rows % (2 * block)
    table = jnp.arange(deal.shape[0], dtype=jnp.int32)
    pair = jnp.sum(jnp.where(owner[:, None] == table[None, :], deal[None, :], 0), axis=1)
    return jnp.where(
        local < block, pair * block + local, (2 * deal.shape[0] - 1 - pair) * block + local - block
    )


def ff_results_kernel(wa_ref, got_ref, bgu_ref, ad_ref, *, part_ff):
    n_ctx, n_wa, _, lanes = got_ref.shape
    own = wa_ref[0]
    rank = bgu_ref.shape[2]
    b_rows = bgu_ref.shape[0] * 2 * rank // n_ctx
    a_rows = ad_ref.shape[0] * rank // n_ctx
    starts = [j * part_ff // 128 * 128 for j in range(n_wa)]

    def write(read, store):
        left = None
        for j in range(n_wa):
            block = read(j).astype(F32)
            stop = starts[j + 1] - starts[j] if j + 1 < n_wa else lanes
            if left is not None:
                store(starts[j], block[:, :128] + left)
            first = 0 if left is None else 128
            store(starts[j] + first, block[:, first:stop])
            left = block[:, stop:] if stop < lanes else None

    for c in range(n_ctx):
        at = c * b_rows
        slot, half, low = at // (2 * rank), at // rank % 2, at % rank

        def put_b(lane, value):
            bgu_ref[slot, half, low : low + b_rows, lane : lane + value.shape[1]] = value

        write(lambda j: got_ref[c, own ^ j, :b_rows], put_b)
        at = c * a_rows
        slot, low = at // rank, at % rank

        def put_a(lane, value):
            ad_ref[slot, low : low + a_rows, lane : lane + value.shape[1]] = value

        write(lambda j: got_ref[c, own ^ j, b_rows:], put_a)


def ff_results(wa, got, slots, rank, part_ff):
    n_wa = got.shape[1]
    return pl.pallas_call(
        lambda *refs: ff_results_kernel(*refs, part_ff=part_ff),
        out_shape=(
            jax.ShapeDtypeStruct((slots, 2, rank, n_wa * part_ff), F32),
            jax.ShapeDtypeStruct((slots, rank, n_wa * part_ff), F32),
        ),
        in_specs=[pl.BlockSpec(memory_space=pltpu.SMEM), pl.BlockSpec(memory_space=pltpu.VMEM)],
        out_specs=(pl.BlockSpec(memory_space=pltpu.VMEM),) * 2,
        compiler_params=pltpu.CompilerParams(vmem_limit_bytes=48 << 20),
    )(wa, got)


def seq_results_kernel(own_ref, index_ref, got_ref, *out_refs, layout):
    _, n_chip, n_wa, share, third = got_ref.shape
    n_ctx = 2 * n_chip
    own, here = own_ref[0], own_ref[1]
    slots = out_refs[0].shape[0]
    for c in range(n_ctx):
        off = here ^ c
        terms = [got_ref[off & 1, off >> 1, own ^ j].astype(F32) for j in range(n_wa)]
        for slot in range(slots):
            total = jnp.zeros((share, third), F32)
            for j in range(n_wa):
                total = total + jnp.where(index_ref[own ^ j] == slot, terms[j], 0.0)
            for ref, (start, tall) in zip(out_refs, layout):
                for part in range(3 if len(ref.shape) == 3 else 1):
                    first = start + part * tall
                    low, high = max(first, c * share), min(first + tall, (c + 1) * share)
                    if low >= high:
                        continue
                    value = total[low - c * share : high - c * share]
                    at = slice(low - first, high - first)
                    if len(ref.shape) == 3:
                        ref[slot, at, part * third : (part + 1) * third] = value
                    else:
                        wide = ref.shape[3]
                        for i in range(ref.shape[1]):
                            ref[slot, i, at, :] = value[:, i * wide : (i + 1) * wide]


def seq_results(wa, index_all, got, shapes, layout):
    smem = pl.BlockSpec(memory_space=pltpu.SMEM)
    vmem = pl.BlockSpec(memory_space=pltpu.VMEM)
    return pl.pallas_call(
        lambda *refs: seq_results_kernel(*refs, layout=layout),
        out_shape=tuple(jax.ShapeDtypeStruct(shape, F32) for shape in shapes),
        in_specs=[smem, smem, vmem],
        out_specs=(vmem,) * len(shapes),
        compiler_params=pltpu.CompilerParams(vmem_limit_bytes=48 << 20),
    )(wa, index_all, got)


def local_call(kernel, out_shapes, *args, scratch=(), tight=False, cost=None, scalars=()):
    vmem = pl.BlockSpec(memory_space=pltpu.VMEM)
    smem = pl.BlockSpec(memory_space=pltpu.SMEM)
    limit = 56 << 20
    if tight:
        held = sum(arg.size * arg.dtype.itemsize for arg in args)
        held += sum(math.prod(shape) * jnp.dtype(kind).itemsize for shape, kind in out_shapes)
        limit = min(held + (20 << 20), limit)
    return pl.pallas_call(
        kernel,
        out_shape=tuple(jax.ShapeDtypeStruct(shape, kind) for shape, kind in out_shapes),
        in_specs=[smem] * len(scalars) + [vmem] * len(args),
        out_specs=(vmem,) * len(out_shapes),
        scratch_shapes=list(scratch),
        compiler_params=pltpu.CompilerParams(vmem_limit_bytes=limit),
        cost_estimate=cost and pl.CostEstimate(flops=cost, bytes_accessed=0, transcendentals=0),
    )(*scalars, *args)


def project_kernel(h1_ref, w_ref, a_ref, b_ref, bias_ref, sent_ref, u1_ref, *, q_cols):
    n_ctx, rows, wide = sent_ref.shape
    kv_cols = w_ref.shape[1] - q_cols
    h1 = h1_ref[...]
    u1 = dot_nt(h1, a_ref[...]).astype(BF16)
    u1_ref[...] = u1
    lin = dot_nn(h1, w_ref[...]) + bias_ref[...] + ADAPTER_SCALE * dot_nn(u1, b_ref[...])
    lin = lin.astype(BF16)
    pieces = [lin[c * rows : (c + 1) * rows, q_cols:] for c in range(n_ctx)]
    kv = jnp.concatenate(pieces, axis=1)
    fill = jnp.zeros((rows, wide - n_ctx * kv_cols - q_cols), BF16)
    for c in range(n_ctx):
        sent_ref[c, :, : n_ctx * kv_cols] = kv
        own = lin[c * rows : (c + 1) * rows, :q_cols]
        sent_ref[c, :, n_ctx * kv_cols :] = jnp.concatenate([own, fill], axis=1)


def turn(value, cosine, sine):
    return value * cosine + pltpu.roll(value, HD // 2, 1) * sine


def turn_back(value, cosine, sine):
    return value * cosine + pltpu.roll(value * sine, HD // 2, 1)


def heads_stacked(table, first, group):
    return jnp.concatenate(
        [table[:, (first + j) * HD : (first + j + 1) * HD] for j in range(group)], axis=0
    )


def attend_kernel(
    got_ref, cos_ref, sin_ref, kcos_ref, ksin_ref, qpos_ref, kpos_ref, qb_ref, kb_ref, vb_ref,
    lse_ref, attn_ref, ob_ref,
):
    n_ctx = got_ref.shape[0]
    rows, width = attn_ref.shape
    kvd = kb_ref.shape[1]
    kvh, heads = kvd // HD, width // HD
    group = heads // kvh
    q_cols, kv_cols = width // n_ctx, 2 * kvd // n_ctx
    scale = 1.0 / math.sqrt(HD)
    cosine, sine = cos_ref[...], sin_ref[...]
    q_lin = jnp.concatenate(
        [got_ref[c, :, 2 * kvd : 2 * kvd + q_cols] for c in range(n_ctx)], axis=1
    )
    for h in range(heads):
        lane = slice(h * HD, (h + 1) * HD)
        qb_ref[:, lane] = turn(q_lin[:, lane].astype(F32), cosine, sine).astype(BF16)
    for g in range(n_ctx):
        at = slice(g * rows, (g + 1) * rows)
        cut = slice(g * kv_cols, (g + 1) * kv_cols)
        kv_lin = jnp.concatenate([got_ref[c, :, cut] for c in range(n_ctx)], axis=1)
        kcos, ksin = kcos_ref[at, :], ksin_ref[at, :]
        for h in range(kvh):
            lane = slice(h * HD, (h + 1) * HD)
            kb_ref[at, lane] = turn(kv_lin[:, lane].astype(F32), kcos, ksin).astype(BF16)
        vb_ref[at, :] = kv_lin[:, kvd:]
    qpos = jnp.concatenate([qpos_ref[...]] * group, axis=0)
    seen = kpos_ref[...] <= qpos
    for g in range(kvh):
        q = heads_stacked(qb_ref, g * group, group)
        s = dot_nt(q, kb_ref[:, g * HD : (g + 1) * HD]) * scale
        s = jnp.where(seen, s, MASKED)
        top = jnp.max(s, axis=1, keepdims=True)
        e = jnp.exp(s - top)
        total = jnp.sum(e, axis=1, keepdims=True)
        lse_ref[g] = top + jnp.log(total)
        pb = (e * (1.0 / total)).astype(BF16)
        o = dot_nn(pb, vb_ref[:, g * HD : (g + 1) * HD])
        for j in range(group):
            lane = slice((g * group + j) * HD, (g * group + j + 1) * HD)
            attn_ref[:, lane] = o[j * rows : (j + 1) * rows]
    ob_ref[...] = attn_ref[...].astype(BF16)


def output_kernel(
    own_ref, ob_ref, x_ref, wo_ref, wo2_ref, ao_ref, lo_ref, gain_ref, uo_ref, x1_ref, h2_ref,
    projected,
):
    n_ctx = projected.shape[0]
    ob = ob_ref[...]
    uo = dot_nt(ob, ao_ref[...]).astype(BF16)
    uo_ref[...] = uo
    for r in range(n_ctx):
        block = (wo2_ref if r % 2 else wo_ref)[r // 2]
        projected[own_ref[0] ^ r] = dot_nt(ob, block)
    blocks = [projected[c] for c in range(n_ctx)]
    x1 = x_ref[...].astype(F32) + jnp.concatenate(blocks, axis=1)
    x1 = x1 + ADAPTER_SCALE * dot_nn(uo, lo_ref[...])
    x1_ref[...] = x1
    h2_ref[...] = (x1 * inverse_norm(x1) * gain_ref[...]).astype(BF16)


def flat_starts(rank):
    starts, at = {}, 0
    names = ("a_qkv", 3), ("a_gu", 2), ("lift_down", 1), ("a_o", 1), ("lift_o", 1), ("b_q", 1)
    for name, tall in names:
        starts[name] = at, tall * rank
        at += 3 * tall * rank
    starts["b_kv"] = at, rank
    return starts


def flat_height(rank):
    start, tall = flat_starts(rank)["b_kv"]
    return start + tall


def attend_back_kernel(own_ref, *refs, n_wa, n_ctx):
    parts, refs = refs[:n_wa], refs[n_wa:]
    (
        agu_ref, gain_ref, x1_ref, g_ref, h2_ref, wo_ref, wo2_ref, lo_ref, ao_ref, attn_ref, ob_ref, uo_ref,
        qb_ref, kb_ref, vb_ref, lse_ref, qpos_ref, kpos_ref, cos_ref, sin_ref, kcos_ref, ksin_ref,
        u1all_ref, h1_ref, h1all_ref, bq_ref, bkv_ref, dx1_ref, dlq_ref, sent_ref, ud_ref, dob, dq_acc, flat, bkv_acc, du_acc, go_cut,
    ) = refs
    rows, width = x1_ref.shape
    keys, kvd = kb_ref.shape
    kvh, heads = kvd // HD, width // HD
    group = heads // kvh
    rank = uo_ref.shape[1]
    scale = 1.0 / math.sqrt(HD)
    got = parts[0][...].astype(F32)
    for part in parts[1:]:
        got = got + part[...].astype(F32)
    small = got[:, width : width + 3 * rank].astype(BF16)
    dug, ud = small[:, : 2 * rank], small[:, 2 * rank :]
    ud_ref[...] = ud
    d_h2 = got[:, :width] + dot_nn(dug, agu_ref[...])
    x1 = x1_ref[...]
    g = g_ref[...]
    d_x1 = g.astype(F32) + norm_pull(x1, inverse_norm(x1), gain_ref[...], d_h2)
    dx1_ref[...] = d_x1
    go = d_x1.astype(BF16)
    duo = (ADAPTER_SCALE * dot_nt(go, lo_ref[...])).astype(BF16)
    third = width // 3
    starts = flat_starts(rank)

    def put(name, value, row=0):
        start, tall = starts[name]
        for i in range(3):
            at = start + i * tall + row
            flat[at : at + value.shape[0], :] = value[:, i * third : (i + 1) * third]

    put("a_gu", dot_tn(dug, h2_ref[...]))
    put("lift_down", ADAPTER_SCALE * dot_tn(ud, g))
    put("a_o", dot_tn(duo, ob_ref[...]))
    put("lift_o", ADAPTER_SCALE * dot_tn(uo_ref[...], go))
    d_attn = dot_nn(duo, ao_ref[...])
    cols = width // n_ctx
    for c in range(n_ctx):
        go_cut[c] = go[:, c * cols : (c + 1) * cols]
    for r in range(n_ctx):
        block = (wo2_ref if r % 2 else wo_ref)[r // 2]
        d_attn = d_attn + dot_nn(go_cut[own_ref[0] ^ r], block)
    dob[...] = d_attn.astype(BF16)
    qpos = jnp.concatenate([qpos_ref[...]] * group, axis=0)
    step = math.gcd(keys, 1024)
    share = step // rows
    bkv_acc[...] = jnp.zeros_like(bkv_acc)
    for kv in range(kvh):
        lane = slice(kv * HD, (kv + 1) * HD)
        v_lane = slice(kvd + kv * HD, kvd + (kv + 1) * HD)
        q = heads_stacked(qb_ref, kv * group, group)
        do = heads_stacked(dob, kv * group, group)
        o = heads_stacked(attn_ref, kv * group, group)
        delta = jnp.sum(do.astype(F32) * o, axis=1, keepdims=True)
        lse = lse_ref[kv]
        dq_acc[...] = jnp.zeros_like(dq_acc)

        def visit(turn_index):
            at = pl.ds(pl.multiple_of(turn_index * step, step), step)
            k = kb_ref[at, lane]
            s = dot_nt(q, k) * scale
            seen = kpos_ref[:, at] <= qpos
            p = jnp.exp(jnp.where(seen, s, MASKED) - lse)
            dp = dot_nt(do, vb_ref[at, lane])
            ds = (p * (dp - delta)).astype(BF16)
            dq_acc[...] += dot_nn(ds, k)
            dk = turn_back(dot_tn(ds, q) * scale, kcos_ref[at, :], ksin_ref[at, :]).astype(BF16)
            dv = dot_tn(p.astype(BF16), do).astype(BF16)
            u1 = u1all_ref[at, :]
            bkv_acc[:, lane] += dot_tn(u1[:, rank : 2 * rank], dk)
            bkv_acc[:, v_lane] += dot_tn(u1[:, 2 * rank :], dv)
            owners = pl.ds(turn_index * share, share)
            sent_ref[owners, :rows, lane] = dk.reshape(share, rows, HD)
            sent_ref[owners, :rows, v_lane] = dv.reshape(share, rows, HD)

        if keys == step:
            visit(0)
        else:
            pl.loop(0, keys // step)(visit)
        for j in range(group):
            head = slice((kv * group + j) * HD, (kv * group + j + 1) * HD)
            dq = dq_acc[j * rows : (j + 1) * rows] * scale
            dlq_ref[:, head] = turn_back(dq, cos_ref[...], sin_ref[...]).astype(BF16)
    d_lq = dlq_ref[...]
    mine = u1all_ref[pl.ds(pl.multiple_of(own_ref[0] * rows, rows), rows), :]
    put("b_q", ADAPTER_SCALE * dot_tn(mine[:, :rank], d_lq))
    start, tall = starts["b_kv"]
    flat[start : start + tall, :] = bkv_acc[...] * ADAPTER_SCALE
    for c in range(n_ctx):
        at = slice(c * rows, (c + 1) * rows)
        low = [dot_nt(sent_ref[c, :rows, :kvd], bkv_ref[0]), dot_nt(sent_ref[c, :rows, kvd:], bkv_ref[1])]
        du_acc[at, :] = (ADAPTER_SCALE * jnp.concatenate(low, axis=1)).astype(BF16)
    duq = (ADAPTER_SCALE * dot_nt(d_lq, bq_ref[...])).astype(BF16)
    put("a_qkv", dot_tn(duq, h1_ref[...]))
    put("a_qkv", dot_tn(du_acc[...], h1all_ref[...]), rank)
    count = flat.shape[0] // n_ctx
    for c in range(n_ctx):
        share = flat[c * count : (c + 1) * count, :]
        sent_ref[c, rows:, :] = share.astype(BF16)


def collect_kernel(got_ref, dlq_ref, bq_ref, bkv_ref, dlkv_ref, du1_ref, share_ref):
    rows = dlq_ref.shape[0]
    rank = bq_ref.shape[0]
    kvd = bkv_ref.shape[2]
    total = got_ref[0].astype(F32)
    for c in range(1, got_ref.shape[0]):
        total = total + got_ref[c].astype(F32)
    dlkv = total[:rows].astype(BF16)
    dlkv_ref[...] = dlkv
    share_ref[...] = total[rows:].astype(BF16)
    du1 = [
        dot_nt(dlq_ref[...], bq_ref[...]),
        dot_nt(dlkv[:, :kvd], bkv_ref[0]),
        dot_nt(dlkv[:, kvd:], bkv_ref[1]),
    ]
    du1_ref[...] = (ADAPTER_SCALE * jnp.concatenate(du1, axis=1)).astype(BF16)


def finish_kernel(*refs, n_wa):
    parts, refs = refs[:n_wa], refs[n_wa:]
    (
        x1_ref, ud_ref, ld_ref, x_ref, gain_ref, dx1_ref, dlq_ref, dlkv_ref, du1_ref, w_ref, a_ref,
        out_ref, gx_ref,
    ) = refs
    n_ctx = w_ref.shape[0]
    q_cols, kv_cols = dlq_ref.shape[1] // n_ctx, dlkv_ref.shape[1] // n_ctx
    out = x1_ref[...] + ADAPTER_SCALE * dot_nn(ud_ref[...], ld_ref[...])
    for part in parts:
        out = out + part[...].astype(F32)
    out_ref[...] = out.astype(BF16)
    d_h1 = dot_nn(du1_ref[...], a_ref[...])
    for c in range(n_ctx):
        block = jnp.concatenate(
            [
                dlq_ref[:, c * q_cols : (c + 1) * q_cols],
                dlkv_ref[:, c * kv_cols : (c + 1) * kv_cols],
            ],
            axis=1,
        )
        d_h1 = d_h1 + dot_nt(block, w_ref[c])
    x = x_ref[...].astype(F32)
    gx_ref[...] = dx1_ref[...] + norm_pull(x, inverse_norm(x), gain_ref[...], d_h1)


def mlp_kernel(*refs, chunks, part_ff, tile, begin, last):
    refs = list(refs)
    index_ref, shift_ref = refs[:2]
    h2_refs, g_refs = refs[2 : 2 + chunks], refs[2 + chunks : 2 + 2 * chunks]
    refs = refs[2 + 2 * chunks :]
    agu_ref, ld_ref, gu_ref, down_ref, lift_ref, ad_ref = refs[:6]
    prior_ref = None if begin else refs[6]
    refs = refs[6 if begin else 7 :]
    out_refs, dh_refs = refs[:chunks], refs[chunks : 2 * chunks]
    grads_ref = refs[2 * chunks]
    h2, gd, low, low_t, out_acc, dh_acc, small_acc, grads = refs[2 * chunks + 1 :]
    rows, width = h2_refs[0].shape
    slots, _, rank, _ = lift_ref.shape
    span = slots * rank
    step, steps = pl.program_id(0), pl.num_programs(0)

    def row_slot(lanes):
        return jnp.concatenate(
            [jnp.full((rows, lanes), index_ref[k], jnp.int32) for k in range(chunks)], axis=0
        )

    @pl.when(step == 0)
    def _():
        for k in range(chunks):
            h2[k * rows : (k + 1) * rows, :] = h2_refs[k][...]
            gd[k * rows : (k + 1) * rows, :] = g_refs[k][...]
        out_acc[...] = jnp.zeros_like(out_acc)
        dh_acc[...] = jnp.zeros_like(dh_acc)
        small_acc[...] = jnp.zeros_like(small_acc)
        grads[...] = jnp.zeros_like(grads) if begin else prior_ref[...]
        lane = lax.broadcasted_iota(jnp.int32, (chunks * rows, span), 1)
        own = lane // rank == row_slot(span)
        flat_a = agu_ref[...]
        parts = [
            dot_nt(h2[...], flat_a[:, :rank].reshape(span, width)).astype(BF16),
            dot_nt(h2[...], flat_a[:, rank:].reshape(span, width)).astype(BF16),
            dot_nt(gd[...], ld_ref[...].reshape(span, width)).astype(BF16),
        ]
        for i, part in enumerate(parts):
            value = jnp.where(own, part.astype(F32) * ADAPTER_SCALE, 0.0)
            low[i] = value.astype(BF16)
            low_t[i] = value.T.astype(BF16)

    def work(first, wide):
        lanes = pl.ds(first, wide)
        w_g, w_u = gu_ref[0, :wide, :], gu_ref[1, :wide, :]
        w_d = down_ref[:wide, :]
        l_g = lift_ref[:, 0, :, :wide].reshape(span, wide)
        l_u = lift_ref[:, 1, :, :wide].reshape(span, wide)
        a_d = ad_ref[:, :, :wide].reshape(span, wide)
        gate = dot_nt(h2[...], w_g) + dot_nn(low[0], l_g)
        up = dot_nt(h2[...], w_u) + dot_nn(low[1], l_u)
        sigma = 1.0 / (1.0 + jnp.exp(-gate))
        swish = gate * sigma
        hidden = (swish * up).astype(BF16)
        d_hidden = dot_nt(gd[...], w_d) + dot_nn(low[2], a_d)
        d_gate = (d_hidden * up * (sigma + swish * (1.0 - sigma))).astype(BF16)
        d_up = (d_hidden * swish).astype(BF16)
        out_acc[...] += dot_nn(hidden, w_d)
        dh_acc[...] += dot_nn(d_gate, w_g) + dot_nn(d_up, w_u)
        small_acc[0] += dot_nt(d_gate, l_g)
        small_acc[1] += dot_nt(d_up, l_u)
        small_acc[2] += dot_nt(hidden, a_d)
        grads[0, :, lanes] += dot_nn(low_t[0], d_gate)
        grads[1, :, lanes] += dot_nn(low_t[1], d_up)
        grads[2, :, lanes] += dot_nn(low_t[2], hidden)

    rest = part_ff % tile
    if rest:
        pl.when(step < steps - 1)(lambda: work(pl.multiple_of(step * tile, tile), tile))
        pl.when(step == steps - 1)(lambda: work(part_ff - rest, rest))
    else:
        work(pl.multiple_of(step * tile, tile), tile)

    @pl.when(step == steps - 1)
    def _():
        for k in range(chunks):
            at = slice(k * rows, (k + 1) * rows)
            out_refs[k][...] = out_acc[at, :].astype(BF16)
            dh_refs[k][:, :width] = dh_acc[at, :].astype(BF16)
            picked = []
            for i in range(3):
                value = jnp.zeros((rows, rank), F32)
                for slot in range(slots):
                    mine = small_acc[i, at, slot * rank : (slot + 1) * rank]
                    value = value + jnp.where(index_ref[k] == slot, mine, 0.0)
                picked.append(value * (ADAPTER_SCALE if i < 2 else 1.0))
            picked.append(jnp.zeros((rows, 128 - 3 * rank), F32))
            dh_refs[k][:, width:] = jnp.concatenate(picked, axis=1).astype(BF16)
        if not last:
            grads_ref[...] = grads[...]
        else:
            n_ctx = grads_ref.shape[0]
            b_rows, a_rows = 2 * span // n_ctx, span // n_ctx
            odd = shift_ref[0] != 0
            tables = []
            for i in range(3):
                value = grads[i]
                if rest % 128:
                    value = jnp.where(odd, pltpu.roll(value, part_ff % 128, 1), value)
                tables.append(value.astype(BF16))
            for c in range(n_ctx):
                at = c * b_rows
                slot, half, at = at // (2 * rank), at // rank % 2, at % rank
                at += slot * rank
                grads_ref[c, :b_rows, :] = tables[half][at : at + b_rows]
                grads_ref[c, b_rows:, :] = tables[2][c * a_rows : (c + 1) * a_rows]


def mlp_call(index, shift, h2s, gs, a_gu, lift_down, w_gu, w_down, lift, a_down, prior, lanes, n_ctx):
    chunks = len(h2s)
    rows, width = h2s[0].shape
    part_ff = w_down.shape[0]
    slots, _, rank, _ = lift.shape
    span = slots * rank
    tile = 768
    steps = -(-part_ff // tile)
    priors = [] if prior is None else [prior]
    smem = pl.BlockSpec(memory_space=pltpu.SMEM)

    def whole(shape):
        return pl.BlockSpec(shape, lambda i: (0,) * len(shape))

    if n_ctx is None:
        grads_shape = jax.ShapeDtypeStruct((3, span, lanes), F32)
    else:
        grads_shape = jax.ShapeDtypeStruct((n_ctx, 3 * span // n_ctx, lanes), BF16)
    total = chunks * rows
    outs = pl.pallas_call(
        lambda *refs: mlp_kernel(
            *refs,
            chunks=chunks,
            part_ff=part_ff,
            tile=tile,
            begin=prior is None,
            last=n_ctx is not None,
        ),
        grid=(steps,),
        out_shape=(jax.ShapeDtypeStruct((rows, width), BF16),) * chunks
        + (jax.ShapeDtypeStruct((rows, width + 128), BF16),) * chunks
        + (grads_shape,),
        in_specs=[smem, smem]
        + [whole((rows, width))] * (2 * chunks)
        + [
            whole(a_gu.shape),
            whole(lift_down.shape),
            pl.BlockSpec((2, tile, width), lambda i: (0, i, 0)),
            pl.BlockSpec((tile, width), lambda i: (i, 0)),
            pl.BlockSpec((slots, 2, rank, tile), lambda i: (0, 0, 0, i)),
            pl.BlockSpec((slots, rank, tile), lambda i: (0, 0, i)),
        ]
        + [whole(table.shape) for table in priors],
        out_specs=(whole((rows, width)),) * chunks
        + (whole((rows, width + 128)),) * chunks
        + (whole(grads_shape.shape),),
        scratch_shapes=[
            pltpu.VMEM((total, width), BF16),
            pltpu.VMEM((total, width), BF16),
            pltpu.VMEM((3, total, span), BF16),
            pltpu.VMEM((3, span, total), BF16),
            pltpu.VMEM((total, width), F32),
            pltpu.VMEM((total, width), F32),
            pltpu.VMEM((3, total, span), F32),
            pltpu.VMEM((3, span, lanes), F32),
        ],
        compiler_params=pltpu.CompilerParams(vmem_limit_bytes=50 << 20),
        cost_estimate=pl.CostEstimate(
            flops=12 * total * width * part_ff,
            bytes_accessed=6 * width * part_ff,
            transcendentals=0,
        ),
    )(index, shift, *h2s, *gs, a_gu, lift_down, w_gu, w_down, lift, a_down, *priors)
    return outs[:chunks], outs[chunks : 2 * chunks], outs[-1]


def swap(value, axis, count, k):
    return lax.ppermute(value, axis, [(i, i ^ k) for i in range(count)])


def make_per_device(n_ctx, n_wa):
    def wa_exchange(value):
        return [value] + [swap(value, "wa", n_wa, k) for k in range(1, n_wa)]

    def absolute(parts, axis):
        own = lax.axis_index(axis)
        parts = list(parts)
        bit = 1
        while bit < len(parts):
            other = own & bit != 0
            parts = [jnp.where(other, parts[i ^ bit], parts[i]) for i in range(len(parts))]
            bit *= 2
        return parts

    def gather_near(value):
        return [value] + [swap(value, "ctx", n_ctx, 2 * r) for r in range(1, n_ctx // 2)]

    def gather_cores(same):
        same = jnp.stack(same)
        return same, swap(same, "ctx", n_ctx, 1)

    def per_device(
        tokens,
        cotangent,
        adapter_index,
        deal,
        w_qkv,
        b_qkv,
        w_o,
        w_gu,
        w_down,
        gain_attn,
        gain_mlp,
        a_qkv,
        b_q,
        b_kv,
        a_o,
        lift_o,
        a_gu,
        lift_gu,
        a_down,
        lift_down,
    ):
        rows, width = tokens.shape[1:]
        block = rows // 2
        rank = b_q.shape[1]
        slots = a_qkv.shape[0]
        kvd = b_kv.shape[3]
        heads = width // HD
        kvh = kvd // HD
        group = heads // kvh
        part_ff = w_down.shape[0]
        wa = lax.axis_index("wa")
        ctx = lax.axis_index("ctx")
        chosen = adapter_index[0]

        def picked(table):
            return lax.dynamic_index_in_dim(table, chosen, 0, keepdims=False)

        grad_out_bf = cotangent[0]
        x_bf = tokens[0]
        q_cols, kv_cols = width // n_ctx, 2 * kvd // n_ctx
        gain_one = gain_attn.astype(F32)[None]
        gain_two = gain_mlp.astype(F32)[None]
        s_aqkv, s_bq, s_bkv = picked(a_qkv), picked(b_q), picked(b_kv)
        s_ao, s_lo, s_agu, s_ld = picked(a_o), picked(lift_o), picked(a_gu), picked(lift_down)

        x = x_bf.astype(F32)
        h1 = (x * inverse_norm(x) * gain_one).astype(BF16)
        h1_all = lax.all_gather(h1, "ctx", axis=0, tiled=True)

        def block_of(table):
            return jnp.concatenate(
                [
                    lax.dynamic_slice_in_dim(table[:, :width], ctx * q_cols, q_cols, 1),
                    lax.dynamic_slice_in_dim(table[:, width:], ctx * kv_cols, kv_cols, 1),
                ],
                axis=1,
            )

        o_mine = lax.dynamic_slice_in_dim(w_o, ctx * q_cols, q_cols, 1).T
        mark = jnp.full((16, q_cols + kv_cols), chosen, jnp.int32).astype(BF16)
        w_mine = jnp.concatenate([block_of(w_qkv), mark], axis=0)
        depth = w_qkv.shape[0]
        o_parts = wa_exchange(o_mine)
        o_parts, w_mine = lax.optimization_barrier((o_parts, w_mine))
        w_parts = wa_exchange(w_mine)
        o_block = jnp.concatenate(absolute(o_parts, "wa"), axis=1)
        o_near = gather_near(o_block)
        b_all = jnp.concatenate(
            [
                jnp.pad(s_bq, ((0, 0), (0, 2 * kvd))),
                jnp.pad(s_bkv[0], ((0, 0), (width, kvd))),
                jnp.pad(s_bkv[1], ((0, 0), (width + kvd, 0))),
            ],
            axis=0,
        )
        key_pos = row_positions(deal, jnp.arange(n_ctx * rows, dtype=jnp.int32), block)
        key_cos, key_sin = rope_tables(key_pos)

        def own_rows(table):
            return lax.dynamic_slice_in_dim(table, ctx * rows, rows, 0)

        query_pos, cosine, sine = own_rows(key_pos)[:, None], own_rows(key_cos), own_rows(key_sin)
        key_pos = key_pos[None]
        lift_part = lax.dynamic_slice_in_dim(lift_gu, wa * part_ff, part_ff, 3)
        down_part = lax.dynamic_slice_in_dim(a_down, wa * part_ff, part_ff, 2)
        tables = (key_cos, key_sin, cosine, sine, query_pos, key_pos)
        picks = (s_aqkv, s_bq, s_bkv, s_ao, s_lo, s_agu, s_ld, lift_part, down_part)
        sides = (block_of(b_all), block_of(b_qkv[None]).astype(F32))
        w_parts, grad_sent = lax.optimization_barrier((tuple(w_parts), grad_out_bf))
        held = (h1_all, w_parts, o_near, tables, picks, sides)
        held = lax.optimization_barrier(held)
        h1_all, w_parts, o_near, tables, picks, sides = held
        key_cos, key_sin, cosine, sine, query_pos, key_pos = tables
        s_aqkv, s_bq, s_bkv, s_ao, s_lo, s_agu, s_ld, lift_part, down_part = picks
        w_block = jnp.concatenate(absolute([part[:depth] for part in w_parts], "wa"), axis=0)
        index_all = jnp.stack([part[depth, 0] for part in w_parts]).astype(jnp.int32)
        sent, u1_all = local_call(
            functools.partial(project_kernel, q_cols=q_cols),
            [
                ((n_ctx, rows, -(-(2 * kvd + q_cols) // 128) * 128), BF16),
                ((n_ctx * rows, 3 * rank), BF16),
            ],
            h1_all,
            w_block,
            s_aqkv,
            *sides,
            tight=True,
        )
        grads_all = wa_exchange(grad_sent)
        got = lax.all_to_all(sent, "ctx", 0, 0, tiled=True)
        u1_all, o_near = lax.optimization_barrier((u1_all, o_near))
        o_near = gather_cores(o_near)
        held = (got, o_near, index_all)
        got, o_near, index_all = lax.optimization_barrier(held)
        own_ctx = ctx.astype(jnp.int32)[None]
        qb, kb, vb, lse, attn, ob = local_call(
            attend_kernel,
            [
                ((rows, width), BF16),
                ((n_ctx * rows, kvd), BF16),
                ((n_ctx * rows, kvd), BF16),
                ((kvh, group * rows, 1), F32),
                ((rows, width), F32),
                ((rows, width), BF16),
            ],
            got,
            cosine,
            sine,
            key_cos,
            key_sin,
            query_pos,
            key_pos,
            tight=True,
            cost=9 * 10**9,
        )
        ob, grads_all = lax.optimization_barrier((ob, grads_all))
        uo, x1, h2 = local_call(
            output_kernel,
            [((rows, rank), BF16), ((rows, width), F32), ((rows, width), BF16)],
            ob,
            x_bf,
            *o_near,
            s_ao,
            s_lo,
            gain_two,
            tight=True,
            scalars=(own_ctx,),
            scratch=[pltpu.VMEM((n_ctx, rows, q_cols), F32)],
        )

        h2, w_block = lax.optimization_barrier((h2, w_block))
        w_blocks = lax.all_gather(w_block, "ctx", axis=0, tiled=False)

        first = wa * part_ff
        lanes = -(-max(part_ff + j * part_ff % 128 for j in range(n_wa)) // 128) * 128
        ff_grads = None
        shift = (first % 128).astype(jnp.int32)[None]
        w_gu_t = w_gu.transpose(0, 2, 1)
        h2_all = [h2] + [swap(h2, "wa", n_wa, k) for k in range(1, n_wa - 1)]
        h2_last, h2_all, grads_all = lax.optimization_barrier((h2, h2_all, grads_all))
        h2_all.append(swap(h2_last, "wa", n_wa, n_wa - 1))
        out_sent, d_h2_sent = {}, {}
        groups = [[0], [1, 2], [3]] if n_wa == 4 else [[k] for k in range(n_wa)]
        for at, group_wa in enumerate(groups):
            done = mlp_call(
                jnp.concatenate([index_all[k : k + 1] for k in group_wa]),
                shift,
                [h2 if k == 0 else h2_all[k] for k in group_wa],
                [grad_out_bf if k == 0 else grads_all[k] for k in group_wa],
                a_gu,
                lift_down,
                w_gu_t,
                w_down,
                lift_part,
                down_part,
                ff_grads,
                lanes,
                n_ctx if at == len(groups) - 1 else None,
            )
            for k, part, d_part in zip(group_wa, done[0], done[1]):
                out_sent[k], d_h2_sent[k] = part, d_part
            ff_grads = done[2]

        def wa_return(parts):
            return [parts[0]] + [swap(parts[k], "wa", n_wa, k) for k in range(1, n_wa)]

        d_h2_parts = wa_return(d_h2_sent)
        held = (tuple(out_sent[k] for k in range(n_wa)), tuple(d_h2_parts), w_blocks)
        out_sent, d_h2_parts, w_blocks = lax.optimization_barrier(held)
        ff_got = lax.all_to_all(ff_grads, "ctx", 0, 0, tiled=True)
        ff_share = jnp.sum(ff_got.astype(F32), axis=0).astype(BF16)
        count = flat_height(rank) // n_ctx
        d_x1, dl_q, sent, ud = local_call(
            functools.partial(attend_back_kernel, n_wa=n_wa, n_ctx=n_ctx),
            [
                ((rows, width), F32),
                ((rows, width), BF16),
                ((n_ctx, rows + count, 2 * kvd), BF16),
                ((rows, rank), BF16),
            ],
            *d_h2_parts,
            s_agu,
            gain_two,
            x1,
            grad_out_bf,
            h2,
            *o_near,
            s_lo,
            s_ao,
            attn,
            ob,
            uo,
            qb,
            kb,
            vb,
            lse,
            query_pos,
            key_pos,
            cosine,
            sine,
            key_cos,
            key_sin,
            u1_all,
            h1,
            h1_all,
            s_bq,
            s_bkv,
            scalars=(own_ctx,),
            scratch=[
                pltpu.VMEM((rows, width), BF16),
                pltpu.VMEM((group * rows, HD), F32),
                pltpu.VMEM((count * n_ctx, width // 3), F32),
                pltpu.VMEM((rank, 2 * kvd), F32),
                pltpu.VMEM((n_ctx * rows, 2 * rank), BF16),
                pltpu.VMEM((n_ctx, rows, q_cols), BF16),
            ],
        )
        got = lax.all_to_all(sent, "ctx", 0, 0, tiled=True)
        ff_wa = jnp.stack(wa_exchange(ff_share))
        out_parts = [
            lax.psum_scatter(
                jnp.concatenate(absolute(out_sent, "wa"), axis=0),
                "wa",
                scatter_dimension=0,
                tiled=True,
            )
        ]
        got, ff_wa, out_parts = lax.optimization_barrier((got, ff_wa, out_parts))
        ff_all = lax.all_gather(ff_wa, "ctx", axis=0, tiled=False)
        dl_kv, du1, share = local_call(
            collect_kernel,
            [
                ((rows, 2 * kvd), BF16),
                ((rows, 3 * rank), BF16),
                ((count, 2 * kvd), BF16),
            ],
            got,
            dl_q,
            s_bq,
            s_bkv,
        )
        share_wa = jnp.stack(wa_exchange(share))
        share_near = gather_near(share_wa)
        out, grad_x = local_call(
            functools.partial(finish_kernel, n_wa=len(out_parts)),
            [((rows, width), BF16), ((rows, width), F32)],
            *out_parts,
            x1,
            ud,
            s_ld,
            x_bf,
            gain_one,
            d_x1,
            dl_q,
            dl_kv,
            du1,
            w_blocks,
            s_aqkv,
            cost=7 * 10**9,
        )
        held = (share_near, out, grad_x)
        share_near, out, grad_x = lax.optimization_barrier(held)
        seq_all = jnp.stack(gather_cores(share_near))
        own_wa = wa.astype(jnp.int32)[None]
        r_bgu, r_ad = ff_results(own_wa, ff_all, slots, rank, part_ff)
        tables = {
            "a_qkv": a_qkv,
            "b_q": b_q,
            "b_kv": b_kv,
            "a_o": a_o,
            "lift_o": lift_o,
            "a_gu": a_gu,
            "lift_down": lift_down,
        }
        layout = tuple(flat_starts(rank)[name] for name in tables)
        r_aqkv, r_bq, r_bkv, r_ao, r_lo, r_agu, r_ld = seq_results(
            jnp.concatenate([own_wa, own_ctx]), index_all, seq_all, [table.shape for table in tables.values()], layout
        )
        return (
            out[None],
            grad_x[None],
            r_aqkv,
            r_bq,
            r_bkv,
            r_ao,
            r_lo,
            r_agu,
            r_bgu,
            r_ad,
            r_ld,
        )

    return per_device


def solution(mesh):
    rep = P()
    return jax.shard_map(
        make_per_device(mesh.shape["ctx"], mesh.shape["wa"]),
        mesh=mesh,
        in_specs=(
            P("wa", "ctx", None),
            P("wa", "ctx", None),
            P("wa"),
            rep,
            P("wa", None),
            rep,
            P("wa", None),
            P(None, None, "wa"),
            P("wa", None),
        )
        + (rep,) * 11,
        out_specs=(P("wa", "ctx", None), P("wa", "ctx", None)) + (rep,) * 9,
        check_vma=False,
    )
```

```python
import functools
import math

import jax
import jax.numpy as jnp
from jax import lax
from jax.experimental import pallas as pl
from jax.experimental.pallas import tpu as pltpu
from jax.sharding import PartitionSpec as P

HD = 128
EPS = 1e-06
ROPE_BASE = 1000000.0
ADAPTER_SCALE = 2.0
MASKED = -1e30
F32 = jnp.float32
BF16 = jnp.bfloat16


def dot_nn(a, b):
    return lax.dot_general(a, b, (((1,), (0,)), ((), ())), preferred_element_type=F32)


def dot_tn(a, b):
    return lax.dot_general(a, b, (((0,), (0,)), ((), ())), preferred_element_type=F32)


def dot_nt(a, b):
    return lax.dot_general(a, b, (((1,), (1,)), ((), ())), preferred_element_type=F32)


def inverse_norm(rows):
    return lax.rsqrt(jnp.mean(rows * rows, axis=-1, keepdims=True) + EPS)


def norm_pull(rows, inv, gain, grad):
    scaled = gain * grad
    return inv * scaled - rows * (inv * inv * inv) * jnp.mean(rows * scaled, axis=-1, keepdims=True)


def rope_tables(pos):
    half = HD // 2
    freq = ROPE_BASE ** (-jnp.arange(half, dtype=F32) * 2.0 / HD)
    angle = pos.astype(F32)[:, None] * freq[None, :]
    cosine, sine = jnp.cos(angle), jnp.sin(angle)
    return jnp.concatenate([cosine, cosine], axis=1), jnp.concatenate([-sine, sine], axis=1)


def row_positions(deal, rows, block):
    owner = rows // (2 * block)
    local = rows % (2 * block)
    table = jnp.arange(deal.shape[0], dtype=jnp.int32)
    pair = jnp.sum(jnp.where(owner[:, None] == table[None, :], deal[None, :], 0), axis=1)
    return jnp.where(
        local < block, pair * block + local, (2 * deal.shape[0] - 1 - pair) * block + local - block
    )


def ff_results_kernel(wa_ref, got_ref, bgu_ref, ad_ref, *, part_ff):
    n_ctx, n_wa, _, lanes = got_ref.shape
    own = wa_ref[0]
    rank = bgu_ref.shape[2]
    b_rows = bgu_ref.shape[0] * 2 * rank // n_ctx
    a_rows = ad_ref.shape[0] * rank // n_ctx
    starts = [j * part_ff // 128 * 128 for j in range(n_wa)]

    def write(read, store):
        left = None
        for j in range(n_wa):
            block = read(j).astype(F32)
            stop = starts[j + 1] - starts[j] if j + 1 < n_wa else lanes
            if left is not None:
                store(starts[j], block[:, :128] + left)
            first = 0 if left is None else 128
            store(starts[j] + first, block[:, first:stop])
            left = block[:, stop:] if stop < lanes else None

    for c in range(n_ctx):
        at = c * b_rows
        slot, half, low = at // (2 * rank), at // rank % 2, at % rank

        def put_b(lane, value):
            bgu_ref[slot, half, low : low + b_rows, lane : lane + value.shape[1]] = value

        write(lambda j: got_ref[c, own ^ j, :b_rows], put_b)
        at = c * a_rows
        slot, low = at // rank, at % rank

        def put_a(lane, value):
            ad_ref[slot, low : low + a_rows, lane : lane + value.shape[1]] = value

        write(lambda j: got_ref[c, own ^ j, b_rows:], put_a)


def ff_results(wa, got, slots, rank, part_ff):
    n_wa = got.shape[1]
    return pl.pallas_call(
        lambda *refs: ff_results_kernel(*refs, part_ff=part_ff),
        out_shape=(
            jax.ShapeDtypeStruct((slots, 2, rank, n_wa * part_ff), F32),
            jax.ShapeDtypeStruct((slots, rank, n_wa * part_ff), F32),
        ),
        in_specs=[pl.BlockSpec(memory_space=pltpu.SMEM), pl.BlockSpec(memory_space=pltpu.VMEM)],
        out_specs=(pl.BlockSpec(memory_space=pltpu.VMEM),) * 2,
        compiler_params=pltpu.CompilerParams(vmem_limit_bytes=48 << 20),
    )(wa, got)


def seq_results_kernel(own_ref, index_ref, got_ref, *out_refs, layout):
    _, n_chip, n_wa, share, third = got_ref.shape
    n_ctx = 2 * n_chip
    own, here = own_ref[0], own_ref[1]
    slots = out_refs[0].shape[0]
    for c in range(n_ctx):
        off = here ^ c
        terms = [got_ref[off & 1, off >> 1, own ^ j].astype(F32) for j in range(n_wa)]
        for slot in range(slots):
            total = jnp.zeros((share, third), F32)
            for j in range(n_wa):
                total = total + jnp.where(index_ref[own ^ j] == slot, terms[j], 0.0)
            for ref, (start, tall) in zip(out_refs, layout):
                for part in range(3 if len(ref.shape) == 3 else 1):
                    first = start + part * tall
                    low, high = max(first, c * share), min(first + tall, (c + 1) * share)
                    if low >= high:
                        continue
                    value = total[low - c * share : high - c * share]
                    at = slice(low - first, high - first)
                    if len(ref.shape) == 3:
                        ref[slot, at, part * third : (part + 1) * third] = value
                    else:
                        wide = ref.shape[3]
                        for i in range(ref.shape[1]):
                            ref[slot, i, at, :] = value[:, i * wide : (i + 1) * wide]


def seq_results(wa, index_all, got, shapes, layout):
    smem = pl.BlockSpec(memory_space=pltpu.SMEM)
    vmem = pl.BlockSpec(memory_space=pltpu.VMEM)
    return pl.pallas_call(
        lambda *refs: seq_results_kernel(*refs, layout=layout),
        out_shape=tuple(jax.ShapeDtypeStruct(shape, F32) for shape in shapes),
        in_specs=[smem, smem, vmem],
        out_specs=(vmem,) * len(shapes),
        compiler_params=pltpu.CompilerParams(vmem_limit_bytes=48 << 20),
    )(wa, index_all, got)


def local_call(kernel, out_shapes, *args, scratch=(), tight=False, cost=None, scalars=(), far=()):
    vmem = pl.BlockSpec(memory_space=pltpu.VMEM)
    smem = pl.BlockSpec(memory_space=pltpu.SMEM)
    limit = 56 << 20
    if tight:
        held = sum(arg.size * arg.dtype.itemsize for arg in args)
        held += sum(math.prod(shape) * jnp.dtype(kind).itemsize for shape, kind in out_shapes)
        limit = min(held + (20 << 20), limit)
    return pl.pallas_call(
        kernel,
        out_shape=tuple(jax.ShapeDtypeStruct(shape, kind) for shape, kind in out_shapes),
        in_specs=[smem] * len(scalars)
        + [pl.BlockSpec(memory_space=pl.ANY) if i in far else vmem for i in range(len(args))],
        out_specs=(vmem,) * len(out_shapes),
        scratch_shapes=list(scratch),
        compiler_params=pltpu.CompilerParams(vmem_limit_bytes=limit),
        cost_estimate=cost and pl.CostEstimate(flops=cost, bytes_accessed=0, transcendentals=0),
    )(*scalars, *args)


def project_kernel(h1_ref, w_ref, a_ref, b_ref, bias_ref, sent_ref, u1_ref, *, q_cols):
    n_ctx, rows, wide = sent_ref.shape
    kv_cols = w_ref.shape[1] - q_cols
    h1 = h1_ref[...]
    u1 = dot_nt(h1, a_ref[...]).astype(BF16)
    u1_ref[...] = u1
    lin = dot_nn(h1, w_ref[...]) + bias_ref[...] + ADAPTER_SCALE * dot_nn(u1, b_ref[...])
    lin = lin.astype(BF16)
    pieces = [lin[c * rows : (c + 1) * rows, q_cols:] for c in range(n_ctx)]
    kv = jnp.concatenate(pieces, axis=1)
    fill = jnp.zeros((rows, wide - n_ctx * kv_cols - q_cols), BF16)
    for c in range(n_ctx):
        sent_ref[c, :, : n_ctx * kv_cols] = kv
        own = lin[c * rows : (c + 1) * rows, :q_cols]
        sent_ref[c, :, n_ctx * kv_cols :] = jnp.concatenate([own, fill], axis=1)


def turn(value, cosine, sine):
    return value * cosine + pltpu.roll(value, HD // 2, 1) * sine


def turn_back(value, cosine, sine):
    return value * cosine + pltpu.roll(value * sine, HD // 2, 1)


def heads_stacked(table, first, group):
    return jnp.concatenate(
        [table[:, (first + j) * HD : (first + j + 1) * HD] for j in range(group)], axis=0
    )


def attend_kernel(
    got_ref, cos_ref, sin_ref, kcos_ref, ksin_ref, qpos_ref, kpos_ref, qb_ref, kb_ref, vb_ref,
    lse_ref, attn_ref, ob_ref,
):
    n_ctx = got_ref.shape[0]
    rows, width = attn_ref.shape
    kvd = kb_ref.shape[1]
    kvh, heads = kvd // HD, width // HD
    group = heads // kvh
    q_cols, kv_cols = width // n_ctx, 2 * kvd // n_ctx
    scale = 1.0 / math.sqrt(HD)
    cosine, sine = cos_ref[...], sin_ref[...]
    q_lin = jnp.concatenate(
        [got_ref[c, :, 2 * kvd : 2 * kvd + q_cols] for c in range(n_ctx)], axis=1
    )
    for h in range(heads):
        lane = slice(h * HD, (h + 1) * HD)
        qb_ref[:, lane] = turn(q_lin[:, lane].astype(F32), cosine, sine).astype(BF16)
    for g in range(n_ctx):
        at = slice(g * rows, (g + 1) * rows)
        cut = slice(g * kv_cols, (g + 1) * kv_cols)
        kv_lin = jnp.concatenate([got_ref[c, :, cut] for c in range(n_ctx)], axis=1)
        kcos, ksin = kcos_ref[at, :], ksin_ref[at, :]
        for h in range(kvh):
            lane = slice(h * HD, (h + 1) * HD)
            kb_ref[at, lane] = turn(kv_lin[:, lane].astype(F32), kcos, ksin).astype(BF16)
        vb_ref[at, :] = kv_lin[:, kvd:]
    qpos = jnp.concatenate([qpos_ref[...]] * group, axis=0)
    seen = kpos_ref[...] <= qpos
    for g in range(kvh):
        q = heads_stacked(qb_ref, g * group, group)
        s = dot_nt(q, kb_ref[:, g * HD : (g + 1) * HD]) * scale
        s = jnp.where(seen, s, MASKED)
        top = jnp.max(s, axis=1, keepdims=True)
        e = jnp.exp(s - top)
        total = jnp.sum(e, axis=1, keepdims=True)
        lse_ref[g] = top + jnp.log(total)
        pb = (e * (1.0 / total)).astype(BF16)
        o = dot_nn(pb, vb_ref[:, g * HD : (g + 1) * HD])
        for j in range(group):
            lane = slice((g * group + j) * HD, (g * group + j + 1) * HD)
            attn_ref[:, lane] = o[j * rows : (j + 1) * rows]
    ob_ref[...] = attn_ref[...].astype(BF16)


def output_kernel(
    own_ref, ob_ref, x_ref, wo_ref, wo2_ref, ao_ref, lo_ref, gain_ref, uo_ref, x1_ref, h2_ref,
    projected,
):
    n_ctx = projected.shape[0]
    ob = ob_ref[...]
    uo = dot_nt(ob, ao_ref[...]).astype(BF16)
    uo_ref[...] = uo
    for r in range(n_ctx):
        block = (wo2_ref if r % 2 else wo_ref)[r // 2]
        projected[own_ref[0] ^ r] = dot_nt(ob, block)
    blocks = [projected[c] for c in range(n_ctx)]
    x1 = x_ref[...].astype(F32) + jnp.concatenate(blocks, axis=1)
    x1 = x1 + ADAPTER_SCALE * dot_nn(uo, lo_ref[...])
    x1_ref[...] = x1
    h2_ref[...] = (x1 * inverse_norm(x1) * gain_ref[...]).astype(BF16)


def flat_starts(rank):
    starts, at = {}, 0
    names = ("a_qkv", 3), ("a_gu", 2), ("lift_down", 1), ("a_o", 1), ("lift_o", 1), ("b_q", 1)
    for name, tall in names:
        starts[name] = at, tall * rank
        at += 3 * tall * rank
    starts["b_kv"] = at, rank
    return starts


def flat_height(rank):
    start, tall = flat_starts(rank)["b_kv"]
    return start + tall


def attend_back_kernel(own_ref, *refs, n_wa, n_ctx):
    parts, refs = refs[:n_wa], refs[n_wa:]
    (
        agu_ref, gain_ref, x1_ref, g_ref, h2_ref, wo_ref, wo2_ref, lo_ref, ao_ref, attn_ref, ob_ref, uo_ref,
        qb_ref, kb_ref, vb_ref, lse_ref, qpos_ref, kpos_ref, cos_ref, sin_ref, kcos_ref, ksin_ref,
        u1all_ref, h1_ref, h1all_ref, bq_ref, bkv_ref, dx1_ref, dlq_ref, sent_ref, ud_ref, dob, dq_acc, flat, bkv_acc, du_acc, go_cut,
        wo_held, wo2_held, h1all_held, arrive,
    ) = refs
    rows, width = x1_ref.shape
    keys, kvd = kb_ref.shape
    kvh, heads = kvd // HD, width // HD
    group = heads // kvh
    rank = uo_ref.shape[1]
    scale = 1.0 / math.sqrt(HD)
    pairs = (wo_ref, wo_held), (wo2_ref, wo2_held), (h1all_ref, h1all_held)
    copies = [pltpu.make_async_copy(a, b, arrive.at[i]) for i, (a, b) in enumerate(pairs)]
    for copy in copies:
        copy.start()
    got = parts[0][...].astype(F32)
    for part in parts[1:]:
        got = got + part[...].astype(F32)
    small = got[:, width : width + 3 * rank].astype(BF16)
    dug, ud = small[:, : 2 * rank], small[:, 2 * rank :]
    ud_ref[...] = ud
    d_h2 = got[:, :width] + dot_nn(dug, agu_ref[...])
    x1 = x1_ref[...]
    g = g_ref[...]
    d_x1 = g.astype(F32) + norm_pull(x1, inverse_norm(x1), gain_ref[...], d_h2)
    dx1_ref[...] = d_x1
    go = d_x1.astype(BF16)
    duo = (ADAPTER_SCALE * dot_nt(go, lo_ref[...])).astype(BF16)
    third = width // 3
    starts = flat_starts(rank)

    def put(name, value, row=0):
        start, tall = starts[name]
        for i in range(3):
            at = start + i * tall + row
            flat[at : at + value.shape[0], :] = value[:, i * third : (i + 1) * third]

    put("a_gu", dot_tn(dug, h2_ref[...]))
    put("lift_down", ADAPTER_SCALE * dot_tn(ud, g))
    put("a_o", dot_tn(duo, ob_ref[...]))
    put("lift_o", ADAPTER_SCALE * dot_tn(uo_ref[...], go))
    d_attn = dot_nn(duo, ao_ref[...])
    cols = width // n_ctx
    for c in range(n_ctx):
        go_cut[c] = go[:, c * cols : (c + 1) * cols]
    copies[0].wait()
    copies[1].wait()
    for r in range(n_ctx):
        block = (wo2_held if r % 2 else wo_held)[r // 2]
        d_attn = d_attn + dot_nn(go_cut[own_ref[0] ^ r], block)
    dob[...] = d_attn.astype(BF16)
    qpos = jnp.concatenate([qpos_ref[...]] * group, axis=0)
    step = math.gcd(keys, 1024)
    share = step // rows
    bkv_acc[...] = jnp.zeros_like(bkv_acc)
    for kv in range(kvh):
        lane = slice(kv * HD, (kv + 1) * HD)
        v_lane = slice(kvd + kv * HD, kvd + (kv + 1) * HD)
        q = heads_stacked(qb_ref, kv * group, group)
        do = heads_stacked(dob, kv * group, group)
        o = heads_stacked(attn_ref, kv * group, group)
        delta = jnp.sum(do.astype(F32) * o, axis=1, keepdims=True)
        lse = lse_ref[kv]
        dq_acc[...] = jnp.zeros_like(dq_acc)

        def visit(turn_index):
            at = pl.ds(pl.multiple_of(turn_index * step, step), step)
            k = kb_ref[at, lane]
            s = dot_nt(q, k) * scale
            seen = kpos_ref[:, at] <= qpos
            p = jnp.exp(jnp.where(seen, s, MASKED) - lse)
            dp = dot_nt(do, vb_ref[at, lane])
            ds = (p * (dp - delta)).astype(BF16)
            dq_acc[...] += dot_nn(ds, k)
            dk = turn_back(dot_tn(ds, q) * scale, kcos_ref[at, :], ksin_ref[at, :]).astype(BF16)
            dv = dot_tn(p.astype(BF16), do).astype(BF16)
            u1 = u1all_ref[at, :]
            bkv_acc[:, lane] += dot_tn(u1[:, rank : 2 * rank], dk)
            bkv_acc[:, v_lane] += dot_tn(u1[:, 2 * rank :], dv)
            owners = pl.ds(turn_index * share, share)
            sent_ref[owners, :rows, lane] = dk.reshape(share, rows, HD)
            sent_ref[owners, :rows, v_lane] = dv.reshape(share, rows, HD)

        if keys == step:
            visit(0)
        else:
            pl.loop(0, keys // step)(visit)
        for j in range(group):
            head = slice((kv * group + j) * HD, (kv * group + j + 1) * HD)
            dq = dq_acc[j * rows : (j + 1) * rows] * scale
            dlq_ref[:, head] = turn_back(dq, cos_ref[...], sin_ref[...]).astype(BF16)
    d_lq = dlq_ref[...]
    mine = u1all_ref[pl.ds(pl.multiple_of(own_ref[0] * rows, rows), rows), :]
    put("b_q", ADAPTER_SCALE * dot_tn(mine[:, :rank], d_lq))
    start, tall = starts["b_kv"]
    flat[start : start + tall, :] = bkv_acc[...] * ADAPTER_SCALE
    for c in range(n_ctx):
        at = slice(c * rows, (c + 1) * rows)
        low = [dot_nt(sent_ref[c, :rows, :kvd], bkv_ref[0]), dot_nt(sent_ref[c, :rows, kvd:], bkv_ref[1])]
        du_acc[at, :] = (ADAPTER_SCALE * jnp.concatenate(low, axis=1)).astype(BF16)
    duq = (ADAPTER_SCALE * dot_nt(d_lq, bq_ref[...])).astype(BF16)
    put("a_qkv", dot_tn(duq, h1_ref[...]))
    copies[2].wait()
    put("a_qkv", dot_tn(du_acc[...], h1all_held[...]), rank)
    count = flat.shape[0] // n_ctx
    for c in range(n_ctx):
        share = flat[c * count : (c + 1) * count, :]
        sent_ref[c, rows:, :] = share.astype(BF16)


def collect_kernel(got_ref, dlq_ref, bq_ref, bkv_ref, dlkv_ref, du1_ref, share_ref):
    rows = dlq_ref.shape[0]
    rank = bq_ref.shape[0]
    kvd = bkv_ref.shape[2]
    total = got_ref[0].astype(F32)
    for c in range(1, got_ref.shape[0]):
        total = total + got_ref[c].astype(F32)
    dlkv = total[:rows].astype(BF16)
    dlkv_ref[...] = dlkv
    share_ref[...] = total[rows:].astype(BF16)
    du1 = [
        dot_nt(dlq_ref[...], bq_ref[...]),
        dot_nt(dlkv[:, :kvd], bkv_ref[0]),
        dot_nt(dlkv[:, kvd:], bkv_ref[1]),
    ]
    du1_ref[...] = (ADAPTER_SCALE * jnp.concatenate(du1, axis=1)).astype(BF16)


def finish_kernel(*refs, n_wa):
    parts, refs = refs[:n_wa], refs[n_wa:]
    (
        x1_ref, ud_ref, ld_ref, x_ref, gain_ref, dx1_ref, dlq_ref, dlkv_ref, du1_ref, w_ref, a_ref,
        out_ref, gx_ref, w_held, arrive,
    ) = refs
    copy = pltpu.make_async_copy(w_ref, w_held, arrive)
    copy.start()
    n_ctx = w_ref.shape[0]
    q_cols, kv_cols = dlq_ref.shape[1] // n_ctx, dlkv_ref.shape[1] // n_ctx
    out = x1_ref[...] + ADAPTER_SCALE * dot_nn(ud_ref[...], ld_ref[...])
    for part in parts:
        out = out + part[...].astype(F32)
    out_ref[...] = out.astype(BF16)
    d_h1 = dot_nn(du1_ref[...], a_ref[...])
    copy.wait()
    for c in range(n_ctx):
        block = jnp.concatenate(
            [
                dlq_ref[:, c * q_cols : (c + 1) * q_cols],
                dlkv_ref[:, c * kv_cols : (c + 1) * kv_cols],
            ],
            axis=1,
        )
        d_h1 = d_h1 + dot_nt(block, w_held[c])
    x = x_ref[...].astype(F32)
    gx_ref[...] = dx1_ref[...] + norm_pull(x, inverse_norm(x), gain_ref[...], d_h1)


def mlp_kernel(*refs, chunks, part_ff, tile, begin, last):
    refs = list(refs)
    index_ref, shift_ref = refs[:2]
    h2_refs, g_refs = refs[2 : 2 + chunks], refs[2 + chunks : 2 + 2 * chunks]
    refs = refs[2 + 2 * chunks :]
    agu_ref, ld_ref, gu_ref, down_ref, lift_ref, ad_ref = refs[:6]
    prior_ref = None if begin else refs[6]
    refs = refs[6 if begin else 7 :]
    out_refs, dh_refs = refs[:chunks], refs[chunks : 2 * chunks]
    grads_ref = refs[2 * chunks]
    h2, gd, low, low_t, out_acc, dh_acc, small_acc, grads = refs[2 * chunks + 1 :]
    rows, width = h2_refs[0].shape
    slots, _, rank, _ = lift_ref.shape
    span = slots * rank
    step, steps = pl.program_id(0), pl.num_programs(0)

    def row_slot(lanes):
        return jnp.concatenate(
            [jnp.full((rows, lanes), index_ref[k], jnp.int32) for k in range(chunks)], axis=0
        )

    @pl.when(step == 0)
    def _():
        for k in range(chunks):
            h2[k * rows : (k + 1) * rows, :] = h2_refs[k][...]
            gd[k * rows : (k + 1) * rows, :] = g_refs[k][...]
        out_acc[...] = jnp.zeros_like(out_acc)
        dh_acc[...] = jnp.zeros_like(dh_acc)
        small_acc[...] = jnp.zeros_like(small_acc)
        grads[...] = jnp.zeros_like(grads) if begin else prior_ref[...]
        lane = lax.broadcasted_iota(jnp.int32, (chunks * rows, span), 1)
        own = lane // rank == row_slot(span)
        flat_a = agu_ref[...]
        parts = [
            dot_nt(h2[...], flat_a[:, :rank].reshape(span, width)).astype(BF16),
            dot_nt(h2[...], flat_a[:, rank:].reshape(span, width)).astype(BF16),
            dot_nt(gd[...], ld_ref[...].reshape(span, width)).astype(BF16),
        ]
        for i, part in enumerate(parts):
            value = jnp.where(own, part.astype(F32) * ADAPTER_SCALE, 0.0)
            low[i] = value.astype(BF16)
            low_t[i] = value.T.astype(BF16)

    def work(first, wide):
        lanes = pl.ds(first, wide)
        w_g, w_u = gu_ref[0, :wide, :], gu_ref[1, :wide, :]
        w_d = down_ref[:wide, :]
        l_g = lift_ref[:, 0, :, :wide].reshape(span, wide)
        l_u = lift_ref[:, 1, :, :wide].reshape(span, wide)
        a_d = ad_ref[:, :, :wide].reshape(span, wide)
        gate = dot_nt(h2[...], w_g) + dot_nn(low[0], l_g)
        up = dot_nt(h2[...], w_u) + dot_nn(low[1], l_u)
        sigma = 1.0 / (1.0 + jnp.exp(-gate))
        swish = gate * sigma
        hidden = (swish * up).astype(BF16)
        d_hidden = dot_nt(gd[...], w_d) + dot_nn(low[2], a_d)
        d_gate = (d_hidden * up * (sigma + swish * (1.0 - sigma))).astype(BF16)
        d_up = (d_hidden * swish).astype(BF16)
        out_acc[...] += dot_nn(hidden, w_d)
        dh_acc[...] += dot_nn(d_gate, w_g) + dot_nn(d_up, w_u)
        small_acc[0] += dot_nt(d_gate, l_g)
        small_acc[1] += dot_nt(d_up, l_u)
        small_acc[2] += dot_nt(hidden, a_d)
        grads[0, :, lanes] += dot_nn(low_t[0], d_gate)
        grads[1, :, lanes] += dot_nn(low_t[1], d_up)
        grads[2, :, lanes] += dot_nn(low_t[2], hidden)

    rest = part_ff % tile
    if rest:
        pl.when(step < steps - 1)(lambda: work(pl.multiple_of(step * tile, tile), tile))
        pl.when(step == steps - 1)(lambda: work(part_ff - rest, rest))
    else:
        work(pl.multiple_of(step * tile, tile), tile)

    @pl.when(step == steps - 1)
    def _():
        for k in range(chunks):
            at = slice(k * rows, (k + 1) * rows)
            out_refs[k][...] = out_acc[at, :].astype(BF16)
            dh_refs[k][:, :width] = dh_acc[at, :].astype(BF16)
            picked = []
            for i in range(3):
                value = jnp.zeros((rows, rank), F32)
                for slot in range(slots):
                    mine = small_acc[i, at, slot * rank : (slot + 1) * rank]
                    value = value + jnp.where(index_ref[k] == slot, mine, 0.0)
                picked.append(value * (ADAPTER_SCALE if i < 2 else 1.0))
            picked.append(jnp.zeros((rows, 128 - 3 * rank), F32))
            dh_refs[k][:, width:] = jnp.concatenate(picked, axis=1).astype(BF16)
        if not last:
            grads_ref[...] = grads[...]
        else:
            n_ctx = grads_ref.shape[0]
            b_rows, a_rows = 2 * span // n_ctx, span // n_ctx
            odd = shift_ref[0] != 0
            tables = []
            for i in range(3):
                value = grads[i]
                if rest % 128:
                    value = jnp.where(odd, pltpu.roll(value, part_ff % 128, 1), value)
                tables.append(value.astype(BF16))
            for c in range(n_ctx):
                at = c * b_rows
                slot, half, at = at // (2 * rank), at // rank % 2, at % rank
                at += slot * rank
                grads_ref[c, :b_rows, :] = tables[half][at : at + b_rows]
                grads_ref[c, b_rows:, :] = tables[2][c * a_rows : (c + 1) * a_rows]


def mlp_call(index, shift, h2s, gs, a_gu, lift_down, w_gu, w_down, lift, a_down, prior, lanes, n_ctx):
    chunks = len(h2s)
    rows, width = h2s[0].shape
    part_ff = w_down.shape[0]
    slots, _, rank, _ = lift.shape
    span = slots * rank
    tile = 768
    steps = -(-part_ff // tile)
    priors = [] if prior is None else [prior]
    smem = pl.BlockSpec(memory_space=pltpu.SMEM)

    def whole(shape):
        return pl.BlockSpec(shape, lambda i: (0,) * len(shape))

    if n_ctx is None:
        grads_shape = jax.ShapeDtypeStruct((3, span, lanes), F32)
    else:
        grads_shape = jax.ShapeDtypeStruct((n_ctx, 3 * span // n_ctx, lanes), BF16)
    total = chunks * rows
    outs = pl.pallas_call(
        lambda *refs: mlp_kernel(
            *refs,
            chunks=chunks,
            part_ff=part_ff,
            tile=tile,
            begin=prior is None,
            last=n_ctx is not None,
        ),
        grid=(steps,),
        out_shape=(jax.ShapeDtypeStruct((rows, width), BF16),) * chunks
        + (jax.ShapeDtypeStruct((rows, width + 128), BF16),) * chunks
        + (grads_shape,),
        in_specs=[smem, smem]
        + [whole((rows, width))] * (2 * chunks)
        + [
            whole(a_gu.shape),
            whole(lift_down.shape),
            pl.BlockSpec((2, tile, width), lambda i: (0, i, 0)),
            pl.BlockSpec((tile, width), lambda i: (i, 0)),
            pl.BlockSpec((slots, 2, rank, tile), lambda i: (0, 0, 0, i)),
            pl.BlockSpec((slots, rank, tile), lambda i: (0, 0, i)),
        ]
        + [whole(table.shape) for table in priors],
        out_specs=(whole((rows, width)),) * chunks
        + (whole((rows, width + 128)),) * chunks
        + (whole(grads_shape.shape),),
        scratch_shapes=[
            pltpu.VMEM((total, width), BF16),
            pltpu.VMEM((total, width), BF16),
            pltpu.VMEM((3, total, span), BF16),
            pltpu.VMEM((3, span, total), BF16),
            pltpu.VMEM((total, width), F32),
            pltpu.VMEM((total, width), F32),
            pltpu.VMEM((3, total, span), F32),
            pltpu.VMEM((3, span, lanes), F32),
        ],
        compiler_params=pltpu.CompilerParams(vmem_limit_bytes=50 << 20),
        cost_estimate=pl.CostEstimate(
            flops=12 * total * width * part_ff,
            bytes_accessed=6 * width * part_ff,
            transcendentals=0,
        ),
    )(index, shift, *h2s, *gs, a_gu, lift_down, w_gu, w_down, lift, a_down, *priors)
    return outs[:chunks], outs[chunks : 2 * chunks], outs[-1]


def swap(value, axis, count, k):
    return lax.ppermute(value, axis, [(i, i ^ k) for i in range(count)])


def make_per_device(n_ctx, n_wa):
    def wa_exchange(value):
        return [value] + [swap(value, "wa", n_wa, k) for k in range(1, n_wa)]

    def absolute(parts, axis):
        own = lax.axis_index(axis)
        parts = list(parts)
        bit = 1
        while bit < len(parts):
            other = own & bit != 0
            parts = [jnp.where(other, parts[i ^ bit], parts[i]) for i in range(len(parts))]
            bit *= 2
        return parts

    def gather_near(value):
        return [value] + [swap(value, "ctx", n_ctx, 2 * r) for r in range(1, n_ctx // 2)]

    def gather_cores(same):
        same = jnp.stack(same)
        return same, swap(same, "ctx", n_ctx, 1)

    def per_device(
        tokens,
        cotangent,
        adapter_index,
        deal,
        w_qkv,
        b_qkv,
        w_o,
        w_gu,
        w_down,
        gain_attn,
        gain_mlp,
        a_qkv,
        b_q,
        b_kv,
        a_o,
        lift_o,
        a_gu,
        lift_gu,
        a_down,
        lift_down,
    ):
        rows, width = tokens.shape[1:]
        block = rows // 2
        rank = b_q.shape[1]
        slots = a_qkv.shape[0]
        kvd = b_kv.shape[3]
        heads = width // HD
        kvh = kvd // HD
        group = heads // kvh
        part_ff = w_down.shape[0]
        wa = lax.axis_index("wa")
        ctx = lax.axis_index("ctx")
        chosen = adapter_index[0]

        def picked(table):
            return lax.dynamic_index_in_dim(table, chosen, 0, keepdims=False)

        grad_out_bf = cotangent[0]
        x_bf = tokens[0]
        q_cols, kv_cols = width // n_ctx, 2 * kvd // n_ctx
        gain_one = gain_attn.astype(F32)[None]
        gain_two = gain_mlp.astype(F32)[None]
        s_aqkv, s_bq, s_bkv = picked(a_qkv), picked(b_q), picked(b_kv)
        s_ao, s_lo, s_agu, s_ld = picked(a_o), picked(lift_o), picked(a_gu), picked(lift_down)

        x = x_bf.astype(F32)
        h1 = (x * inverse_norm(x) * gain_one).astype(BF16)
        h1_all = lax.all_gather(h1, "ctx", axis=0, tiled=True)

        def block_of(table):
            return jnp.concatenate(
                [
                    lax.dynamic_slice_in_dim(table[:, :width], ctx * q_cols, q_cols, 1),
                    lax.dynamic_slice_in_dim(table[:, width:], ctx * kv_cols, kv_cols, 1),
                ],
                axis=1,
            )

        o_mine = lax.dynamic_slice_in_dim(w_o, ctx * q_cols, q_cols, 1).T
        mark = jnp.full((16, q_cols + kv_cols), chosen, jnp.int32).astype(BF16)
        w_mine = jnp.concatenate([block_of(w_qkv), mark], axis=0)
        depth = w_qkv.shape[0]
        o_parts = wa_exchange(o_mine)
        o_parts, w_mine = lax.optimization_barrier((o_parts, w_mine))
        w_parts = wa_exchange(w_mine)
        o_block = jnp.concatenate(absolute(o_parts, "wa"), axis=1)
        o_near = gather_near(o_block)
        b_all = jnp.concatenate(
            [
                jnp.pad(s_bq, ((0, 0), (0, 2 * kvd))),
                jnp.pad(s_bkv[0], ((0, 0), (width, kvd))),
                jnp.pad(s_bkv[1], ((0, 0), (width + kvd, 0))),
            ],
            axis=0,
        )
        key_pos = row_positions(deal, jnp.arange(n_ctx * rows, dtype=jnp.int32), block)
        key_cos, key_sin = rope_tables(key_pos)

        def own_rows(table):
            return lax.dynamic_slice_in_dim(table, ctx * rows, rows, 0)

        query_pos, cosine, sine = own_rows(key_pos)[:, None], own_rows(key_cos), own_rows(key_sin)
        key_pos = key_pos[None]
        lift_part = lax.dynamic_slice_in_dim(lift_gu, wa * part_ff, part_ff, 3)
        down_part = lax.dynamic_slice_in_dim(a_down, wa * part_ff, part_ff, 2)
        tables = (key_cos, key_sin, cosine, sine, query_pos, key_pos)
        picks = (s_aqkv, s_bq, s_bkv, s_ao, s_lo, s_agu, s_ld, lift_part, down_part)
        sides = (block_of(b_all), block_of(b_qkv[None]).astype(F32))
        w_parts, grad_sent = lax.optimization_barrier((tuple(w_parts), grad_out_bf))
        held = (h1_all, w_parts, o_near, tables, picks, sides)
        held = lax.optimization_barrier(held)
        h1_all, w_parts, o_near, tables, picks, sides = held
        key_cos, key_sin, cosine, sine, query_pos, key_pos = tables
        s_aqkv, s_bq, s_bkv, s_ao, s_lo, s_agu, s_ld, lift_part, down_part = picks
        w_block = jnp.concatenate(absolute([part[:depth] for part in w_parts], "wa"), axis=0)
        index_all = jnp.stack([part[depth, 0] for part in w_parts]).astype(jnp.int32)
        sent, u1_all = local_call(
            functools.partial(project_kernel, q_cols=q_cols),
            [
                ((n_ctx, rows, -(-(2 * kvd + q_cols) // 128) * 128), BF16),
                ((n_ctx * rows, 3 * rank), BF16),
            ],
            h1_all,
            w_block,
            s_aqkv,
            *sides,
            tight=True,
        )
        grads_all = wa_exchange(grad_sent)
        got = lax.all_to_all(sent, "ctx", 0, 0, tiled=True)
        u1_all, o_near = lax.optimization_barrier((u1_all, o_near))
        o_near = gather_cores(o_near)
        held = (got, o_near, index_all)
        got, o_near, index_all = lax.optimization_barrier(held)
        own_ctx = ctx.astype(jnp.int32)[None]
        qb, kb, vb, lse, attn, ob = local_call(
            attend_kernel,
            [
                ((rows, width), BF16),
                ((n_ctx * rows, kvd), BF16),
                ((n_ctx * rows, kvd), BF16),
                ((kvh, group * rows, 1), F32),
                ((rows, width), F32),
                ((rows, width), BF16),
            ],
            got,
            cosine,
            sine,
            key_cos,
            key_sin,
            query_pos,
            key_pos,
            tight=True,
            cost=9 * 10**9,
        )
        ob, grads_all = lax.optimization_barrier((ob, grads_all))
        uo, x1, h2 = local_call(
            output_kernel,
            [((rows, rank), BF16), ((rows, width), F32), ((rows, width), BF16)],
            ob,
            x_bf,
            *o_near,
            s_ao,
            s_lo,
            gain_two,
            tight=True,
            scalars=(own_ctx,),
            scratch=[pltpu.VMEM((n_ctx, rows, q_cols), F32)],
        )

        h2, w_block = lax.optimization_barrier((h2, w_block))
        w_blocks = lax.all_gather(w_block, "ctx", axis=0, tiled=False)

        first = wa * part_ff
        lanes = -(-max(part_ff + j * part_ff % 128 for j in range(n_wa)) // 128) * 128
        ff_grads = None
        shift = (first % 128).astype(jnp.int32)[None]
        w_gu_t = w_gu.transpose(0, 2, 1)
        h2_all = [h2] + [swap(h2, "wa", n_wa, k) for k in range(1, n_wa - 1)]
        h2_last, h2_all, grads_all = lax.optimization_barrier((h2, h2_all, grads_all))
        h2_all.append(swap(h2_last, "wa", n_wa, n_wa - 1))
        out_sent, d_h2_sent = {}, {}
        groups = [[1, 2], [3, 0]] if n_wa == 4 else [[k] for k in range(n_wa)]
        for at, group_wa in enumerate(groups):
            done = mlp_call(
                jnp.concatenate([index_all[k : k + 1] for k in group_wa]),
                shift,
                [h2 if k == 0 else h2_all[k] for k in group_wa],
                [grad_out_bf if k == 0 else grads_all[k] for k in group_wa],
                a_gu,
                lift_down,
                w_gu_t,
                w_down,
                lift_part,
                down_part,
                ff_grads,
                lanes,
                n_ctx if at == len(groups) - 1 else None,
            )
            for k, part, d_part in zip(group_wa, done[0], done[1]):
                out_sent[k], d_h2_sent[k] = part, d_part
            ff_grads = done[2]

        def wa_return(parts):
            return [parts[0]] + [swap(parts[k], "wa", n_wa, k) for k in range(1, n_wa)]

        d_h2_parts = wa_return(d_h2_sent)
        held = (tuple(out_sent[k] for k in range(n_wa)), tuple(d_h2_parts), w_blocks)
        out_sent, d_h2_parts, w_blocks = lax.optimization_barrier(held)
        ff_got = lax.all_to_all(ff_grads, "ctx", 0, 0, tiled=True)
        ff_share = jnp.sum(ff_got.astype(F32), axis=0).astype(BF16)
        count = flat_height(rank) // n_ctx
        d_x1, dl_q, sent, ud = local_call(
            functools.partial(attend_back_kernel, n_wa=n_wa, n_ctx=n_ctx),
            [
                ((rows, width), F32),
                ((rows, width), BF16),
                ((n_ctx, rows + count, 2 * kvd), BF16),
                ((rows, rank), BF16),
            ],
            *d_h2_parts,
            s_agu,
            gain_two,
            x1,
            grad_out_bf,
            h2,
            *o_near,
            s_lo,
            s_ao,
            attn,
            ob,
            uo,
            qb,
            kb,
            vb,
            lse,
            query_pos,
            key_pos,
            cosine,
            sine,
            key_cos,
            key_sin,
            u1_all,
            h1,
            h1_all,
            s_bq,
            s_bkv,
            scalars=(own_ctx,),
            scratch=[
                pltpu.VMEM((rows, width), BF16),
                pltpu.VMEM((group * rows, HD), F32),
                pltpu.VMEM((count * n_ctx, width // 3), F32),
                pltpu.VMEM((rank, 2 * kvd), F32),
                pltpu.VMEM((n_ctx * rows, 2 * rank), BF16),
                pltpu.VMEM((n_ctx, rows, q_cols), BF16),
                pltpu.VMEM(o_near[0].shape, BF16),
                pltpu.VMEM(o_near[1].shape, BF16),
                pltpu.VMEM(h1_all.shape, BF16),
                pltpu.SemaphoreType.DMA((3,)),
            ],
            far=(n_wa + 5, n_wa + 6, n_wa + 24),
        )
        got = lax.all_to_all(sent, "ctx", 0, 0, tiled=True)
        ff_wa = jnp.stack(wa_exchange(ff_share))
        out_parts = [
            lax.psum_scatter(
                jnp.concatenate(absolute(out_sent, "wa"), axis=0),
                "wa",
                scatter_dimension=0,
                tiled=True,
            )
        ]
        got, ff_wa, out_parts = lax.optimization_barrier((got, ff_wa, out_parts))
        ff_all = lax.all_gather(ff_wa, "ctx", axis=0, tiled=False)
        dl_kv, du1, share = local_call(
            collect_kernel,
            [
                ((rows, 2 * kvd), BF16),
                ((rows, 3 * rank), BF16),
                ((count, 2 * kvd), BF16),
            ],
            got,
            dl_q,
            s_bq,
            s_bkv,
        )
        share_wa = jnp.stack(wa_exchange(share))
        share_near = gather_near(share_wa)
        out, grad_x = local_call(
            functools.partial(finish_kernel, n_wa=len(out_parts)),
            [((rows, width), BF16), ((rows, width), F32)],
            *out_parts,
            x1,
            ud,
            s_ld,
            x_bf,
            gain_one,
            d_x1,
            dl_q,
            dl_kv,
            du1,
            w_blocks,
            s_aqkv,
            scratch=[pltpu.VMEM(w_blocks.shape, BF16), pltpu.SemaphoreType.DMA(())],
            far=(len(out_parts) + 9,),
            cost=7 * 10**9,
        )
        held = (share_near, out, grad_x)
        share_near, out, grad_x = lax.optimization_barrier(held)
        seq_all = jnp.stack(gather_cores(share_near))
        own_wa = wa.astype(jnp.int32)[None]
        r_bgu, r_ad = ff_results(own_wa, ff_all, slots, rank, part_ff)
        tables = {
            "a_qkv": a_qkv,
            "b_q": b_q,
            "b_kv": b_kv,
            "a_o": a_o,
            "lift_o": lift_o,
            "a_gu": a_gu,
            "lift_down": lift_down,
        }
        layout = tuple(flat_starts(rank)[name] for name in tables)
        r_aqkv, r_bq, r_bkv, r_ao, r_lo, r_agu, r_ld = seq_results(
            jnp.concatenate([own_wa, own_ctx]), index_all, seq_all, [table.shape for table in tables.values()], layout
        )
        return (
            out[None],
            grad_x[None],
            r_aqkv,
            r_bq,
            r_bkv,
            r_ao,
            r_lo,
            r_agu,
            r_bgu,
            r_ad,
            r_ld,
        )

    return per_device


def solution(mesh):
    rep = P()
    return jax.shard_map(
        make_per_device(mesh.shape["ctx"], mesh.shape["wa"]),
        mesh=mesh,
        in_specs=(
            P("wa", "ctx", None),
            P("wa", "ctx", None),
            P("wa"),
            rep,
            P("wa", None),
            rep,
            P("wa", None),
            P(None, None, "wa"),
            P("wa", None),
        )
        + (rep,) * 11,
        out_specs=(P("wa", "ctx", None), P("wa", "ctx", None)) + (rep,) * 9,
        check_vma=False,
    )
```

```python
import functools
import math

import jax
import jax.numpy as jnp
from jax import lax
from jax.experimental import pallas as pl
from jax.experimental.pallas import tpu as pltpu
from jax.sharding import PartitionSpec as P

HD = 128
EPS = 1e-06
ROPE_BASE = 1000000.0
ADAPTER_SCALE = 2.0
MASKED = -1e30
F32 = jnp.float32
BF16 = jnp.bfloat16


def dot_nn(a, b):
    return lax.dot_general(a, b, (((1,), (0,)), ((), ())), preferred_element_type=F32)


def dot_tn(a, b):
    return lax.dot_general(a, b, (((0,), (0,)), ((), ())), preferred_element_type=F32)


def dot_nt(a, b):
    return lax.dot_general(a, b, (((1,), (1,)), ((), ())), preferred_element_type=F32)


def inverse_norm(rows):
    return lax.rsqrt(jnp.mean(rows * rows, axis=-1, keepdims=True) + EPS)


def norm_pull(rows, inv, gain, grad):
    scaled = gain * grad
    return inv * scaled - rows * (inv * inv * inv) * jnp.mean(rows * scaled, axis=-1, keepdims=True)


def rope_tables(pos):
    half = HD // 2
    freq = ROPE_BASE ** (-jnp.arange(half, dtype=F32) * 2.0 / HD)
    angle = pos.astype(F32)[:, None] * freq[None, :]
    cosine, sine = jnp.cos(angle), jnp.sin(angle)
    return jnp.concatenate([cosine, cosine], axis=1), jnp.concatenate([-sine, sine], axis=1)


def row_positions(deal, rows, block):
    owner = rows // (2 * block)
    local = rows % (2 * block)
    table = jnp.arange(deal.shape[0], dtype=jnp.int32)
    pair = jnp.sum(jnp.where(owner[:, None] == table[None, :], deal[None, :], 0), axis=1)
    return jnp.where(
        local < block, pair * block + local, (2 * deal.shape[0] - 1 - pair) * block + local - block
    )


def ff_results_kernel(wa_ref, got_ref, bgu_ref, ad_ref, *, part_ff):
    n_ctx, n_wa, _, lanes = got_ref.shape
    own = wa_ref[0]
    rank = bgu_ref.shape[2]
    b_rows = bgu_ref.shape[0] * 2 * rank // n_ctx
    a_rows = ad_ref.shape[0] * rank // n_ctx
    starts = [j * part_ff // 128 * 128 for j in range(n_wa)]

    def write(read, store):
        left = None
        for j in range(n_wa):
            block = read(j).astype(F32)
            stop = starts[j + 1] - starts[j] if j + 1 < n_wa else lanes
            if left is not None:
                store(starts[j], block[:, :128] + left)
            first = 0 if left is None else 128
            store(starts[j] + first, block[:, first:stop])
            left = block[:, stop:] if stop < lanes else None

    for c in range(n_ctx):
        at = c * b_rows
        slot, half, low = at // (2 * rank), at // rank % 2, at % rank

        def put_b(lane, value):
            bgu_ref[slot, half, low : low + b_rows, lane : lane + value.shape[1]] = value

        write(lambda j: got_ref[c, own ^ j, :b_rows], put_b)
        at = c * a_rows
        slot, low = at // rank, at % rank

        def put_a(lane, value):
            ad_ref[slot, low : low + a_rows, lane : lane + value.shape[1]] = value

        write(lambda j: got_ref[c, own ^ j, b_rows:], put_a)


def ff_results(wa, got, slots, rank, part_ff):
    n_wa = got.shape[1]
    return pl.pallas_call(
        lambda *refs: ff_results_kernel(*refs, part_ff=part_ff),
        out_shape=(
            jax.ShapeDtypeStruct((slots, 2, rank, n_wa * part_ff), F32),
            jax.ShapeDtypeStruct((slots, rank, n_wa * part_ff), F32),
        ),
        in_specs=[pl.BlockSpec(memory_space=pltpu.SMEM), pl.BlockSpec(memory_space=pltpu.VMEM)],
        out_specs=(pl.BlockSpec(memory_space=pltpu.VMEM),) * 2,
        compiler_params=pltpu.CompilerParams(vmem_limit_bytes=48 << 20),
    )(wa, got)


def seq_results_kernel(own_ref, index_ref, got_ref, *out_refs, layout):
    _, n_chip, n_wa, share, third = got_ref.shape
    n_ctx = 2 * n_chip
    own, here = own_ref[0], own_ref[1]
    slots = out_refs[0].shape[0]
    for c in range(n_ctx):
        off = here ^ c
        terms = [got_ref[off & 1, off >> 1, own ^ j].astype(F32) for j in range(n_wa)]
        for slot in range(slots):
            total = jnp.zeros((share, third), F32)
            for j in range(n_wa):
                total = total + jnp.where(index_ref[own ^ j] == slot, terms[j], 0.0)
            for ref, (start, tall) in zip(out_refs, layout):
                for part in range(3 if len(ref.shape) == 3 else 1):
                    first = start + part * tall
                    low, high = max(first, c * share), min(first + tall, (c + 1) * share)
                    if low >= high:
                        continue
                    value = total[low - c * share : high - c * share]
                    at = slice(low - first, high - first)
                    if len(ref.shape) == 3:
                        ref[slot, at, part * third : (part + 1) * third] = value
                    else:
                        wide = ref.shape[3]
                        for i in range(ref.shape[1]):
                            ref[slot, i, at, :] = value[:, i * wide : (i + 1) * wide]


def seq_results(wa, index_all, got, shapes, layout):
    smem = pl.BlockSpec(memory_space=pltpu.SMEM)
    vmem = pl.BlockSpec(memory_space=pltpu.VMEM)
    return pl.pallas_call(
        lambda *refs: seq_results_kernel(*refs, layout=layout),
        out_shape=tuple(jax.ShapeDtypeStruct(shape, F32) for shape in shapes),
        in_specs=[smem, smem, vmem],
        out_specs=(vmem,) * len(shapes),
        compiler_params=pltpu.CompilerParams(vmem_limit_bytes=48 << 20),
    )(wa, index_all, got)


def local_call(kernel, out_shapes, *args, scratch=(), tight=False, cost=None, scalars=(), far=()):
    vmem = pl.BlockSpec(memory_space=pltpu.VMEM)
    smem = pl.BlockSpec(memory_space=pltpu.SMEM)
    limit = 56 << 20
    if tight:
        held = sum(arg.size * arg.dtype.itemsize for arg in args)
        held += sum(math.prod(shape) * jnp.dtype(kind).itemsize for shape, kind in out_shapes)
        limit = min(held + (20 << 20), limit)
    return pl.pallas_call(
        kernel,
        out_shape=tuple(jax.ShapeDtypeStruct(shape, kind) for shape, kind in out_shapes),
        in_specs=[smem] * len(scalars)
        + [pl.BlockSpec(memory_space=pl.ANY) if i in far else vmem for i in range(len(args))],
        out_specs=(vmem,) * len(out_shapes),
        scratch_shapes=list(scratch),
        compiler_params=pltpu.CompilerParams(vmem_limit_bytes=limit),
        cost_estimate=cost and pl.CostEstimate(flops=cost, bytes_accessed=0, transcendentals=0),
    )(*scalars, *args)


def project_kernel(h1_ref, w_ref, a_ref, b_ref, bias_ref, sent_ref, u1_ref, *, q_cols):
    n_ctx, rows, wide = sent_ref.shape
    kv_cols = w_ref.shape[1] - q_cols
    h1 = h1_ref[...]
    u1 = dot_nt(h1, a_ref[...]).astype(BF16)
    u1_ref[...] = u1
    lin = dot_nn(h1, w_ref[...]) + bias_ref[...] + ADAPTER_SCALE * dot_nn(u1, b_ref[...])
    lin = lin.astype(BF16)
    pieces = [lin[c * rows : (c + 1) * rows, q_cols:] for c in range(n_ctx)]
    kv = jnp.concatenate(pieces, axis=1)
    fill = jnp.zeros((rows, wide - n_ctx * kv_cols - q_cols), BF16)
    for c in range(n_ctx):
        sent_ref[c, :, : n_ctx * kv_cols] = kv
        own = lin[c * rows : (c + 1) * rows, :q_cols]
        sent_ref[c, :, n_ctx * kv_cols :] = jnp.concatenate([own, fill], axis=1)


def turn(value, cosine, sine):
    return value * cosine + pltpu.roll(value, HD // 2, 1) * sine


def turn_back(value, cosine, sine):
    return value * cosine + pltpu.roll(value * sine, HD // 2, 1)


def heads_stacked(table, first, group):
    return jnp.concatenate(
        [table[:, (first + j) * HD : (first + j + 1) * HD] for j in range(group)], axis=0
    )


def attend_kernel(
    got_ref, cos_ref, sin_ref, kcos_ref, ksin_ref, qpos_ref, kpos_ref, qb_ref, kb_ref, vb_ref,
    lse_ref, attn_ref, ob_ref,
):
    n_ctx = got_ref.shape[0]
    rows, width = attn_ref.shape
    kvd = kb_ref.shape[1]
    kvh, heads = kvd // HD, width // HD
    group = heads // kvh
    q_cols, kv_cols = width // n_ctx, 2 * kvd // n_ctx
    scale = 1.0 / math.sqrt(HD)
    cosine, sine = cos_ref[...], sin_ref[...]
    q_lin = jnp.concatenate(
        [got_ref[c, :, 2 * kvd : 2 * kvd + q_cols] for c in range(n_ctx)], axis=1
    )
    for h in range(heads):
        lane = slice(h * HD, (h + 1) * HD)
        qb_ref[:, lane] = turn(q_lin[:, lane].astype(F32), cosine, sine).astype(BF16)
    for g in range(n_ctx):
        at = slice(g * rows, (g + 1) * rows)
        cut = slice(g * kv_cols, (g + 1) * kv_cols)
        kv_lin = jnp.concatenate([got_ref[c, :, cut] for c in range(n_ctx)], axis=1)
        kcos, ksin = kcos_ref[at, :], ksin_ref[at, :]
        for h in range(kvh):
            lane = slice(h * HD, (h + 1) * HD)
            kb_ref[at, lane] = turn(kv_lin[:, lane].astype(F32), kcos, ksin).astype(BF16)
        vb_ref[at, :] = kv_lin[:, kvd:]
    qpos = jnp.concatenate([qpos_ref[...]] * group, axis=0)
    seen = kpos_ref[...] <= qpos
    for g in range(kvh):
        q = heads_stacked(qb_ref, g * group, group)
        s = dot_nt(q, kb_ref[:, g * HD : (g + 1) * HD]) * scale
        s = jnp.where(seen, s, MASKED)
        top = jnp.max(s, axis=1, keepdims=True)
        e = jnp.exp(s - top)
        total = jnp.sum(e, axis=1, keepdims=True)
        lse_ref[g] = top + jnp.log(total)
        pb = (e * (1.0 / total)).astype(BF16)
        o = dot_nn(pb, vb_ref[:, g * HD : (g + 1) * HD])
        for j in range(group):
            lane = slice((g * group + j) * HD, (g * group + j + 1) * HD)
            attn_ref[:, lane] = o[j * rows : (j + 1) * rows]
    ob_ref[...] = attn_ref[...].astype(BF16)


def output_kernel(
    own_ref, ob_ref, x_ref, wo_ref, wo2_ref, ao_ref, lo_ref, gain_ref, uo_ref, x1_ref, h2_ref,
    projected,
):
    n_ctx = projected.shape[0]
    ob = ob_ref[...]
    uo = dot_nt(ob, ao_ref[...]).astype(BF16)
    uo_ref[...] = uo
    for r in range(n_ctx):
        block = (wo2_ref if r % 2 else wo_ref)[r // 2]
        projected[own_ref[0] ^ r] = dot_nt(ob, block)
    blocks = [projected[c] for c in range(n_ctx)]
    x1 = x_ref[...].astype(F32) + jnp.concatenate(blocks, axis=1)
    x1 = x1 + ADAPTER_SCALE * dot_nn(uo, lo_ref[...])
    x1_ref[...] = x1
    h2_ref[...] = (x1 * inverse_norm(x1) * gain_ref[...]).astype(BF16)


def flat_starts(rank):
    starts, at = {}, 0
    names = ("a_qkv", 3), ("a_gu", 2), ("lift_down", 1), ("a_o", 1), ("lift_o", 1), ("b_q", 1)
    for name, tall in names:
        starts[name] = at, tall * rank
        at += 3 * tall * rank
    starts["b_kv"] = at, rank
    return starts


def flat_height(rank):
    start, tall = flat_starts(rank)["b_kv"]
    return start + tall


def attend_back_kernel(own_ref, *refs, n_wa, n_ctx):
    parts, refs = refs[:n_wa], refs[n_wa:]
    (
        agu_ref, gain_ref, x1_ref, g_ref, h2_ref, wo_ref, wo2_ref, lo_ref, ao_ref, attn_ref, ob_ref, uo_ref,
        qb_ref, kb_ref, vb_ref, lse_ref, qpos_ref, kpos_ref, cos_ref, sin_ref, kcos_ref, ksin_ref,
        u1all_ref, h1_ref, h1all_ref, bq_ref, bkv_ref, dx1_ref, dlq_ref, sent_ref, ud_ref, dob, dq_acc, flat, bkv_acc, du_acc, go_cut,
        wo_held, wo2_held, h1all_held, arrive,
    ) = refs
    rows, width = x1_ref.shape
    keys, kvd = kb_ref.shape
    kvh, heads = kvd // HD, width // HD
    group = heads // kvh
    rank = uo_ref.shape[1]
    scale = 1.0 / math.sqrt(HD)
    pairs = (wo_ref, wo_held), (wo2_ref, wo2_held), (h1all_ref, h1all_held)
    copies = [pltpu.make_async_copy(a, b, arrive.at[i]) for i, (a, b) in enumerate(pairs)]
    for copy in copies:
        copy.start()
    got = parts[0][...].astype(F32)
    for part in parts[1:]:
        got = got + part[...].astype(F32)
    small = got[:, width : width + 3 * rank].astype(BF16)
    dug, ud = small[:, : 2 * rank], small[:, 2 * rank :]
    ud_ref[...] = ud
    d_h2 = got[:, :width] + dot_nn(dug, agu_ref[...])
    x1 = x1_ref[...]
    g = g_ref[...]
    d_x1 = g.astype(F32) + norm_pull(x1, inverse_norm(x1), gain_ref[...], d_h2)
    dx1_ref[...] = d_x1
    go = d_x1.astype(BF16)
    duo = (ADAPTER_SCALE * dot_nt(go, lo_ref[...])).astype(BF16)
    third = width // 3
    starts = flat_starts(rank)

    def put(name, value, row=0):
        start, tall = starts[name]
        for i in range(3):
            at = start + i * tall + row
            flat[at : at + value.shape[0], :] = value[:, i * third : (i + 1) * third]

    put("a_gu", dot_tn(dug, h2_ref[...]))
    put("lift_down", ADAPTER_SCALE * dot_tn(ud, g))
    put("a_o", dot_tn(duo, ob_ref[...]))
    put("lift_o", ADAPTER_SCALE * dot_tn(uo_ref[...], go))
    d_attn = dot_nn(duo, ao_ref[...])
    cols = width // n_ctx
    for c in range(n_ctx):
        go_cut[c] = go[:, c * cols : (c + 1) * cols]
    copies[0].wait()
    copies[1].wait()
    for r in range(n_ctx):
        block = (wo2_held if r % 2 else wo_held)[r // 2]
        d_attn = d_attn + dot_nn(go_cut[own_ref[0] ^ r], block)
    dob[...] = d_attn.astype(BF16)
    qpos = jnp.concatenate([qpos_ref[...]] * group, axis=0)
    step = math.gcd(keys, 1024)
    share = step // rows
    bkv_acc[...] = jnp.zeros_like(bkv_acc)
    for kv in range(kvh):
        lane = slice(kv * HD, (kv + 1) * HD)
        v_lane = slice(kvd + kv * HD, kvd + (kv + 1) * HD)
        q = heads_stacked(qb_ref, kv * group, group)
        do = heads_stacked(dob, kv * group, group)
        o = heads_stacked(attn_ref, kv * group, group)
        delta = jnp.sum(do.astype(F32) * o, axis=1, keepdims=True)
        lse = lse_ref[kv]
        dq_acc[...] = jnp.zeros_like(dq_acc)

        def visit(turn_index):
            at = pl.ds(pl.multiple_of(turn_index * step, step), step)
            k = kb_ref[at, lane]
            s = dot_nt(q, k) * scale
            seen = kpos_ref[:, at] <= qpos
            p = jnp.exp(jnp.where(seen, s, MASKED) - lse)
            dp = dot_nt(do, vb_ref[at, lane])
            ds = (p * (dp - delta)).astype(BF16)
            dq_acc[...] += dot_nn(ds, k)
            dk = turn_back(dot_tn(ds, q) * scale, kcos_ref[at, :], ksin_ref[at, :]).astype(BF16)
            dv = dot_tn(p.astype(BF16), do).astype(BF16)
            u1 = u1all_ref[at, :]
            bkv_acc[:, lane] += dot_tn(u1[:, rank : 2 * rank], dk)
            bkv_acc[:, v_lane] += dot_tn(u1[:, 2 * rank :], dv)
            owners = pl.ds(turn_index * share, share)
            sent_ref[owners, :rows, lane] = dk.reshape(share, rows, HD)
            sent_ref[owners, :rows, v_lane] = dv.reshape(share, rows, HD)

        if keys == step:
            visit(0)
        else:
            pl.loop(0, keys // step)(visit)
        for j in range(group):
            head = slice((kv * group + j) * HD, (kv * group + j + 1) * HD)
            dq = dq_acc[j * rows : (j + 1) * rows] * scale
            dlq_ref[:, head] = turn_back(dq, cos_ref[...], sin_ref[...]).astype(BF16)
    d_lq = dlq_ref[...]
    mine = u1all_ref[pl.ds(pl.multiple_of(own_ref[0] * rows, rows), rows), :]
    put("b_q", ADAPTER_SCALE * dot_tn(mine[:, :rank], d_lq))
    start, tall = starts["b_kv"]
    flat[start : start + tall, :] = bkv_acc[...] * ADAPTER_SCALE
    for c in range(n_ctx):
        at = slice(c * rows, (c + 1) * rows)
        low = [dot_nt(sent_ref[c, :rows, :kvd], bkv_ref[0]), dot_nt(sent_ref[c, :rows, kvd:], bkv_ref[1])]
        du_acc[at, :] = (ADAPTER_SCALE * jnp.concatenate(low, axis=1)).astype(BF16)
    duq = (ADAPTER_SCALE * dot_nt(d_lq, bq_ref[...])).astype(BF16)
    put("a_qkv", dot_tn(duq, h1_ref[...]))
    copies[2].wait()
    put("a_qkv", dot_tn(du_acc[...], h1all_held[...]), rank)
    count = flat.shape[0] // n_ctx
    for c in range(n_ctx):
        share = flat[c * count : (c + 1) * count, :]
        sent_ref[c, rows:, :] = share.astype(BF16)


def collect_kernel(got_ref, dlq_ref, bq_ref, bkv_ref, dlkv_ref, du1_ref, share_ref):
    rows = dlq_ref.shape[0]
    rank = bq_ref.shape[0]
    kvd = bkv_ref.shape[2]
    total = got_ref[0].astype(F32)
    for c in range(1, got_ref.shape[0]):
        total = total + got_ref[c].astype(F32)
    dlkv = total[:rows].astype(BF16)
    dlkv_ref[...] = dlkv
    share_ref[...] = total[rows:].astype(BF16)
    du1 = [
        dot_nt(dlq_ref[...], bq_ref[...]),
        dot_nt(dlkv[:, :kvd], bkv_ref[0]),
        dot_nt(dlkv[:, kvd:], bkv_ref[1]),
    ]
    du1_ref[...] = (ADAPTER_SCALE * jnp.concatenate(du1, axis=1)).astype(BF16)


def finish_kernel(*refs, n_wa):
    parts, refs = refs[:n_wa], refs[n_wa:]
    (
        x1_ref, ud_ref, ld_ref, x_ref, gain_ref, dx1_ref, dlq_ref, dlkv_ref, du1_ref, w_ref, a_ref,
        out_ref, gx_ref, w_held, arrive,
    ) = refs
    copy = pltpu.make_async_copy(w_ref, w_held, arrive)
    copy.start()
    n_ctx = w_ref.shape[0]
    q_cols, kv_cols = dlq_ref.shape[1] // n_ctx, dlkv_ref.shape[1] // n_ctx
    out = x1_ref[...] + ADAPTER_SCALE * dot_nn(ud_ref[...], ld_ref[...])
    for part in parts:
        out = out + part[...].astype(F32)
    out_ref[...] = out.astype(BF16)
    d_h1 = dot_nn(du1_ref[...], a_ref[...])
    copy.wait()
    for c in range(n_ctx):
        block = jnp.concatenate(
            [
                dlq_ref[:, c * q_cols : (c + 1) * q_cols],
                dlkv_ref[:, c * kv_cols : (c + 1) * kv_cols],
            ],
            axis=1,
        )
        d_h1 = d_h1 + dot_nt(block, w_held[c])
    x = x_ref[...].astype(F32)
    gx_ref[...] = dx1_ref[...] + norm_pull(x, inverse_norm(x), gain_ref[...], d_h1)


def mlp_kernel(*refs, chunks, part_ff, tile, begin, last):
    refs = list(refs)
    index_ref, shift_ref = refs[:2]
    h2_refs, g_refs = refs[2 : 2 + chunks], refs[2 + chunks : 2 + 2 * chunks]
    refs = refs[2 + 2 * chunks :]
    agu_ref, ld_ref, gu_ref, down_ref, lift_ref, ad_ref = refs[:6]
    prior_ref = None if begin else refs[6]
    refs = refs[6 if begin else 7 :]
    out_refs, dh_refs = refs[:chunks], refs[chunks : 2 * chunks]
    grads_ref = refs[2 * chunks]
    h2, gd, low, low_t, out_acc, dh_acc, small_acc, grads = refs[2 * chunks + 1 :]
    rows, width = h2_refs[0].shape
    slots, _, rank, _ = lift_ref.shape
    span = slots * rank
    step, steps = pl.program_id(0), pl.num_programs(0)

    def row_slot(lanes):
        return jnp.concatenate(
            [jnp.full((rows, lanes), index_ref[k], jnp.int32) for k in range(chunks)], axis=0
        )

    @pl.when(step == 0)
    def _():
        for k in range(chunks):
            h2[k * rows : (k + 1) * rows, :] = h2_refs[k][...]
            gd[k * rows : (k + 1) * rows, :] = g_refs[k][...]
        out_acc[...] = jnp.zeros_like(out_acc)
        dh_acc[...] = jnp.zeros_like(dh_acc)
        small_acc[...] = jnp.zeros_like(small_acc)
        grads[...] = jnp.zeros_like(grads) if begin else prior_ref[...]
        lane = lax.broadcasted_iota(jnp.int32, (chunks * rows, span), 1)
        own = lane // rank == row_slot(span)
        flat_a = agu_ref[...]
        parts = [
            dot_nt(h2[...], flat_a[:, :rank].reshape(span, width)).astype(BF16),
            dot_nt(h2[...], flat_a[:, rank:].reshape(span, width)).astype(BF16),
            dot_nt(gd[...], ld_ref[...].reshape(span, width)).astype(BF16),
        ]
        for i, part in enumerate(parts):
            value = jnp.where(own, part.astype(F32) * ADAPTER_SCALE, 0.0)
            low[i] = value.astype(BF16)
            low_t[i] = value.T.astype(BF16)

    def work(first, wide):
        lanes = pl.ds(first, wide)
        w_g, w_u = gu_ref[0, :wide, :], gu_ref[1, :wide, :]
        w_d = down_ref[:wide, :]
        l_g = lift_ref[:, 0, :, :wide].reshape(span, wide)
        l_u = lift_ref[:, 1, :, :wide].reshape(span, wide)
        a_d = ad_ref[:, :, :wide].reshape(span, wide)
        gate = dot_nt(h2[...], w_g) + dot_nn(low[0], l_g)
        up = dot_nt(h2[...], w_u) + dot_nn(low[1], l_u)
        sigma = 1.0 / (1.0 + jnp.exp(-gate))
        swish = gate * sigma
        hidden = (swish * up).astype(BF16)
        d_hidden = dot_nt(gd[...], w_d) + dot_nn(low[2], a_d)
        d_gate = (d_hidden * up * (sigma + swish * (1.0 - sigma))).astype(BF16)
        d_up = (d_hidden * swish).astype(BF16)
        out_acc[...] += dot_nn(hidden, w_d)
        dh_acc[...] += dot_nn(d_gate, w_g) + dot_nn(d_up, w_u)
        small_acc[0] += dot_nt(d_gate, l_g)
        small_acc[1] += dot_nt(d_up, l_u)
        small_acc[2] += dot_nt(hidden, a_d)
        grads[0, :, lanes] += dot_nn(low_t[0], d_gate)
        grads[1, :, lanes] += dot_nn(low_t[1], d_up)
        grads[2, :, lanes] += dot_nn(low_t[2], hidden)

    rest = part_ff % tile
    if rest:
        pl.when(step < steps - 1)(lambda: work(pl.multiple_of(step * tile, tile), tile))
        pl.when(step == steps - 1)(lambda: work(part_ff - rest, rest))
    else:
        work(pl.multiple_of(step * tile, tile), tile)

    @pl.when(step == steps - 1)
    def _():
        for k in range(chunks):
            at = slice(k * rows, (k + 1) * rows)
            out_refs[k][...] = out_acc[at, :].astype(BF16)
            dh_refs[k][:, :width] = dh_acc[at, :].astype(BF16)
            picked = []
            for i in range(3):
                value = jnp.zeros((rows, rank), F32)
                for slot in range(slots):
                    mine = small_acc[i, at, slot * rank : (slot + 1) * rank]
                    value = value + jnp.where(index_ref[k] == slot, mine, 0.0)
                picked.append(value * (ADAPTER_SCALE if i < 2 else 1.0))
            picked.append(jnp.zeros((rows, 128 - 3 * rank), F32))
            dh_refs[k][:, width:] = jnp.concatenate(picked, axis=1).astype(BF16)
        if not last:
            grads_ref[...] = grads[...]
        else:
            n_ctx = grads_ref.shape[0]
            b_rows, a_rows = 2 * span // n_ctx, span // n_ctx
            odd = shift_ref[0] != 0
            tables = []
            for i in range(3):
                value = grads[i]
                if rest % 128:
                    value = jnp.where(odd, pltpu.roll(value, part_ff % 128, 1), value)
                tables.append(value.astype(BF16))
            for c in range(n_ctx):
                at = c * b_rows
                slot, half, at = at // (2 * rank), at // rank % 2, at % rank
                at += slot * rank
                grads_ref[c, :b_rows, :] = tables[half][at : at + b_rows]
                grads_ref[c, b_rows:, :] = tables[2][c * a_rows : (c + 1) * a_rows]


def mlp_call(index, shift, h2s, gs, a_gu, lift_down, w_gu, w_down, lift, a_down, prior, lanes, n_ctx):
    chunks = len(h2s)
    rows, width = h2s[0].shape
    part_ff = w_down.shape[0]
    slots, _, rank, _ = lift.shape
    span = slots * rank
    tile = 768
    steps = -(-part_ff // tile)
    priors = [] if prior is None else [prior]
    smem = pl.BlockSpec(memory_space=pltpu.SMEM)

    def whole(shape):
        return pl.BlockSpec(shape, lambda i: (0,) * len(shape))

    if n_ctx is None:
        grads_shape = jax.ShapeDtypeStruct((3, span, lanes), F32)
    else:
        grads_shape = jax.ShapeDtypeStruct((n_ctx, 3 * span // n_ctx, lanes), BF16)
    total = chunks * rows
    outs = pl.pallas_call(
        lambda *refs: mlp_kernel(
            *refs,
            chunks=chunks,
            part_ff=part_ff,
            tile=tile,
            begin=prior is None,
            last=n_ctx is not None,
        ),
        grid=(steps,),
        out_shape=(jax.ShapeDtypeStruct((rows, width), BF16),) * chunks
        + (jax.ShapeDtypeStruct((rows, width + 128), BF16),) * chunks
        + (grads_shape,),
        in_specs=[smem, smem]
        + [whole((rows, width))] * (2 * chunks)
        + [
            whole(a_gu.shape),
            whole(lift_down.shape),
            pl.BlockSpec((2, tile, width), lambda i: (0, i, 0)),
            pl.BlockSpec((tile, width), lambda i: (i, 0)),
            pl.BlockSpec((slots, 2, rank, tile), lambda i: (0, 0, 0, i)),
            pl.BlockSpec((slots, rank, tile), lambda i: (0, 0, i)),
        ]
        + [whole(table.shape) for table in priors],
        out_specs=(whole((rows, width)),) * chunks
        + (whole((rows, width + 128)),) * chunks
        + (whole(grads_shape.shape),),
        scratch_shapes=[
            pltpu.VMEM((total, width), BF16),
            pltpu.VMEM((total, width), BF16),
            pltpu.VMEM((3, total, span), BF16),
            pltpu.VMEM((3, span, total), BF16),
            pltpu.VMEM((total, width), F32),
            pltpu.VMEM((total, width), F32),
            pltpu.VMEM((3, total, span), F32),
            pltpu.VMEM((3, span, lanes), F32),
        ],
        compiler_params=pltpu.CompilerParams(vmem_limit_bytes=40 << 20),
        cost_estimate=pl.CostEstimate(
            flops=12 * total * width * part_ff,
            bytes_accessed=6 * width * part_ff,
            transcendentals=0,
        ),
    )(index, shift, *h2s, *gs, a_gu, lift_down, w_gu, w_down, lift, a_down, *priors)
    return outs[:chunks], outs[chunks : 2 * chunks], outs[-1]


def swap(value, axis, count, k):
    return lax.ppermute(value, axis, [(i, i ^ k) for i in range(count)])


def make_per_device(n_ctx, n_wa):
    def wa_exchange(value):
        return [value] + [swap(value, "wa", n_wa, k) for k in range(1, n_wa)]

    def absolute(parts, axis):
        own = lax.axis_index(axis)
        parts = list(parts)
        bit = 1
        while bit < len(parts):
            other = own & bit != 0
            parts = [jnp.where(other, parts[i ^ bit], parts[i]) for i in range(len(parts))]
            bit *= 2
        return parts

    def gather_near(value):
        return [value] + [swap(value, "ctx", n_ctx, 2 * r) for r in range(1, n_ctx // 2)]

    def gather_cores(same):
        same = jnp.stack(same)
        return same, swap(same, "ctx", n_ctx, 1)

    def per_device(
        tokens,
        cotangent,
        adapter_index,
        deal,
        w_qkv,
        b_qkv,
        w_o,
        w_gu,
        w_down,
        gain_attn,
        gain_mlp,
        a_qkv,
        b_q,
        b_kv,
        a_o,
        lift_o,
        a_gu,
        lift_gu,
        a_down,
        lift_down,
    ):
        rows, width = tokens.shape[1:]
        block = rows // 2
        rank = b_q.shape[1]
        slots = a_qkv.shape[0]
        kvd = b_kv.shape[3]
        heads = width // HD
        kvh = kvd // HD
        group = heads // kvh
        part_ff = w_down.shape[0]
        wa = lax.axis_index("wa")
        ctx = lax.axis_index("ctx")
        chosen = adapter_index[0]

        def picked(table):
            return lax.dynamic_index_in_dim(table, chosen, 0, keepdims=False)

        grad_out_bf = cotangent[0]
        x_bf = tokens[0]
        q_cols, kv_cols = width // n_ctx, 2 * kvd // n_ctx
        gain_one = gain_attn.astype(F32)[None]
        gain_two = gain_mlp.astype(F32)[None]
        s_aqkv, s_bq, s_bkv = picked(a_qkv), picked(b_q), picked(b_kv)
        s_ao, s_lo, s_agu, s_ld = picked(a_o), picked(lift_o), picked(a_gu), picked(lift_down)

        x = x_bf.astype(F32)
        h1 = (x * inverse_norm(x) * gain_one).astype(BF16)
        h1_all = lax.all_gather(h1, "ctx", axis=0, tiled=True)

        def block_of(table):
            return jnp.concatenate(
                [
                    lax.dynamic_slice_in_dim(table[:, :width], ctx * q_cols, q_cols, 1),
                    lax.dynamic_slice_in_dim(table[:, width:], ctx * kv_cols, kv_cols, 1),
                ],
                axis=1,
            )

        o_mine = lax.dynamic_slice_in_dim(w_o, ctx * q_cols, q_cols, 1).T
        mark = jnp.full((16, q_cols + kv_cols), chosen, jnp.int32).astype(BF16)
        w_mine = jnp.concatenate([block_of(w_qkv), mark], axis=0)
        depth = w_qkv.shape[0]
        o_parts = wa_exchange(o_mine)
        o_parts, w_mine = lax.optimization_barrier((o_parts, w_mine))
        w_parts = wa_exchange(w_mine)
        o_block = jnp.concatenate(absolute(o_parts, "wa"), axis=1)
        o_near = gather_near(o_block)
        b_all = jnp.concatenate(
            [
                jnp.pad(s_bq, ((0, 0), (0, 2 * kvd))),
                jnp.pad(s_bkv[0], ((0, 0), (width, kvd))),
                jnp.pad(s_bkv[1], ((0, 0), (width + kvd, 0))),
            ],
            axis=0,
        )
        key_pos = row_positions(deal, jnp.arange(n_ctx * rows, dtype=jnp.int32), block)
        key_cos, key_sin = rope_tables(key_pos)

        def own_rows(table):
            return lax.dynamic_slice_in_dim(table, ctx * rows, rows, 0)

        query_pos, cosine, sine = own_rows(key_pos)[:, None], own_rows(key_cos), own_rows(key_sin)
        key_pos = key_pos[None]
        lift_part = lax.dynamic_slice_in_dim(lift_gu, wa * part_ff, part_ff, 3)
        down_part = lax.dynamic_slice_in_dim(a_down, wa * part_ff, part_ff, 2)
        tables = (key_cos, key_sin, cosine, sine, query_pos, key_pos)
        picks = (s_aqkv, s_bq, s_bkv, s_ao, s_lo, s_agu, s_ld, lift_part, down_part)
        sides = (block_of(b_all), block_of(b_qkv[None]).astype(F32))
        w_parts, grad_sent = lax.optimization_barrier((tuple(w_parts), grad_out_bf))
        held = (h1_all, w_parts, o_near, tables, picks, sides)
        held = lax.optimization_barrier(held)
        h1_all, w_parts, o_near, tables, picks, sides = held
        key_cos, key_sin, cosine, sine, query_pos, key_pos = tables
        s_aqkv, s_bq, s_bkv, s_ao, s_lo, s_agu, s_ld, lift_part, down_part = picks
        w_block = jnp.concatenate(absolute([part[:depth] for part in w_parts], "wa"), axis=0)
        index_all = jnp.stack([part[depth, 0] for part in w_parts]).astype(jnp.int32)
        sent, u1_all = local_call(
            functools.partial(project_kernel, q_cols=q_cols),
            [
                ((n_ctx, rows, -(-(2 * kvd + q_cols) // 128) * 128), BF16),
                ((n_ctx * rows, 3 * rank), BF16),
            ],
            h1_all,
            w_block,
            s_aqkv,
            *sides,
            tight=True,
        )
        grads_all = wa_exchange(grad_sent)
        got = lax.all_to_all(sent, "ctx", 0, 0, tiled=True)
        u1_all, o_near = lax.optimization_barrier((u1_all, o_near))
        o_near = gather_cores(o_near)
        held = (got, o_near, index_all)
        got, o_near, index_all = lax.optimization_barrier(held)
        own_ctx = ctx.astype(jnp.int32)[None]
        qb, kb, vb, lse, attn, ob = local_call(
            attend_kernel,
            [
                ((rows, width), BF16),
                ((n_ctx * rows, kvd), BF16),
                ((n_ctx * rows, kvd), BF16),
                ((kvh, group * rows, 1), F32),
                ((rows, width), F32),
                ((rows, width), BF16),
            ],
            got,
            cosine,
            sine,
            key_cos,
            key_sin,
            query_pos,
            key_pos,
            tight=True,
            cost=9 * 10**9,
        )
        ob, grads_all = lax.optimization_barrier((ob, grads_all))
        uo, x1, h2 = local_call(
            output_kernel,
            [((rows, rank), BF16), ((rows, width), F32), ((rows, width), BF16)],
            ob,
            x_bf,
            *o_near,
            s_ao,
            s_lo,
            gain_two,
            tight=True,
            scalars=(own_ctx,),
            scratch=[pltpu.VMEM((n_ctx, rows, q_cols), F32)],
        )

        h2, w_block = lax.optimization_barrier((h2, w_block))
        w_blocks = lax.all_gather(w_block, "ctx", axis=0, tiled=False)

        first = wa * part_ff
        lanes = -(-max(part_ff + j * part_ff % 128 for j in range(n_wa)) // 128) * 128
        ff_grads = None
        shift = (first % 128).astype(jnp.int32)[None]
        w_gu_t = w_gu.transpose(0, 2, 1)
        h2_all = [h2] + [swap(h2, "wa", n_wa, k) for k in range(1, n_wa - 1)]
        h2_last, h2_all, grads_all = lax.optimization_barrier((h2, h2_all, grads_all))
        h2_all.append(swap(h2_last, "wa", n_wa, n_wa - 1))
        out_sent, d_h2_sent = {}, {}
        groups = [[1, 2], [3, 0]] if n_wa == 4 else [[k] for k in range(n_wa)]
        for at, group_wa in enumerate(groups):
            done = mlp_call(
                jnp.concatenate([index_all[k : k + 1] for k in group_wa]),
                shift,
                [h2 if k == 0 else h2_all[k] for k in group_wa],
                [grad_out_bf if k == 0 else grads_all[k] for k in group_wa],
                a_gu,
                lift_down,
                w_gu_t,
                w_down,
                lift_part,
                down_part,
                ff_grads,
                lanes,
                n_ctx if at == len(groups) - 1 else None,
            )
            for k, part, d_part in zip(group_wa, done[0], done[1]):
                out_sent[k], d_h2_sent[k] = part, d_part
            ff_grads = done[2]

        def wa_return(parts):
            return [parts[0]] + [swap(parts[k], "wa", n_wa, k) for k in range(1, n_wa)]

        d_h2_parts = wa_return(d_h2_sent)
        held = (tuple(out_sent[k] for k in range(n_wa)), tuple(d_h2_parts), w_blocks)
        out_sent, d_h2_parts, w_blocks = lax.optimization_barrier(held)
        ff_got = lax.all_to_all(ff_grads, "ctx", 0, 0, tiled=True)
        ff_share = jnp.sum(ff_got.astype(F32), axis=0).astype(BF16)
        count = flat_height(rank) // n_ctx
        d_x1, dl_q, sent, ud = local_call(
            functools.partial(attend_back_kernel, n_wa=n_wa, n_ctx=n_ctx),
            [
                ((rows, width), F32),
                ((rows, width), BF16),
                ((n_ctx, rows + count, 2 * kvd), BF16),
                ((rows, rank), BF16),
            ],
            *d_h2_parts,
            s_agu,
            gain_two,
            x1,
            grad_out_bf,
            h2,
            *o_near,
            s_lo,
            s_ao,
            attn,
            ob,
            uo,
            qb,
            kb,
            vb,
            lse,
            query_pos,
            key_pos,
            cosine,
            sine,
            key_cos,
            key_sin,
            u1_all,
            h1,
            h1_all,
            s_bq,
            s_bkv,
            scalars=(own_ctx,),
            scratch=[
                pltpu.VMEM((rows, width), BF16),
                pltpu.VMEM((group * rows, HD), F32),
                pltpu.VMEM((count * n_ctx, width // 3), F32),
                pltpu.VMEM((rank, 2 * kvd), F32),
                pltpu.VMEM((n_ctx * rows, 2 * rank), BF16),
                pltpu.VMEM((n_ctx, rows, q_cols), BF16),
                pltpu.VMEM(o_near[0].shape, BF16),
                pltpu.VMEM(o_near[1].shape, BF16),
                pltpu.VMEM(h1_all.shape, BF16),
                pltpu.SemaphoreType.DMA((3,)),
            ],
            far=(n_wa + 5, n_wa + 6, n_wa + 24),
        )
        got = lax.all_to_all(sent, "ctx", 0, 0, tiled=True)
        ff_wa = jnp.stack(wa_exchange(ff_share))
        out_parts = [
            lax.psum_scatter(
                jnp.concatenate(absolute(out_sent, "wa"), axis=0),
                "wa",
                scatter_dimension=0,
                tiled=True,
            )
        ]
        got, ff_wa, out_parts = lax.optimization_barrier((got, ff_wa, out_parts))
        ff_all = lax.all_gather(ff_wa, "ctx", axis=0, tiled=False)
        dl_kv, du1, share = local_call(
            collect_kernel,
            [
                ((rows, 2 * kvd), BF16),
                ((rows, 3 * rank), BF16),
                ((count, 2 * kvd), BF16),
            ],
            got,
            dl_q,
            s_bq,
            s_bkv,
        )
        share_wa = jnp.stack(wa_exchange(share))
        share_near = gather_near(share_wa)
        out, grad_x = local_call(
            functools.partial(finish_kernel, n_wa=len(out_parts)),
            [((rows, width), BF16), ((rows, width), F32)],
            *out_parts,
            x1,
            ud,
            s_ld,
            x_bf,
            gain_one,
            d_x1,
            dl_q,
            dl_kv,
            du1,
            w_blocks,
            s_aqkv,
            scratch=[pltpu.VMEM(w_blocks.shape, BF16), pltpu.SemaphoreType.DMA(())],
            far=(len(out_parts) + 9,),
            cost=7 * 10**9,
        )
        held = (share_near, out, grad_x)
        share_near, out, grad_x = lax.optimization_barrier(held)
        seq_all = jnp.stack(gather_cores(share_near))
        own_wa = wa.astype(jnp.int32)[None]
        r_bgu, r_ad = ff_results(own_wa, ff_all, slots, rank, part_ff)
        tables = {
            "a_qkv": a_qkv,
            "b_q": b_q,
            "b_kv": b_kv,
            "a_o": a_o,
            "lift_o": lift_o,
            "a_gu": a_gu,
            "lift_down": lift_down,
        }
        layout = tuple(flat_starts(rank)[name] for name in tables)
        r_aqkv, r_bq, r_bkv, r_ao, r_lo, r_agu, r_ld = seq_results(
            jnp.concatenate([own_wa, own_ctx]), index_all, seq_all, [table.shape for table in tables.values()], layout
        )
        return (
            out[None],
            grad_x[None],
            r_aqkv,
            r_bq,
            r_bkv,
            r_ao,
            r_lo,
            r_agu,
            r_bgu,
            r_ad,
            r_ld,
        )

    return per_device


def solution(mesh):
    rep = P()
    return jax.shard_map(
        make_per_device(mesh.shape["ctx"], mesh.shape["wa"]),
        mesh=mesh,
        in_specs=(
            P("wa", "ctx", None),
            P("wa", "ctx", None),
            P("wa"),
            rep,
            P("wa", None),
            rep,
            P("wa", None),
            P(None, None, "wa"),
            P("wa", None),
        )
        + (rep,) * 11,
        out_specs=(P("wa", "ctx", None), P("wa", "ctx", None)) + (rep,) * 9,
        check_vma=False,
    )
```

```python
import functools
import math

import jax
import jax.numpy as jnp
from jax import lax
from jax.experimental import pallas as pl
from jax.experimental.pallas import tpu as pltpu
from jax.sharding import PartitionSpec as P

HD = 128
EPS = 1e-06
ROPE_BASE = 1000000.0
ADAPTER_SCALE = 2.0
MASKED = -1e30
F32 = jnp.float32
BF16 = jnp.bfloat16


def dot_nn(a, b):
    return lax.dot_general(a, b, (((1,), (0,)), ((), ())), preferred_element_type=F32)


def dot_tn(a, b):
    return lax.dot_general(a, b, (((0,), (0,)), ((), ())), preferred_element_type=F32)


def dot_nt(a, b):
    return lax.dot_general(a, b, (((1,), (1,)), ((), ())), preferred_element_type=F32)


def inverse_norm(rows):
    return lax.rsqrt(jnp.mean(rows * rows, axis=-1, keepdims=True) + EPS)


def norm_pull(rows, inv, gain, grad):
    scaled = gain * grad
    return inv * scaled - rows * (inv * inv * inv) * jnp.mean(rows * scaled, axis=-1, keepdims=True)


def rope_tables(pos):
    half = HD // 2
    freq = ROPE_BASE ** (-jnp.arange(half, dtype=F32) * 2.0 / HD)
    angle = pos.astype(F32)[:, None] * freq[None, :]
    cosine, sine = jnp.cos(angle), jnp.sin(angle)
    return jnp.concatenate([cosine, cosine], axis=1), jnp.concatenate([-sine, sine], axis=1)


def row_positions(deal, rows, block):
    owner = rows // (2 * block)
    local = rows % (2 * block)
    table = jnp.arange(deal.shape[0], dtype=jnp.int32)
    pair = jnp.sum(jnp.where(owner[:, None] == table[None, :], deal[None, :], 0), axis=1)
    return jnp.where(
        local < block, pair * block + local, (2 * deal.shape[0] - 1 - pair) * block + local - block
    )


def ff_results_kernel(wa_ref, got_ref, bgu_ref, ad_ref, *, part_ff):
    n_ctx, n_wa, _, lanes = got_ref.shape
    own = wa_ref[0]
    rank = bgu_ref.shape[2]
    b_rows = bgu_ref.shape[0] * 2 * rank // n_ctx
    a_rows = ad_ref.shape[0] * rank // n_ctx
    starts = [j * part_ff // 128 * 128 for j in range(n_wa)]

    def write(read, store):
        left = None
        for j in range(n_wa):
            block = read(j).astype(F32)
            stop = starts[j + 1] - starts[j] if j + 1 < n_wa else lanes
            if left is not None:
                store(starts[j], block[:, :128] + left)
            first = 0 if left is None else 128
            store(starts[j] + first, block[:, first:stop])
            left = block[:, stop:] if stop < lanes else None

    for c in range(n_ctx):
        at = c * b_rows
        slot, half, low = at // (2 * rank), at // rank % 2, at % rank

        def put_b(lane, value):
            bgu_ref[slot, half, low : low + b_rows, lane : lane + value.shape[1]] = value

        write(lambda j: got_ref[c, own ^ j, :b_rows], put_b)
        at = c * a_rows
        slot, low = at // rank, at % rank

        def put_a(lane, value):
            ad_ref[slot, low : low + a_rows, lane : lane + value.shape[1]] = value

        write(lambda j: got_ref[c, own ^ j, b_rows:], put_a)


def ff_results(wa, got, slots, rank, part_ff):
    n_wa = got.shape[1]
    return pl.pallas_call(
        lambda *refs: ff_results_kernel(*refs, part_ff=part_ff),
        out_shape=(
            jax.ShapeDtypeStruct((slots, 2, rank, n_wa * part_ff), F32),
            jax.ShapeDtypeStruct((slots, rank, n_wa * part_ff), F32),
        ),
        in_specs=[pl.BlockSpec(memory_space=pltpu.SMEM), pl.BlockSpec(memory_space=pltpu.VMEM)],
        out_specs=(pl.BlockSpec(memory_space=pltpu.VMEM),) * 2,
        compiler_params=pltpu.CompilerParams(vmem_limit_bytes=48 << 20),
    )(wa, got)


def seq_results_kernel(own_ref, index_ref, got_ref, *out_refs, layout):
    _, n_chip, n_wa, share, third = got_ref.shape
    n_ctx = 2 * n_chip
    own, here = own_ref[0], own_ref[1]
    slots = out_refs[0].shape[0]
    for c in range(n_ctx):
        off = here ^ c
        terms = [got_ref[off & 1, off >> 1, own ^ j].astype(F32) for j in range(n_wa)]
        for slot in range(slots):
            total = jnp.zeros((share, third), F32)
            for j in range(n_wa):
                total = total + jnp.where(index_ref[own ^ j] == slot, terms[j], 0.0)
            for ref, (start, tall) in zip(out_refs, layout):
                for part in range(3 if len(ref.shape) == 3 else 1):
                    first = start + part * tall
                    low, high = max(first, c * share), min(first + tall, (c + 1) * share)
                    if low >= high:
                        continue
                    value = total[low - c * share : high - c * share]
                    at = slice(low - first, high - first)
                    if len(ref.shape) == 3:
                        ref[slot, at, part * third : (part + 1) * third] = value
                    else:
                        wide = ref.shape[3]
                        for i in range(ref.shape[1]):
                            ref[slot, i, at, :] = value[:, i * wide : (i + 1) * wide]


def seq_results(wa, index_all, got, shapes, layout):
    smem = pl.BlockSpec(memory_space=pltpu.SMEM)
    vmem = pl.BlockSpec(memory_space=pltpu.VMEM)
    return pl.pallas_call(
        lambda *refs: seq_results_kernel(*refs, layout=layout),
        out_shape=tuple(jax.ShapeDtypeStruct(shape, F32) for shape in shapes),
        in_specs=[smem, smem, vmem],
        out_specs=(vmem,) * len(shapes),
        compiler_params=pltpu.CompilerParams(vmem_limit_bytes=48 << 20),
    )(wa, index_all, got)


def local_call(kernel, out_shapes, *args, scratch=(), tight=False, cost=None, scalars=(), far=()):
    vmem = pl.BlockSpec(memory_space=pltpu.VMEM)
    smem = pl.BlockSpec(memory_space=pltpu.SMEM)
    limit = 56 << 20
    if tight:
        held = sum(arg.size * arg.dtype.itemsize for arg in args)
        held += sum(math.prod(shape) * jnp.dtype(kind).itemsize for shape, kind in out_shapes)
        limit = min(held + (20 << 20), limit)
    return pl.pallas_call(
        kernel,
        out_shape=tuple(jax.ShapeDtypeStruct(shape, kind) for shape, kind in out_shapes),
        in_specs=[smem] * len(scalars)
        + [pl.BlockSpec(memory_space=pl.ANY) if i in far else vmem for i in range(len(args))],
        out_specs=(vmem,) * len(out_shapes),
        scratch_shapes=list(scratch),
        compiler_params=pltpu.CompilerParams(vmem_limit_bytes=limit),
        cost_estimate=cost and pl.CostEstimate(flops=cost, bytes_accessed=0, transcendentals=0),
    )(*scalars, *args)


def project_kernel(h1_ref, w_ref, a_ref, b_ref, bias_ref, sent_ref, u1_ref, *, q_cols):
    n_ctx, rows, wide = sent_ref.shape
    kv_cols = w_ref.shape[1] - q_cols
    h1 = h1_ref[...]
    u1 = dot_nt(h1, a_ref[...]).astype(BF16)
    u1_ref[...] = u1
    lin = dot_nn(h1, w_ref[...]) + bias_ref[...] + ADAPTER_SCALE * dot_nn(u1, b_ref[...])
    lin = lin.astype(BF16)
    pieces = [lin[c * rows : (c + 1) * rows, q_cols:] for c in range(n_ctx)]
    kv = jnp.concatenate(pieces, axis=1)
    fill = jnp.zeros((rows, wide - n_ctx * kv_cols - q_cols), BF16)
    for c in range(n_ctx):
        sent_ref[c, :, : n_ctx * kv_cols] = kv
        own = lin[c * rows : (c + 1) * rows, :q_cols]
        sent_ref[c, :, n_ctx * kv_cols :] = jnp.concatenate([own, fill], axis=1)


def turn(value, cosine, sine):
    return value * cosine + pltpu.roll(value, HD // 2, 1) * sine


def turn_back(value, cosine, sine):
    return value * cosine + pltpu.roll(value * sine, HD // 2, 1)


def heads_stacked(table, first, group):
    return jnp.concatenate(
        [table[:, (first + j) * HD : (first + j + 1) * HD] for j in range(group)], axis=0
    )


def attend_kernel(
    got_ref, cos_ref, sin_ref, kcos_ref, ksin_ref, qpos_ref, kpos_ref, qb_ref, kb_ref, vb_ref,
    lse_ref, attn_ref, ob_ref,
):
    n_ctx = got_ref.shape[0]
    rows, width = attn_ref.shape
    kvd = kb_ref.shape[1]
    kvh, heads = kvd // HD, width // HD
    group = heads // kvh
    q_cols, kv_cols = width // n_ctx, 2 * kvd // n_ctx
    scale = 1.0 / math.sqrt(HD)
    cosine, sine = cos_ref[...], sin_ref[...]
    q_lin = jnp.concatenate(
        [got_ref[c, :, 2 * kvd : 2 * kvd + q_cols] for c in range(n_ctx)], axis=1
    )
    for h in range(heads):
        lane = slice(h * HD, (h + 1) * HD)
        qb_ref[:, lane] = turn(q_lin[:, lane].astype(F32), cosine, sine).astype(BF16)
    for g in range(n_ctx):
        at = slice(g * rows, (g + 1) * rows)
        cut = slice(g * kv_cols, (g + 1) * kv_cols)
        kv_lin = jnp.concatenate([got_ref[c, :, cut] for c in range(n_ctx)], axis=1)
        kcos, ksin = kcos_ref[at, :], ksin_ref[at, :]
        for h in range(kvh):
            lane = slice(h * HD, (h + 1) * HD)
            kb_ref[at, lane] = turn(kv_lin[:, lane].astype(F32), kcos, ksin).astype(BF16)
        vb_ref[at, :] = kv_lin[:, kvd:]
    qpos = jnp.concatenate([qpos_ref[...]] * group, axis=0)
    seen = kpos_ref[...] <= qpos
    for g in range(kvh):
        q = heads_stacked(qb_ref, g * group, group)
        s = dot_nt(q, kb_ref[:, g * HD : (g + 1) * HD]) * scale
        s = jnp.where(seen, s, MASKED)
        top = jnp.max(s, axis=1, keepdims=True)
        e = jnp.exp(s - top)
        total = jnp.sum(e, axis=1, keepdims=True)
        lse_ref[g] = top + jnp.log(total)
        pb = (e * (1.0 / total)).astype(BF16)
        o = dot_nn(pb, vb_ref[:, g * HD : (g + 1) * HD])
        for j in range(group):
            lane = slice((g * group + j) * HD, (g * group + j + 1) * HD)
            attn_ref[:, lane] = o[j * rows : (j + 1) * rows]
    ob_ref[...] = attn_ref[...].astype(BF16)


def output_kernel(
    own_ref, ob_ref, x_ref, wo_ref, wo2_ref, ao_ref, lo_ref, gain_ref, uo_ref, x1_ref, h2_ref,
    projected,
):
    n_ctx = projected.shape[0]
    ob = ob_ref[...]
    uo = dot_nt(ob, ao_ref[...]).astype(BF16)
    uo_ref[...] = uo
    for r in range(n_ctx):
        block = (wo2_ref if r % 2 else wo_ref)[r // 2]
        projected[own_ref[0] ^ r] = dot_nt(ob, block)
    blocks = [projected[c] for c in range(n_ctx)]
    x1 = x_ref[...].astype(F32) + jnp.concatenate(blocks, axis=1)
    x1 = x1 + ADAPTER_SCALE * dot_nn(uo, lo_ref[...])
    x1_ref[...] = x1
    h2_ref[...] = (x1 * inverse_norm(x1) * gain_ref[...]).astype(BF16)


def flat_starts(rank):
    starts, at = {}, 0
    names = ("a_qkv", 3), ("a_gu", 2), ("lift_down", 1), ("a_o", 1), ("lift_o", 1), ("b_q", 1)
    for name, tall in names:
        starts[name] = at, tall * rank
        at += 3 * tall * rank
    starts["b_kv"] = at, rank
    return starts


def flat_height(rank):
    start, tall = flat_starts(rank)["b_kv"]
    return start + tall


def attend_back_kernel(own_ref, *refs, n_wa, n_ctx):
    parts, refs = refs[:n_wa], refs[n_wa:]
    (
        agu_ref, gain_ref, x1_ref, g_ref, h2_ref, wo_ref, wo2_ref, lo_ref, ao_ref, attn_ref, ob_ref, uo_ref,
        qb_ref, kb_ref, vb_ref, lse_ref, qpos_ref, kpos_ref, cos_ref, sin_ref, kcos_ref, ksin_ref,
        u1all_ref, h1_ref, h1all_ref, bq_ref, bkv_ref, dx1_ref, dlq_ref, sent_ref, ud_ref, dob, dq_acc, flat, bkv_acc, du_acc, go_cut,
        wo_held, wo2_held, h1all_held, arrive,
    ) = refs
    rows, width = x1_ref.shape
    keys, kvd = kb_ref.shape
    kvh, heads = kvd // HD, width // HD
    group = heads // kvh
    rank = uo_ref.shape[1]
    scale = 1.0 / math.sqrt(HD)
    pairs = (wo_ref, wo_held), (wo2_ref, wo2_held), (h1all_ref, h1all_held)
    copies = [pltpu.make_async_copy(a, b, arrive.at[i]) for i, (a, b) in enumerate(pairs)]
    for copy in copies:
        copy.start()
    got = parts[0][...].astype(F32)
    for part in parts[1:]:
        got = got + part[...].astype(F32)
    small = got[:, width : width + 3 * rank].astype(BF16)
    dug, ud = small[:, : 2 * rank], small[:, 2 * rank :]
    ud_ref[...] = ud
    d_h2 = got[:, :width] + dot_nn(dug, agu_ref[...])
    x1 = x1_ref[...]
    g = g_ref[...]
    d_x1 = g.astype(F32) + norm_pull(x1, inverse_norm(x1), gain_ref[...], d_h2)
    dx1_ref[...] = d_x1
    go = d_x1.astype(BF16)
    duo = (ADAPTER_SCALE * dot_nt(go, lo_ref[...])).astype(BF16)
    third = width // 3
    starts = flat_starts(rank)

    def put(name, value, row=0):
        start, tall = starts[name]
        for i in range(3):
            at = start + i * tall + row
            flat[at : at + value.shape[0], :] = value[:, i * third : (i + 1) * third]

    put("a_gu", dot_tn(dug, h2_ref[...]))
    put("lift_down", ADAPTER_SCALE * dot_tn(ud, g))
    put("a_o", dot_tn(duo, ob_ref[...]))
    put("lift_o", ADAPTER_SCALE * dot_tn(uo_ref[...], go))
    d_attn = dot_nn(duo, ao_ref[...])
    cols = width // n_ctx
    for c in range(n_ctx):
        go_cut[c] = go[:, c * cols : (c + 1) * cols]
    copies[0].wait()
    copies[1].wait()
    for r in range(n_ctx):
        block = (wo2_held if r % 2 else wo_held)[r // 2]
        d_attn = d_attn + dot_nn(go_cut[own_ref[0] ^ r], block)
    dob[...] = d_attn.astype(BF16)
    qpos = jnp.concatenate([qpos_ref[...]] * group, axis=0)
    step = math.gcd(keys, 1024)
    share = step // rows
    bkv_acc[...] = jnp.zeros_like(bkv_acc)
    for kv in range(kvh):
        lane = slice(kv * HD, (kv + 1) * HD)
        v_lane = slice(kvd + kv * HD, kvd + (kv + 1) * HD)
        q = heads_stacked(qb_ref, kv * group, group)
        do = heads_stacked(dob, kv * group, group)
        o = heads_stacked(attn_ref, kv * group, group)
        delta = jnp.sum(do.astype(F32) * o, axis=1, keepdims=True)
        lse = lse_ref[kv]
        dq_acc[...] = jnp.zeros_like(dq_acc)

        def visit(turn_index):
            at = pl.ds(pl.multiple_of(turn_index * step, step), step)
            k = kb_ref[at, lane]
            s = dot_nt(q, k) * scale
            seen = kpos_ref[:, at] <= qpos
            p = jnp.exp(jnp.where(seen, s, MASKED) - lse)
            dp = dot_nt(do, vb_ref[at, lane])
            ds = (p * (dp - delta)).astype(BF16)
            dq_acc[...] += dot_nn(ds, k)
            dk = turn_back(dot_tn(ds, q) * scale, kcos_ref[at, :], ksin_ref[at, :]).astype(BF16)
            dv = dot_tn(p.astype(BF16), do).astype(BF16)
            u1 = u1all_ref[at, :]
            bkv_acc[:, lane] += dot_tn(u1[:, rank : 2 * rank], dk)
            bkv_acc[:, v_lane] += dot_tn(u1[:, 2 * rank :], dv)
            owners = pl.ds(turn_index * share, share)
            sent_ref[owners, :rows, lane] = dk.reshape(share, rows, HD)
            sent_ref[owners, :rows, v_lane] = dv.reshape(share, rows, HD)

        if keys == step:
            visit(0)
        else:
            pl.loop(0, keys // step)(visit)
        for j in range(group):
            head = slice((kv * group + j) * HD, (kv * group + j + 1) * HD)
            dq = dq_acc[j * rows : (j + 1) * rows] * scale
            dlq_ref[:, head] = turn_back(dq, cos_ref[...], sin_ref[...]).astype(BF16)
    d_lq = dlq_ref[...]
    mine = u1all_ref[pl.ds(pl.multiple_of(own_ref[0] * rows, rows), rows), :]
    put("b_q", ADAPTER_SCALE * dot_tn(mine[:, :rank], d_lq))
    start, tall = starts["b_kv"]
    flat[start : start + tall, :] = bkv_acc[...] * ADAPTER_SCALE
    for c in range(n_ctx):
        at = slice(c * rows, (c + 1) * rows)
        low = [dot_nt(sent_ref[c, :rows, :kvd], bkv_ref[0]), dot_nt(sent_ref[c, :rows, kvd:], bkv_ref[1])]
        du_acc[at, :] = (ADAPTER_SCALE * jnp.concatenate(low, axis=1)).astype(BF16)
    duq = (ADAPTER_SCALE * dot_nt(d_lq, bq_ref[...])).astype(BF16)
    put("a_qkv", dot_tn(duq, h1_ref[...]))
    copies[2].wait()
    put("a_qkv", dot_tn(du_acc[...], h1all_held[...]), rank)
    count = flat.shape[0] // n_ctx
    for c in range(n_ctx):
        share = flat[c * count : (c + 1) * count, :]
        sent_ref[c, rows:, :] = share.astype(BF16)


def collect_kernel(got_ref, dlq_ref, bq_ref, bkv_ref, dlkv_ref, du1_ref, share_ref):
    rows = dlq_ref.shape[0]
    rank = bq_ref.shape[0]
    kvd = bkv_ref.shape[2]
    total = got_ref[0].astype(F32)
    for c in range(1, got_ref.shape[0]):
        total = total + got_ref[c].astype(F32)
    dlkv = total[:rows].astype(BF16)
    dlkv_ref[...] = dlkv
    share_ref[...] = total[rows:].astype(BF16)
    du1 = [
        dot_nt(dlq_ref[...], bq_ref[...]),
        dot_nt(dlkv[:, :kvd], bkv_ref[0]),
        dot_nt(dlkv[:, kvd:], bkv_ref[1]),
    ]
    du1_ref[...] = (ADAPTER_SCALE * jnp.concatenate(du1, axis=1)).astype(BF16)


def finish_kernel(*refs, n_wa):
    parts, refs = refs[:n_wa], refs[n_wa:]
    (
        x1_ref, ud_ref, ld_ref, x_ref, gain_ref, dx1_ref, dlq_ref, dlkv_ref, du1_ref, w_ref, a_ref,
        out_ref, gx_ref, w_held, arrive,
    ) = refs
    copy = pltpu.make_async_copy(w_ref, w_held, arrive)
    copy.start()
    n_ctx = w_ref.shape[0]
    q_cols, kv_cols = dlq_ref.shape[1] // n_ctx, dlkv_ref.shape[1] // n_ctx
    out = x1_ref[...] + ADAPTER_SCALE * dot_nn(ud_ref[...], ld_ref[...])
    for part in parts:
        out = out + part[...].astype(F32)
    out_ref[...] = out.astype(BF16)
    d_h1 = dot_nn(du1_ref[...], a_ref[...])
    copy.wait()
    for c in range(n_ctx):
        block = jnp.concatenate(
            [
                dlq_ref[:, c * q_cols : (c + 1) * q_cols],
                dlkv_ref[:, c * kv_cols : (c + 1) * kv_cols],
            ],
            axis=1,
        )
        d_h1 = d_h1 + dot_nt(block, w_held[c])
    x = x_ref[...].astype(F32)
    gx_ref[...] = dx1_ref[...] + norm_pull(x, inverse_norm(x), gain_ref[...], d_h1)


def mlp_kernel(*refs, chunks, part_ff, tile, begin, last):
    refs = list(refs)
    index_ref, shift_ref = refs[:2]
    h2_refs, g_refs = refs[2 : 2 + chunks], refs[2 + chunks : 2 + 2 * chunks]
    refs = refs[2 + 2 * chunks :]
    agu_ref, ld_ref, gu_ref, down_ref, lift_ref, ad_ref = refs[:6]
    prior_ref = None if begin else refs[6]
    refs = refs[6 if begin else 7 :]
    out_refs, dh_refs = refs[:chunks], refs[chunks : 2 * chunks]
    grads_ref = refs[2 * chunks]
    h2, gd, low, low_t, out_acc, dh_acc, small_acc, grads = refs[2 * chunks + 1 :]
    rows, width = h2_refs[0].shape
    slots, _, rank, _ = lift_ref.shape
    span = slots * rank
    step, steps = pl.program_id(0), pl.num_programs(0)

    def row_slot(lanes):
        return jnp.concatenate(
            [jnp.full((rows, lanes), index_ref[k], jnp.int32) for k in range(chunks)], axis=0
        )

    @pl.when(step == 0)
    def _():
        for k in range(chunks):
            h2[k * rows : (k + 1) * rows, :] = h2_refs[k][...]
            gd[k * rows : (k + 1) * rows, :] = g_refs[k][...]
        out_acc[...] = jnp.zeros_like(out_acc)
        dh_acc[...] = jnp.zeros_like(dh_acc)
        small_acc[...] = jnp.zeros_like(small_acc)
        grads[...] = jnp.zeros_like(grads) if begin else prior_ref[...]
        lane = lax.broadcasted_iota(jnp.int32, (chunks * rows, span), 1)
        own = lane // rank == row_slot(span)
        flat_a = agu_ref[...]
        parts = [
            dot_nt(h2[...], flat_a[:, :rank].reshape(span, width)).astype(BF16),
            dot_nt(h2[...], flat_a[:, rank:].reshape(span, width)).astype(BF16),
            dot_nt(gd[...], ld_ref[...].reshape(span, width)).astype(BF16),
        ]
        for i, part in enumerate(parts):
            value = jnp.where(own, part.astype(F32) * ADAPTER_SCALE, 0.0)
            low[i] = value.astype(BF16)
            low_t[i] = value.T.astype(BF16)

    def work(first, wide):
        lanes = pl.ds(first, wide)
        w_g, w_u = gu_ref[0, :wide, :], gu_ref[1, :wide, :]
        w_d = down_ref[:wide, :]
        l_g = lift_ref[:, 0, :, :wide].reshape(span, wide)
        l_u = lift_ref[:, 1, :, :wide].reshape(span, wide)
        a_d = ad_ref[:, :, :wide].reshape(span, wide)
        gate = dot_nt(h2[...], w_g) + dot_nn(low[0], l_g)
        up = dot_nt(h2[...], w_u) + dot_nn(low[1], l_u)
        sigma = 1.0 / (1.0 + jnp.exp(-gate))
        swish = gate * sigma
        hidden = (swish * up).astype(BF16)
        d_hidden = dot_nt(gd[...], w_d) + dot_nn(low[2], a_d)
        d_gate = (d_hidden * up * (sigma + swish * (1.0 - sigma))).astype(BF16)
        d_up = (d_hidden * swish).astype(BF16)
        out_acc[...] += dot_nn(hidden, w_d)
        dh_acc[...] += dot_nn(d_gate, w_g) + dot_nn(d_up, w_u)
        small_acc[0] += dot_nt(d_gate, l_g)
        small_acc[1] += dot_nt(d_up, l_u)
        small_acc[2] += dot_nt(hidden, a_d)
        grads[0, :, lanes] += dot_nn(low_t[0], d_gate)
        grads[1, :, lanes] += dot_nn(low_t[1], d_up)
        grads[2, :, lanes] += dot_nn(low_t[2], hidden)

    rest = part_ff % tile
    if rest:
        pl.when(step < steps - 1)(lambda: work(pl.multiple_of(step * tile, tile), tile))
        pl.when(step == steps - 1)(lambda: work(part_ff - rest, rest))
    else:
        work(pl.multiple_of(step * tile, tile), tile)

    @pl.when(step == steps - 1)
    def _():
        for k in range(chunks):
            at = slice(k * rows, (k + 1) * rows)
            out_refs[k][...] = out_acc[at, :].astype(BF16)
            dh_refs[k][:, :width] = dh_acc[at, :].astype(BF16)
            picked = []
            for i in range(3):
                value = jnp.zeros((rows, rank), F32)
                for slot in range(slots):
                    mine = small_acc[i, at, slot * rank : (slot + 1) * rank]
                    value = value + jnp.where(index_ref[k] == slot, mine, 0.0)
                picked.append(value * (ADAPTER_SCALE if i < 2 else 1.0))
            picked.append(jnp.zeros((rows, 128 - 3 * rank), F32))
            dh_refs[k][:, width:] = jnp.concatenate(picked, axis=1).astype(BF16)
        if not last:
            grads_ref[...] = grads[...]
        else:
            n_ctx = grads_ref.shape[0]
            b_rows, a_rows = 2 * span // n_ctx, span // n_ctx
            odd = shift_ref[0] != 0
            tables = []
            for i in range(3):
                value = grads[i]
                if rest % 128:
                    value = jnp.where(odd, pltpu.roll(value, part_ff % 128, 1), value)
                tables.append(value.astype(BF16))
            for c in range(n_ctx):
                at = c * b_rows
                slot, half, at = at // (2 * rank), at // rank % 2, at % rank
                at += slot * rank
                grads_ref[c, :b_rows, :] = tables[half][at : at + b_rows]
                grads_ref[c, b_rows:, :] = tables[2][c * a_rows : (c + 1) * a_rows]


def mlp_call(index, shift, h2s, gs, a_gu, lift_down, w_gu, w_down, lift, a_down, prior, lanes, n_ctx):
    chunks = len(h2s)
    rows, width = h2s[0].shape
    part_ff = w_down.shape[0]
    slots, _, rank, _ = lift.shape
    span = slots * rank
    tile = 768
    steps = -(-part_ff // tile)
    priors = [] if prior is None else [prior]
    smem = pl.BlockSpec(memory_space=pltpu.SMEM)

    def whole(shape):
        return pl.BlockSpec(shape, lambda i: (0,) * len(shape))

    if n_ctx is None:
        grads_shape = jax.ShapeDtypeStruct((3, span, lanes), F32)
    else:
        grads_shape = jax.ShapeDtypeStruct((n_ctx, 3 * span // n_ctx, lanes), BF16)
    total = chunks * rows
    outs = pl.pallas_call(
        lambda *refs: mlp_kernel(
            *refs,
            chunks=chunks,
            part_ff=part_ff,
            tile=tile,
            begin=prior is None,
            last=n_ctx is not None,
        ),
        grid=(steps,),
        out_shape=(jax.ShapeDtypeStruct((rows, width), BF16),) * chunks
        + (jax.ShapeDtypeStruct((rows, width + 128), BF16),) * chunks
        + (grads_shape,),
        in_specs=[smem, smem]
        + [whole((rows, width))] * (2 * chunks)
        + [
            whole(a_gu.shape),
            whole(lift_down.shape),
            pl.BlockSpec((2, tile, width), lambda i: (0, i, 0)),
            pl.BlockSpec((tile, width), lambda i: (i, 0)),
            pl.BlockSpec((slots, 2, rank, tile), lambda i: (0, 0, 0, i)),
            pl.BlockSpec((slots, rank, tile), lambda i: (0, 0, i)),
        ]
        + [whole(table.shape) for table in priors],
        out_specs=(whole((rows, width)),) * chunks
        + (whole((rows, width + 128)),) * chunks
        + (whole(grads_shape.shape),),
        scratch_shapes=[
            pltpu.VMEM((total, width), BF16),
            pltpu.VMEM((total, width), BF16),
            pltpu.VMEM((3, total, span), BF16),
            pltpu.VMEM((3, span, total), BF16),
            pltpu.VMEM((total, width), F32),
            pltpu.VMEM((total, width), F32),
            pltpu.VMEM((3, total, span), F32),
            pltpu.VMEM((3, span, lanes), F32),
        ],
        compiler_params=pltpu.CompilerParams(vmem_limit_bytes=58 << 20),
        cost_estimate=pl.CostEstimate(
            flops=12 * total * width * part_ff,
            bytes_accessed=6 * width * part_ff,
            transcendentals=0,
        ),
    )(index, shift, *h2s, *gs, a_gu, lift_down, w_gu, w_down, lift, a_down, *priors)
    return outs[:chunks], outs[chunks : 2 * chunks], outs[-1]


def swap(value, axis, count, k):
    return lax.ppermute(value, axis, [(i, i ^ k) for i in range(count)])


def make_per_device(n_ctx, n_wa):
    def wa_exchange(value):
        return [value] + [swap(value, "wa", n_wa, k) for k in range(1, n_wa)]

    def absolute(parts, axis):
        own = lax.axis_index(axis)
        parts = list(parts)
        bit = 1
        while bit < len(parts):
            other = own & bit != 0
            parts = [jnp.where(other, parts[i ^ bit], parts[i]) for i in range(len(parts))]
            bit *= 2
        return parts

    def gather_near(value):
        return [value] + [swap(value, "ctx", n_ctx, 2 * r) for r in range(1, n_ctx // 2)]

    def gather_cores(same):
        same = jnp.stack(same)
        return same, swap(same, "ctx", n_ctx, 1)

    def per_device(
        tokens,
        cotangent,
        adapter_index,
        deal,
        w_qkv,
        b_qkv,
        w_o,
        w_gu,
        w_down,
        gain_attn,
        gain_mlp,
        a_qkv,
        b_q,
        b_kv,
        a_o,
        lift_o,
        a_gu,
        lift_gu,
        a_down,
        lift_down,
    ):
        rows, width = tokens.shape[1:]
        block = rows // 2
        rank = b_q.shape[1]
        slots = a_qkv.shape[0]
        kvd = b_kv.shape[3]
        heads = width // HD
        kvh = kvd // HD
        group = heads // kvh
        part_ff = w_down.shape[0]
        wa = lax.axis_index("wa")
        ctx = lax.axis_index("ctx")
        chosen = adapter_index[0]

        def picked(table):
            return lax.dynamic_index_in_dim(table, chosen, 0, keepdims=False)

        grad_out_bf = cotangent[0]
        x_bf = tokens[0]
        q_cols, kv_cols = width // n_ctx, 2 * kvd // n_ctx
        gain_one = gain_attn.astype(F32)[None]
        gain_two = gain_mlp.astype(F32)[None]
        s_aqkv, s_bq, s_bkv = picked(a_qkv), picked(b_q), picked(b_kv)
        s_ao, s_lo, s_agu, s_ld = picked(a_o), picked(lift_o), picked(a_gu), picked(lift_down)

        x = x_bf.astype(F32)
        h1 = (x * inverse_norm(x) * gain_one).astype(BF16)
        h1_all = lax.all_gather(h1, "ctx", axis=0, tiled=True)

        def block_of(table):
            return jnp.concatenate(
                [
                    lax.dynamic_slice_in_dim(table[:, :width], ctx * q_cols, q_cols, 1),
                    lax.dynamic_slice_in_dim(table[:, width:], ctx * kv_cols, kv_cols, 1),
                ],
                axis=1,
            )

        o_mine = lax.dynamic_slice_in_dim(w_o, ctx * q_cols, q_cols, 1).T
        mark = jnp.full((16, q_cols + kv_cols), chosen, jnp.int32).astype(BF16)
        w_mine = jnp.concatenate([block_of(w_qkv), mark], axis=0)
        depth = w_qkv.shape[0]
        o_parts = wa_exchange(o_mine)
        o_parts, w_mine = lax.optimization_barrier((o_parts, w_mine))
        w_parts = wa_exchange(w_mine)
        o_block = jnp.concatenate(absolute(o_parts, "wa"), axis=1)
        o_near = gather_near(o_block)
        b_all = jnp.concatenate(
            [
                jnp.pad(s_bq, ((0, 0), (0, 2 * kvd))),
                jnp.pad(s_bkv[0], ((0, 0), (width, kvd))),
                jnp.pad(s_bkv[1], ((0, 0), (width + kvd, 0))),
            ],
            axis=0,
        )
        key_pos = row_positions(deal, jnp.arange(n_ctx * rows, dtype=jnp.int32), block)
        key_cos, key_sin = rope_tables(key_pos)

        def own_rows(table):
            return lax.dynamic_slice_in_dim(table, ctx * rows, rows, 0)

        query_pos, cosine, sine = own_rows(key_pos)[:, None], own_rows(key_cos), own_rows(key_sin)
        key_pos = key_pos[None]
        lift_part = lax.dynamic_slice_in_dim(lift_gu, wa * part_ff, part_ff, 3)
        down_part = lax.dynamic_slice_in_dim(a_down, wa * part_ff, part_ff, 2)
        tables = (key_cos, key_sin, cosine, sine, query_pos, key_pos)
        picks = (s_aqkv, s_bq, s_bkv, s_ao, s_lo, s_agu, s_ld, lift_part, down_part)
        sides = (block_of(b_all), block_of(b_qkv[None]).astype(F32))
        w_parts, grad_sent = lax.optimization_barrier((tuple(w_parts), grad_out_bf))
        held = (h1_all, w_parts, o_near, tables, picks, sides)
        held = lax.optimization_barrier(held)
        h1_all, w_parts, o_near, tables, picks, sides = held
        key_cos, key_sin, cosine, sine, query_pos, key_pos = tables
        s_aqkv, s_bq, s_bkv, s_ao, s_lo, s_agu, s_ld, lift_part, down_part = picks
        w_block = jnp.concatenate(absolute([part[:depth] for part in w_parts], "wa"), axis=0)
        index_all = jnp.stack([part[depth, 0] for part in w_parts]).astype(jnp.int32)
        sent, u1_all = local_call(
            functools.partial(project_kernel, q_cols=q_cols),
            [
                ((n_ctx, rows, -(-(2 * kvd + q_cols) // 128) * 128), BF16),
                ((n_ctx * rows, 3 * rank), BF16),
            ],
            h1_all,
            w_block,
            s_aqkv,
            *sides,
            tight=True,
        )
        grads_all = wa_exchange(grad_sent)
        got = lax.all_to_all(sent, "ctx", 0, 0, tiled=True)
        u1_all, o_near = lax.optimization_barrier((u1_all, o_near))
        o_near = gather_cores(o_near)
        held = (got, o_near, index_all)
        got, o_near, index_all = lax.optimization_barrier(held)
        own_ctx = ctx.astype(jnp.int32)[None]
        qb, kb, vb, lse, attn, ob = local_call(
            attend_kernel,
            [
                ((rows, width), BF16),
                ((n_ctx * rows, kvd), BF16),
                ((n_ctx * rows, kvd), BF16),
                ((kvh, group * rows, 1), F32),
                ((rows, width), F32),
                ((rows, width), BF16),
            ],
            got,
            cosine,
            sine,
            key_cos,
            key_sin,
            query_pos,
            key_pos,
            tight=True,
            cost=9 * 10**9,
        )
        ob, grads_all = lax.optimization_barrier((ob, grads_all))
        uo, x1, h2 = local_call(
            output_kernel,
            [((rows, rank), BF16), ((rows, width), F32), ((rows, width), BF16)],
            ob,
            x_bf,
            *o_near,
            s_ao,
            s_lo,
            gain_two,
            tight=True,
            scalars=(own_ctx,),
            scratch=[pltpu.VMEM((n_ctx, rows, q_cols), F32)],
        )

        h2, w_block = lax.optimization_barrier((h2, w_block))
        w_blocks = lax.all_gather(w_block, "ctx", axis=0, tiled=False)

        first = wa * part_ff
        lanes = -(-max(part_ff + j * part_ff % 128 for j in range(n_wa)) // 128) * 128
        ff_grads = None
        shift = (first % 128).astype(jnp.int32)[None]
        w_gu_t = w_gu.transpose(0, 2, 1)
        h2_all = [h2] + [swap(h2, "wa", n_wa, k) for k in range(1, n_wa - 1)]
        h2_last, h2_all, grads_all = lax.optimization_barrier((h2, h2_all, grads_all))
        h2_all.append(swap(h2_last, "wa", n_wa, n_wa - 1))
        out_sent, d_h2_sent = {}, {}
        groups = [[1, 2], [3, 0]] if n_wa == 4 else [[k] for k in range(n_wa)]
        for at, group_wa in enumerate(groups):
            done = mlp_call(
                jnp.concatenate([index_all[k : k + 1] for k in group_wa]),
                shift,
                [h2 if k == 0 else h2_all[k] for k in group_wa],
                [grad_out_bf if k == 0 else grads_all[k] for k in group_wa],
                a_gu,
                lift_down,
                w_gu_t,
                w_down,
                lift_part,
                down_part,
                ff_grads,
                lanes,
                n_ctx if at == len(groups) - 1 else None,
            )
            for k, part, d_part in zip(group_wa, done[0], done[1]):
                out_sent[k], d_h2_sent[k] = part, d_part
            ff_grads = done[2]

        def wa_return(parts):
            return [parts[0]] + [swap(parts[k], "wa", n_wa, k) for k in range(1, n_wa)]

        d_h2_parts = wa_return(d_h2_sent)
        held = (tuple(out_sent[k] for k in range(n_wa)), tuple(d_h2_parts), w_blocks)
        out_sent, d_h2_parts, w_blocks = lax.optimization_barrier(held)
        ff_got = lax.all_to_all(ff_grads, "ctx", 0, 0, tiled=True)
        ff_share = jnp.sum(ff_got.astype(F32), axis=0).astype(BF16)
        count = flat_height(rank) // n_ctx
        d_x1, dl_q, sent, ud = local_call(
            functools.partial(attend_back_kernel, n_wa=n_wa, n_ctx=n_ctx),
            [
                ((rows, width), F32),
                ((rows, width), BF16),
                ((n_ctx, rows + count, 2 * kvd), BF16),
                ((rows, rank), BF16),
            ],
            *d_h2_parts,
            s_agu,
            gain_two,
            x1,
            grad_out_bf,
            h2,
            *o_near,
            s_lo,
            s_ao,
            attn,
            ob,
            uo,
            qb,
            kb,
            vb,
            lse,
            query_pos,
            key_pos,
            cosine,
            sine,
            key_cos,
            key_sin,
            u1_all,
            h1,
            h1_all,
            s_bq,
            s_bkv,
            scalars=(own_ctx,),
            scratch=[
                pltpu.VMEM((rows, width), BF16),
                pltpu.VMEM((group * rows, HD), F32),
                pltpu.VMEM((count * n_ctx, width // 3), F32),
                pltpu.VMEM((rank, 2 * kvd), F32),
                pltpu.VMEM((n_ctx * rows, 2 * rank), BF16),
                pltpu.VMEM((n_ctx, rows, q_cols), BF16),
                pltpu.VMEM(o_near[0].shape, BF16),
                pltpu.VMEM(o_near[1].shape, BF16),
                pltpu.VMEM(h1_all.shape, BF16),
                pltpu.SemaphoreType.DMA((3,)),
            ],
            far=(n_wa + 5, n_wa + 6, n_wa + 24),
        )
        got = lax.all_to_all(sent, "ctx", 0, 0, tiled=True)
        ff_wa = jnp.stack(wa_exchange(ff_share))
        out_parts = [
            lax.psum_scatter(
                jnp.concatenate(absolute(out_sent, "wa"), axis=0),
                "wa",
                scatter_dimension=0,
                tiled=True,
            )
        ]
        got, ff_wa, out_parts = lax.optimization_barrier((got, ff_wa, out_parts))
        ff_all = lax.all_gather(ff_wa, "ctx", axis=0, tiled=False)
        dl_kv, du1, share = local_call(
            collect_kernel,
            [
                ((rows, 2 * kvd), BF16),
                ((rows, 3 * rank), BF16),
                ((count, 2 * kvd), BF16),
            ],
            got,
            dl_q,
            s_bq,
            s_bkv,
        )
        share_wa = jnp.stack(wa_exchange(share))
        share_near = gather_near(share_wa)
        out, grad_x = local_call(
            functools.partial(finish_kernel, n_wa=len(out_parts)),
            [((rows, width), BF16), ((rows, width), F32)],
            *out_parts,
            x1,
            ud,
            s_ld,
            x_bf,
            gain_one,
            d_x1,
            dl_q,
            dl_kv,
            du1,
            w_blocks,
            s_aqkv,
            scratch=[pltpu.VMEM(w_blocks.shape, BF16), pltpu.SemaphoreType.DMA(())],
            far=(len(out_parts) + 9,),
            cost=7 * 10**9,
        )
        held = (share_near, out, grad_x)
        share_near, out, grad_x = lax.optimization_barrier(held)
        seq_all = jnp.stack(gather_cores(share_near))
        own_wa = wa.astype(jnp.int32)[None]
        r_bgu, r_ad = ff_results(own_wa, ff_all, slots, rank, part_ff)
        tables = {
            "a_qkv": a_qkv,
            "b_q": b_q,
            "b_kv": b_kv,
            "a_o": a_o,
            "lift_o": lift_o,
            "a_gu": a_gu,
            "lift_down": lift_down,
        }
        layout = tuple(flat_starts(rank)[name] for name in tables)
        r_aqkv, r_bq, r_bkv, r_ao, r_lo, r_agu, r_ld = seq_results(
            jnp.concatenate([own_wa, own_ctx]), index_all, seq_all, [table.shape for table in tables.values()], layout
        )
        return (
            out[None],
            grad_x[None],
            r_aqkv,
            r_bq,
            r_bkv,
            r_ao,
            r_lo,
            r_agu,
            r_bgu,
            r_ad,
            r_ld,
        )

    return per_device


def solution(mesh):
    rep = P()
    return jax.shard_map(
        make_per_device(mesh.shape["ctx"], mesh.shape["wa"]),
        mesh=mesh,
        in_specs=(
            P("wa", "ctx", None),
            P("wa", "ctx", None),
            P("wa"),
            rep,
            P("wa", None),
            rep,
            P("wa", None),
            P(None, None, "wa"),
            P("wa", None),
        )
        + (rep,) * 11,
        out_specs=(P("wa", "ctx", None), P("wa", "ctx", None)) + (rep,) * 9,
        check_vma=False,
    )
```
